32 devices in a mesh: groups: 2 (over y), seq: 4 (over z), dp: 2 (over x), strand: 2 (over core).
Axes of the slice: x: 2, y: 2, z: 4, core: 2. Of those that a mesh axis runs over, the one named last changes fastest.
Arguments:
- tokens: int32 [4, 2048], P(('groups', 'dp'), 'seq'), parts along dimension 0, may hold values from 0 to 3
- stem_table: bfloat16 [15, 4, 1536], replicated, may hold values from -1.5 to 1.5
- conv_weight: bfloat16 [3, 1536, 768], P(None, 'dp'), may hold values from -0.09375 to 0.09375
- gain_in: float32 [1536], replicated, may hold values from 0.1 to 1.9
- gain_mid: float32 [768], replicated, may hold values from 0.1 to 1.9
- point_weight: bfloat16 [768, 1536], P('dp'), may hold values from -0.21875 to 0.21875
Outputs:
- embedding: bfloat16 [4, 2048, 1536], P(('groups', 'dp'), 'seq', 'strand'), parts along dimension 0
The draws below stay inside these ranges and needn't reach their ends.
There are 2 independent parts, one for each index of `groups`. The reference program is written for one: setup_inputs(seed, part) draws one part's arguments, and reference() takes and returns one part's arrays. A program takes and returns all parts, laid end to end along the dimension named above; an argument that names none is the same for every part. Nothing has to cross between parts.
All inputs are finite; a program needn't handle non-finite values.
Results may differ from the reference program's by a relative error of at most 0.009.
Values may be sent and summed in bfloat16 or wider, within the bound.
No kernel may reach another device: no remote copies, remote signals or barrier semaphores. Data moves between devices by JAX's collectives and lax.ppermute only.
A program may use at most 64 MiB of HBM per device.

```python
import jax
import jax.numpy as jnp
from jax import lax

C = 1536
H = 768
TAPS = 15
BASES = 4
DILATION_STEP = 256
BATCH = 2
LENGTH = 2048


def set_ends(result, rng, low, top_value):
    longest = result.shape.index(max(result.shape))
    spots = []
    for shift in (0, 1):
        where = [jax.random.randint(jax.random.fold_in(rng, axis), (), 0, length) for axis, length in enumerate(result.shape)]
        where[longest] = (where[longest] + shift) % result.shape[longest]
        spots.append(tuple(where))
    return result.at[spots[0]].set(low).at[spots[1]].set(top_value)


def shard_levels(key, shape, split, least, high):
    level = 1.0
    for dim, shards_of in split:
        heights = jax.random.uniform(jax.random.fold_in(jax.random.fold_in(key, 6), dim), (shards_of,), jnp.float32, least / len(split), high / len(split))
        level = level * jnp.repeat(jnp.exp(heights), shape[dim] // shards_of).reshape((-1,) + (1,) * (len(shape) - 1 - dim))
    return level


def scatter_about(stream_key, shape, width, limit, cuts=(), kind=jnp.bfloat16):
    entries = jax.random.normal(stream_key, shape, jnp.float32) * width
    if len(cuts) > 0:
        entries = shard_levels(stream_key, shape, cuts, -0.22, 0.18) * entries
    return jnp.clip(entries, min=-limit, max=limit).astype(kind)


def setup_inputs(seed: int = 0, part: int = 0) -> dict:
    key_list = jax.random.split(jax.random.key(seed), 7)
    part_keys = jax.random.split(jax.random.fold_in(key_list[6], part), 7)
    return {
        "tokens": set_ends(jax.random.randint(part_keys[0], (BATCH, LENGTH), 0, 4), jax.random.fold_in(part_keys[0], 1), 0, 3).astype(jnp.int32),
        "stem_table": scatter_about(key_list[1], (TAPS, BASES, C), TAPS ** -0.5, 1.5),
        "conv_weight": scatter_about(key_list[2], (3, C, H), (3 * C) ** -0.5, 0.09375, ((1, 2),)),
        "gain_in": jnp.clip(1.0 + 0.18 * jax.random.normal(key_list[3], (C,), jnp.float32), 0.1, 1.9),
        "gain_mid": jnp.clip(1.0 + 0.18 * jax.random.normal(key_list[4], (H,), jnp.float32), 0.1, 1.9),
        "point_weight": scatter_about(key_list[5], (H, C), H ** -0.5, 0.21875, ((0, 2),)),
    }


def normalize(values, gain):
    scale = lax.rsqrt(lax.optimization_barrier(jnp.mean(values * values, axis=-1, keepdims=True)) + 1e-06)
    return jax.nn.gelu(values * scale * gain.astype(jnp.float32))

def network(base_ids, stem_table, conv_weight, gain_in, gain_mid, point_weight):
    sequence_length = base_ids.shape[0]
    rim_width = TAPS // 2
    onehot = (base_ids[:, None] == jnp.arange(BASES, dtype=jnp.int32)[None, :]).astype(jnp.bfloat16)
    padded_hot = jnp.pad(onehot, ((rim_width, rim_width), (0, 0)))
    windows = jnp.concatenate([padded_hot[tap_position:tap_position + sequence_length] for tap_position in range(TAPS)], axis=1)
    embedded = jnp.dot(windows, stem_table.reshape(TAPS * BASES, C), preferred_element_type=jnp.float32).astype(jnp.bfloat16)
    stream = embedded.astype(jnp.float32)
    gelu_output = normalize(stream, gain_in).astype(jnp.bfloat16)
    padded_activation = jnp.pad(gelu_output, ((DILATION_STEP, DILATION_STEP), (0, 0)))
    conv_out = jnp.zeros((sequence_length, H), jnp.float32)
    for tap_position in range(3):
        tap_slices = padded_activation[tap_position * DILATION_STEP:tap_position * DILATION_STEP + sequence_length]
        conv_out = conv_out + jnp.dot(tap_slices, conv_weight[tap_position], preferred_element_type=jnp.float32)
    middle = normalize(conv_out, gain_mid).astype(jnp.bfloat16)
    branch = jnp.dot(middle, point_weight, preferred_element_type=jnp.float32)
    return (stream + branch).astype(jnp.bfloat16)

def reference(tokens, stem_table, conv_weight, gain_in, gain_mid, point_weight):

    def one_sequence(base_ids):
        forward = network(base_ids, stem_table, conv_weight, gain_in, gain_mid, point_weight)
        reverse_out = network(3 - base_ids[::-1], stem_table, conv_weight, gain_in, gain_mid, point_weight)
        total = forward.astype(jnp.float32) + reverse_out[::-1].astype(jnp.float32)
        return (total * 0.5).astype(jnp.bfloat16)
    return lax.map(one_sequence, tokens)
```

```python
import functools

import jax
import jax.numpy as jnp
from jax import lax
from jax.experimental import pallas as pl
from jax.experimental.pallas import tpu as pltpu
from jax.sharding import PartitionSpec as P

DILATION = 256
REACH = 384
EPS = 1e-06
ROW_STEP = 128
VMEM_BYTES = 24 * 2**20


def shifted_pairs(axis, distance):
    count = lax.axis_size(axis)
    return [(i, i + distance) for i in range(count) if 0 <= i + distance < count]


def ring_pairs(axis, distance):
    count = lax.axis_size(axis)
    return [(i, (i + distance) % count) for i in range(count)]


def one_hot_columns(tok_ref, row_count, length):
    span = row_count + 2 * DILATION
    width = tok_ref.shape[1]
    spread = jnp.broadcast_to(tok_ref[...], (16, width))
    start = width - (REACH - DILATION + 8)
    taps = pltpu.roll(spread, start, 1, stride=1, stride_axis=0)[:, :span]
    lane = lax.broadcasted_iota(jnp.int32, (16, span), 1)
    place = lane + (lax.axis_index("seq") * row_count - DILATION)
    source = place + 8 - lax.broadcasted_iota(jnp.int32, (16, span), 0)
    inside = (place >= 0) & (place < length) & (source >= 0) & (source < length)
    taps = jnp.where(inside, taps, -1)
    hot = jnp.concatenate([(taps == base).astype(jnp.float32) for base in range(4)], axis=0)
    return hot.T.astype(jnp.bfloat16)


def gelu(x):
    inner = x * (0.7978845608028654 + 0.035677408136300125 * (x * x))
    half = 0.5 * x
    return half + half * jnp.tanh(inner)


def partial_kernel(own, length, *refs):
    if own:
        tok_ref, table_ref, both_ref, gain_ref, w_any, out_ref, res_ref, w_ref, act_ref, sem = refs
    else:
        tok_ref, table_ref, gain_ref, w_any, out_ref, w_ref, act_ref, sem = refs
    row_count = out_ref.shape[0]
    depth = gain_ref.shape[1]
    copy = pltpu.make_async_copy(w_any, w_ref, sem)
    copy.start()
    hot = one_hot_columns(tok_ref, row_count, length)
    if own:
        here = hot[DILATION : DILATION + row_count]
        twice = jnp.concatenate([here, here], axis=1)
        res_ref[...] = jnp.dot(twice, both_ref[...], preferred_element_type=jnp.float32)
    gain = gain_ref[...]
    for low in range(0, row_count + 2 * DILATION, ROW_STEP):
        embedded = jnp.dot(
            hot[low : low + ROW_STEP], table_ref[...], preferred_element_type=jnp.float32
        )
        mean = jnp.mean(embedded * embedded, axis=-1, keepdims=True)
        scaled = embedded[:, :depth] * lax.rsqrt(mean + EPS) * gain
        act_ref[low : low + ROW_STEP] = gelu(scaled).astype(jnp.bfloat16)
    copy.wait()
    second = lax.axis_index("strand")
    for low in range(0, row_count, DILATION):
        total = None
        for tap in range(3):
            weight = w_ref[tap + second * (2 - 2 * tap)]
            start = low + tap * DILATION
            part = jnp.dot(
                act_ref[start : start + DILATION], weight, preferred_element_type=jnp.float32
            )
            total = part if total is None else total + part
        out_ref[low : low + DILATION] = total.astype(out_ref.dtype)


def partial_call(own, length, row_count, operands):
    depth, inner = operands[-1].shape[1:]
    vmem = pl.BlockSpec(memory_space=pltpu.VMEM)
    outs = [jax.ShapeDtypeStruct((row_count, inner), jnp.float32 if own else jnp.bfloat16)]
    if own:
        outs.append(jax.ShapeDtypeStruct((row_count, operands[2].shape[1]), jnp.float32))
    return pl.pallas_call(
        functools.partial(partial_kernel, own, length),
        out_shape=outs,
        in_specs=[vmem] * (len(operands) - 1) + [pl.BlockSpec(memory_space=pl.ANY)],
        out_specs=[vmem] * len(outs),
        scratch_shapes=[
            pltpu.VMEM(operands[-1].shape, jnp.bfloat16),
            pltpu.VMEM((row_count + 2 * DILATION, depth), jnp.bfloat16),
            pltpu.SemaphoreType.DMA,
        ],
        compiler_params=pltpu.CompilerParams(vmem_limit_bytes=VMEM_BYTES),
        cost_estimate=pl.CostEstimate(
            flops=6 * row_count * depth * inner, bytes_accessed=12 * 2**20, transcendentals=0
        ),
        name="conv_own" if own else "conv_sent",
    )(*operands)


def middle_kernel(count, *refs):
    own_ref, gain_ref, out_ref = refs[0], refs[count], refs[count + 1]
    for low in range(0, own_ref.shape[0], ROW_STEP):
        rows = slice(low, low + ROW_STEP)
        total = own_ref[rows]
        for ref in refs[1:count]:
            total = total + ref[rows].astype(jnp.float32)
        mean = jnp.mean(total * total, axis=-1, keepdims=True)
        out_ref[rows] = gelu(total * lax.rsqrt(mean + EPS) * gain_ref[...]).astype(jnp.bfloat16)


def final_kernel(count, *refs):
    mine_ref, other_ref, res_ref = refs[:3]
    blocks = refs[3 : 3 + count]
    out_ref, weight_ref, sems = refs[3 + count :]
    depth = blocks[0].shape[0]
    me = lax.axis_index("dp")
    copies = []
    for step, block in enumerate(blocks):
        place = pl.multiple_of(lax.rem(me + step, count) * depth, 16)
        copy = pltpu.make_async_copy(block, weight_ref.at[pl.ds(place, depth)], sems.at[step])
        copy.start()
        copies.append(copy)
    total = mine_ref[...].astype(jnp.float32) + other_ref[...].astype(jnp.float32)
    total = total.astype(jnp.bfloat16)
    for copy in copies:
        copy.wait()
    branch = jnp.dot(total, weight_ref[...], preferred_element_type=jnp.float32)
    out_ref[...] = (0.5 * (branch + res_ref[...])).astype(jnp.bfloat16)


def per_device(tokens, stem_table, conv_weight, gain_in, gain_mid, point_weight):
    row_count = tokens.shape[1]
    tap_total, kinds, width = stem_table.shape
    depth, inner = conv_weight.shape[1:]
    count = lax.axis_size("dp")
    length = row_count * lax.axis_size("seq")
    me = lax.axis_index("dp")
    strand = lax.axis_index("strand")
    second = strand == 1
    half = width // 2
    vmem = pl.BlockSpec(memory_space=pltpu.VMEM)
    params = pltpu.CompilerParams(vmem_limit_bytes=VMEM_BYTES)

    base_ids = tokens[0]
    low = lax.ppermute(base_ids[row_count - REACH :], "seq", shifted_pairs("seq", 1))
    high = lax.ppermute(base_ids[:REACH], "seq", shifted_pairs("seq", -1))
    near = jnp.concatenate([low, base_ids, high])[None]
    sequences = [near] + [
        lax.ppermute(near, "dp", ring_pairs("dp", -step)) for step in range(1, count)
    ]

    by_base = jnp.swapaxes(stem_table, 0, 1)
    blank = jnp.zeros((kinds, 1, width), stem_table.dtype)
    straight = jnp.concatenate([blank, by_base[:, ::-1]], axis=1).reshape(kinds * 16, width)
    flipped = jnp.concatenate([blank, by_base[::-1]], axis=1).reshape(kinds * 16, width)
    table = jnp.where(second, flipped, straight)
    table = lax.dynamic_slice_in_dim(
        jnp.concatenate([table, table], axis=1), me * depth, width, axis=1
    )
    both = lax.dynamic_slice_in_dim(
        jnp.concatenate([straight, flipped], axis=0), strand * half, half, axis=1
    )
    gain_here = lax.dynamic_slice_in_dim(gain_in, me * depth, depth)[None]

    columns = lax.dynamic_slice_in_dim(point_weight, strand * half, half, axis=1)
    blocks = [columns] + [
        lax.ppermute(columns, "dp", ring_pairs("dp", -step)) for step in range(1, count)
    ]

    received = []
    for step in range(1, count):
        (part,) = partial_call(
            False, length, row_count, (sequences[step], table, gain_here, conv_weight)
        )
        received.append(lax.ppermute(part, "dp", ring_pairs("dp", step)))
    own, res = partial_call(
        True, length, row_count, (near, table, both, gain_here, conv_weight)
    )
    middle = pl.pallas_call(
        functools.partial(middle_kernel, count),
        out_shape=jax.ShapeDtypeStruct((row_count, inner), jnp.bfloat16),
        in_specs=[vmem] * (count + 1),
        out_specs=vmem,
        compiler_params=params,
        name="middle",
    )(own, *received, gain_mid[None])
    other = lax.ppermute(middle, "strand", ring_pairs("strand", 1))
    out = pl.pallas_call(
        functools.partial(final_kernel, count),
        out_shape=jax.ShapeDtypeStruct((row_count, half), jnp.bfloat16),
        in_specs=[vmem] * 3 + [pl.BlockSpec(memory_space=pl.ANY)] * count,
        out_specs=vmem,
        scratch_shapes=[
            pltpu.VMEM((inner, half), jnp.bfloat16),
            pltpu.SemaphoreType.DMA((count,)),
        ],
        compiler_params=params,
        name="final",
    )(middle, other, res, *blocks)
    return out[None]


def solution(mesh):
    return jax.shard_map(
        per_device,
        mesh=mesh,
        in_specs=(P(("groups", "dp"), "seq"), P(), P(None, "dp", None), P(), P(), P("dp", None)),
        out_specs=P(("groups", "dp"), "seq", "strand"),
        check_vma=False,
    )
```

```python
import functools

import jax
import jax.numpy as jnp
from jax import lax
from jax.experimental import pallas as pl
from jax.experimental.pallas import tpu as pltpu
from jax.sharding import PartitionSpec as P

DILATION = 256
REACH = 384
EPS = 1e-06
ROW_STEP = 128
KINDS = 4
MIB = 2**20


def shifted_pairs(axis, distance):
    count = lax.axis_size(axis)
    return [(i, i + distance) for i in range(count) if 0 <= i + distance < count]


def ring_pairs(axis, distance):
    count = lax.axis_size(axis)
    return [(i, (i + distance) % count) for i in range(count)]


def base_taps(tok_ref, row_count, length, low, span):
    width = tok_ref.shape[1]
    spread = jnp.broadcast_to(tok_ref[...], (16, width))
    start = width - (REACH - DILATION + low + 8)
    taps = pltpu.roll(spread, start, 1, stride=1, stride_axis=0)[:, :span]
    place = lax.broadcasted_iota(jnp.int32, (16, span), 1)
    place = place + (lax.axis_index("seq") * row_count - DILATION + low)
    source = place + 8 - lax.broadcasted_iota(jnp.int32, (16, span), 0)
    inside = (place >= 0) & (place < length) & (source >= 0) & (source < length)
    return jnp.where(inside, taps, -1).astype(jnp.float32).astype(jnp.bfloat16)


def one_hot(taps, second, table_rows):
    row = lax.broadcasted_iota(jnp.int32, (table_rows, 16), 0) // KINDS
    column = lax.broadcasted_iota(jnp.int32, (table_rows, 16), 1)
    chosen = (column == 15 - row + second * (2 * row - 14)).astype(jnp.float32)
    values = jnp.dot(chosen.astype(jnp.bfloat16), taps, preferred_element_type=jnp.float32)
    base = lax.broadcasted_iota(jnp.int32, values.shape, 0) % KINDS
    base = base + second * (KINDS - 1 - 2 * base)
    return (values == base.astype(jnp.float32)).astype(jnp.float32).T


def gelu(x):
    inner = x * (0.7978845608028654 + 0.035677408136300125 * (x * x))
    half = 0.5 * x
    return half + half * jnp.tanh(inner)


def activate(hot, table_ref, gain_ref, act_ref, low):
    depth = gain_ref.shape[1]
    for start in range(0, hot.shape[0], ROW_STEP):
        embedded = jnp.dot(
            hot[start : start + ROW_STEP], table_ref[...], preferred_element_type=jnp.float32
        )
        mean = jnp.mean(embedded * embedded, axis=-1, keepdims=True)
        scaled = embedded[:, :depth] * lax.rsqrt(mean + EPS) * gain_ref[...]
        act_ref[low + start : low + start + ROW_STEP] = gelu(scaled).astype(jnp.bfloat16)


def convolve(blocks, w_ref):
    second = lax.axis_index("strand")
    total = None
    for tap, block in enumerate(blocks):
        weight = w_ref[tap + second * (2 - 2 * tap)]
        part = jnp.dot(block, weight, preferred_element_type=jnp.float32)
        total = part if total is None else total + part
    return total


def first_kernel(row_count, length, tok_ref, table_ref, gain_ref, w_any, out_ref, kept_ref, w_ref, act_ref, sem):
    copy = pltpu.make_async_copy(w_any, w_ref, sem)
    copy.start()
    taps = base_taps(tok_ref, row_count, length, 0, 3 * DILATION)
    hot = one_hot(taps, lax.axis_index("strand"), table_ref.shape[0]).astype(jnp.bfloat16)
    activate(hot, table_ref, gain_ref, act_ref, 0)
    kept_ref[...] = act_ref[DILATION:]
    copy.wait()
    blocks = [act_ref[t * DILATION : (t + 1) * DILATION] for t in range(3)]
    out_ref[...] = convolve(blocks, w_ref).astype(jnp.bfloat16)


def next_kernel(row_count, length, low, tok_ref, table_ref, gain_ref, kept_ref, w_ref, out_ref, now_ref, act_ref):
    taps = base_taps(tok_ref, row_count, length, low + 2 * DILATION, DILATION)
    hot = one_hot(taps, lax.axis_index("strand"), table_ref.shape[0]).astype(jnp.bfloat16)
    activate(hot, table_ref, gain_ref, act_ref, 0)
    blocks = [kept_ref[:DILATION], kept_ref[DILATION:], act_ref[...]]
    now_ref[:DILATION] = kept_ref[DILATION:]
    now_ref[DILATION:] = act_ref[...]
    out_ref[...] = convolve(blocks, w_ref).astype(jnp.bfloat16)


def own_kernel(length, places, piece_rows, *refs):
    tok_ref, table_ref, plain_ref, gain_ref, w_ref = refs[:5]
    pieces = refs[5 : 5 + len(places)]
    out_ref, res_ref, point_ref, act_ref, sems = refs[5 + len(places) :]
    row_count = out_ref.shape[0]
    count, groups = lax.axis_size("dp"), lax.axis_size("groups")
    me, group = lax.axis_index("dp"), lax.axis_index("groups")
    copies = []
    for index, (step, turn, all_groups) in enumerate(places):
        place = lax.rem(me + step, count) * (piece_rows * groups)
        if not all_groups:
            place = place + lax.rem(group + turn, groups) * piece_rows
        target = pl.ds(pl.multiple_of(place, 16), pieces[index].shape[0])
        copies.append(pltpu.make_async_copy(pieces[index], point_ref.at[target], sems.at[index]))
        copies[-1].start()
    second = lax.axis_index("strand")
    taps = base_taps(tok_ref, row_count, length, 0, row_count + 2 * DILATION)
    hot = one_hot(taps, second, table_ref.shape[0])
    here = slice(DILATION, DILATION + row_count)
    both = hot[here] + one_hot(taps[:, here], 1 - second, table_ref.shape[0])
    res_ref[...] = jnp.dot(
        both.astype(jnp.bfloat16), plain_ref[...], preferred_element_type=jnp.float32
    )
    activate(hot.astype(jnp.bfloat16), table_ref, gain_ref, act_ref, 0)
    for low in range(0, row_count, DILATION):
        blocks = [act_ref[low + t * DILATION : low + (t + 1) * DILATION] for t in range(3)]
        out_ref[low : low + DILATION] = convolve(blocks, w_ref)
    for copy in copies:
        copy.wait()


def middle_kernel(low, own_ref, gain_ref, *refs):
    out_ref = refs[-1]
    for start in range(0, out_ref.shape[0], ROW_STEP):
        total = own_ref[low + start : low + start + ROW_STEP]
        for ref in refs[:-1]:
            total = total + ref[start : start + ROW_STEP].astype(jnp.float32)
        mean = jnp.mean(total * total, axis=-1, keepdims=True)
        value = gelu(total * lax.rsqrt(mean + EPS) * gain_ref[...])
        out_ref[start : start + ROW_STEP] = value.astype(jnp.bfloat16)


def final_kernel(low, mine_ref, other_ref, res_ref, point_ref, *refs):
    out_ref = refs[-1]
    total = mine_ref[...].astype(jnp.float32) + other_ref[...].astype(jnp.float32)
    branch = jnp.dot(
        total.astype(jnp.bfloat16), point_ref[...], preferred_element_type=jnp.float32
    )
    rows = slice(low, low + DILATION)
    out_ref[...] = (0.5 * (branch + res_ref[rows])).astype(jnp.bfloat16)


def cost(micros):
    return pl.CostEstimate(flops=0, bytes_accessed=int(3.6e6 * micros), transcendentals=0)


def per_device(tokens, stem_table, conv_weight, gain_in, gain_mid, point_weight):
    row_count = tokens.shape[1]
    tap_total, kinds, width = stem_table.shape
    depth, inner = conv_weight.shape[1:]
    count, groups = lax.axis_size("dp"), lax.axis_size("groups")
    length = row_count * lax.axis_size("seq")
    me, group, strand = (lax.axis_index(axis) for axis in ("dp", "groups", "strand"))
    half = width // 2
    vmem = pl.BlockSpec(memory_space=pltpu.VMEM)
    anywhere = pl.BlockSpec(memory_space=pl.ANY)
    bf16, f32 = jnp.bfloat16, jnp.float32
    params = pltpu.CompilerParams(vmem_limit_bytes=24 * MIB)

    base_ids = tokens[0]
    low = lax.ppermute(base_ids[row_count - REACH :], "seq", shifted_pairs("seq", 1))
    high = lax.ppermute(base_ids[:REACH], "seq", shifted_pairs("seq", -1))
    near = jnp.concatenate([low, base_ids, high])[None]
    sequences = [near] + [
        lax.ppermute(near, "dp", ring_pairs("dp", -step)) for step in range(1, count)
    ]

    table_rows = 16 * kinds
    flat = jnp.pad(
        stem_table.reshape(tap_total * kinds, width), ((0, table_rows - tap_total * kinds), (0, 0))
    )
    table = lax.dynamic_slice_in_dim(
        jnp.concatenate([flat, flat], axis=1), me * depth, width, axis=1
    )
    plain = lax.dynamic_slice_in_dim(flat, strand * half, half, axis=1)
    gain_here = lax.dynamic_slice_in_dim(gain_in, me * depth, depth)[None]

    columns = lax.dynamic_slice_in_dim(point_weight, strand * half, half, axis=1)
    piece_rows = point_weight.shape[0] // groups
    piece = lax.dynamic_slice_in_dim(columns, group * piece_rows, piece_rows, axis=0)
    places, pieces = [(0, 0, True)], [columns]
    for step in range(1, count):
        crossed = lax.ppermute(piece, "dp", ring_pairs("dp", -step))
        for turn in range(groups):
            places.append((step, turn, False))
            pieces.append(
                lax.ppermute(crossed, "groups", ring_pairs("groups", -turn)) if turn else crossed
            )

    w_here = conv_weight
    received = []
    for step in range(1, count):
        tok = sequences[step]
        kept_shape = jax.ShapeDtypeStruct((2 * DILATION, depth), bf16)
        part_shape = jax.ShapeDtypeStruct((DILATION, inner), bf16)
        part, kept, w_here = pl.pallas_call(
            functools.partial(first_kernel, row_count, length),
            out_shape=[part_shape, kept_shape, jax.ShapeDtypeStruct(conv_weight.shape, bf16)],
            in_specs=[vmem] * 3 + [pl.BlockSpec(memory_space=pltpu.HBM)],
            out_specs=[vmem] * 3,
            scratch_shapes=[
                pltpu.VMEM((3 * DILATION, depth), bf16),
                pltpu.SemaphoreType.DMA,
            ],
            compiler_params=params,
            cost_estimate=cost(3),
            name="conv_first",
        )(tok, table, gain_here, pltpu.with_memory_space_constraint(conv_weight, pltpu.HBM))
        parts = [lax.ppermute(part, "dp", ring_pairs("dp", step))]
        for start in range(DILATION, row_count, DILATION):
            part, kept = pl.pallas_call(
                functools.partial(next_kernel, row_count, length, start),
                out_shape=[part_shape, kept_shape],
                in_specs=[vmem] * 5,
                out_specs=[vmem] * 2,
                scratch_shapes=[pltpu.VMEM((DILATION, depth), bf16)],
                compiler_params=params,
                cost_estimate=cost(2),
                name="conv_next",
            )(tok, table, gain_here, kept, w_here)
            parts.append(lax.ppermute(part, "dp", ring_pairs("dp", step)))
        received.append(parts)

    own, res, point = pl.pallas_call(
        functools.partial(own_kernel, length, places, piece_rows),
        out_shape=[
            jax.ShapeDtypeStruct((row_count, inner), f32),
            jax.ShapeDtypeStruct((row_count, half), f32),
            jax.ShapeDtypeStruct((inner, half), bf16),
        ],
        in_specs=[vmem] * 5 + [anywhere] * len(pieces),
        out_specs=[vmem] * 3,
        scratch_shapes=[
            pltpu.VMEM((row_count + 2 * DILATION, depth), bf16),
            pltpu.SemaphoreType.DMA((len(pieces),)),
        ],
        compiler_params=params,
        cost_estimate=cost(5),
        name="conv_own",
    )(near, table, plain, gain_here, w_here, *pieces)

    out = None
    for index, start in enumerate(range(0, row_count, DILATION)):
        middle = pl.pallas_call(
            functools.partial(middle_kernel, start),
            out_shape=jax.ShapeDtypeStruct((DILATION, inner), bf16),
            in_specs=[vmem] * (count + 1),
            out_specs=vmem,
            compiler_params=params,
            cost_estimate=cost(0.5),
            name="middle",
        )(own, gain_mid[None], *[parts[index] for parts in received])
        other = lax.ppermute(middle, "strand", ring_pairs("strand", 1))
        operands = [middle, other, res, point] + ([] if out is None else [out])
        out = pl.pallas_call(
            functools.partial(final_kernel, start),
            grid=(1,),
            out_shape=jax.ShapeDtypeStruct((row_count, half), bf16),
            in_specs=[vmem] * 4 + [anywhere] * (len(operands) - 4),
            out_specs=pl.BlockSpec((DILATION, half), lambda i, index=index: (index, 0)),
            input_output_aliases={} if out is None else {4: 0},
            compiler_params=params,
            cost_estimate=cost(0.7),
            name="final",
        )(*operands)
    return out[None]


def solution(mesh):
    return jax.shard_map(
        per_device,
        mesh=mesh,
        in_specs=(P(("groups", "dp"), "seq"), P(), P(None, "dp", None), P(), P(), P("dp", None)),
        out_specs=P(("groups", "dp"), "seq", "strand"),
        check_vma=False,
    )
```

```python
import functools

import jax
import jax.numpy as jnp
from jax import lax
from jax.experimental import pallas as pl
from jax.experimental.pallas import tpu as pltpu
from jax.sharding import PartitionSpec as P

DILATION = 256
EPS = 1e-06
ROW_STEP = 128
CHUNKS = ((0, 64), (128, 128), (64, 64))
KINDS = 4
FLOPS = {"early": 0.1, "sent": 1.0, "own": 10.0, "middle": 0.3, "final": 10.0}
MIB = 2**20


def ring_pairs(axis, distance):
    count = lax.axis_size(axis)
    return [(i, (i + distance) % count) for i in range(count)]


def base_taps(tok_ref, step, row_count):
    count, blocks = lax.axis_size("dp"), lax.axis_size("seq")
    here = lax.axis_index("seq")
    first = lax.rem(lax.axis_index("dp") + step, count) * blocks
    sides = [jnp.maximum(here - 1, 0), here, jnp.minimum(here + 1, blocks - 1)]
    bases = jnp.concatenate([tok_ref[pl.ds(first + side, 1), :] for side in sides], axis=1)
    width, span = 3 * row_count, row_count + 2 * DILATION
    spread = jnp.broadcast_to(bases, (16, width))
    start = width - (row_count - DILATION + 8)
    taps = pltpu.roll(spread, start, 1, stride=1, stride_axis=0)[:, :span]
    place = lax.broadcasted_iota(jnp.int32, (16, span), 1) + (here * row_count - DILATION)
    source = place + 8 - lax.broadcasted_iota(jnp.int32, (16, span), 0)
    length = blocks * row_count
    inside = (place >= 0) & (place < length) & (source >= 0) & (source < length)
    return jnp.where(inside, taps, -1).astype(jnp.float32).astype(jnp.bfloat16)


def one_hot(taps, second, table_rows):
    row = lax.broadcasted_iota(jnp.int32, (table_rows, 16), 0) // KINDS
    column = lax.broadcasted_iota(jnp.int32, (table_rows, 16), 1)
    chosen = (column == 15 - row + second * (2 * row - 14)).astype(jnp.float32)
    values = jnp.dot(chosen.astype(jnp.bfloat16), taps, preferred_element_type=jnp.float32)
    base = lax.broadcasted_iota(jnp.int32, values.shape, 0) % KINDS
    base = base + second * (KINDS - 1 - 2 * base)
    return (values == base.astype(jnp.float32)).astype(jnp.float32).T


def gelu(x):
    inner = x * (0.7978845608028654 + 0.035677408136300125 * (x * x))
    half = 0.5 * x
    return half + half * jnp.tanh(inner)


def activate(hot, table_ref, gain_ref, act_ref):
    depth = gain_ref.shape[1]
    for start in range(0, hot.shape[0], ROW_STEP):
        embedded = jnp.dot(
            hot[start : start + ROW_STEP], table_ref[...], preferred_element_type=jnp.float32
        )
        mean = jnp.mean(embedded * embedded, axis=-1, keepdims=True)
        scaled = embedded[:, :depth] * lax.rsqrt(mean + EPS) * gain_ref[...]
        act_ref[start : start + ROW_STEP] = gelu(scaled).astype(jnp.bfloat16)


def convolve(blocks, w_ref):
    second = lax.axis_index("strand")
    total = None
    for tap, block in enumerate(blocks):
        weight = w_ref[tap + second * (2 - 2 * tap)]
        part = jnp.dot(block, weight, preferred_element_type=jnp.float32)
        total = part if total is None else total + part
    return total


def chunk_kernel(step, low, size, row_count, first, operand_count, *refs):
    tok_ref, table_ref, gain_ref, w_ref = refs[:4]
    out_ref = refs[operand_count]
    if first:
        kept_ref, act_ref, sem = refs[-3:]
        copy = pltpu.make_async_copy(w_ref, kept_ref, sem)
        copy.start()
        w_ref = kept_ref
    else:
        act_ref = refs[-1]
    taps = base_taps(tok_ref, step, row_count)
    hot = one_hot(taps, lax.axis_index("strand"), table_ref.shape[0])
    blocks = row_count // DILATION
    pieces = [hot[b * DILATION + low :][:size] for b in range(blocks + 2)]
    activate(jnp.concatenate(pieces).astype(jnp.bfloat16), table_ref, gain_ref, act_ref)
    if first:
        copy.wait()
    parts = [act_ref[t * size : (t + blocks) * size] for t in range(3)]
    out_ref[...] = convolve(parts, w_ref).astype(jnp.bfloat16)


def rows_of(ref, low, size):
    starts = range(low, ref.shape[0], DILATION)
    return jnp.concatenate([ref[start : start + size] for start in starts])


def middle_of(own_ref, gain_ref, parts, low, size):
    total = rows_of(own_ref, low, size)
    for ref in parts:
        total = total + ref[...].astype(jnp.float32)
    mean = jnp.mean(total * total, axis=-1, keepdims=True)
    return gelu(total * lax.rsqrt(mean + EPS) * gain_ref[...]).astype(jnp.bfloat16)


def own_kernel(chunk, *refs):
    tok_ref, table_ref, plain_ref, gain_ref, w_ref, gain_mid_ref = refs[:6]
    parts, (out_ref, res_ref, middle_ref, act_ref) = refs[6:-4], refs[-4:]
    row_count = out_ref.shape[0]
    second = lax.axis_index("strand")
    taps = base_taps(tok_ref, 0, row_count)
    hot = one_hot(taps, second, table_ref.shape[0])
    here = slice(DILATION, DILATION + row_count)
    both = hot[here] + one_hot(taps[:, here], 1 - second, table_ref.shape[0])
    res_ref[...] = jnp.dot(
        both.astype(jnp.bfloat16), plain_ref[...], preferred_element_type=jnp.float32
    )
    activate(hot.astype(jnp.bfloat16), table_ref, gain_ref, act_ref)
    blocks = [act_ref[t * DILATION : t * DILATION + row_count] for t in range(3)]
    out_ref[...] = convolve(blocks, w_ref)
    middle_ref[...] = middle_of(out_ref, gain_mid_ref, parts, *chunk)


def middle_kernel(low, size, count, places, piece_rows, own_ref, gain_ref, *refs):
    parts, pieces = refs[:count], refs[count : count + len(places)]
    out_ref = refs[-3] if places else refs[-1]
    copies = []
    if places:
        point_ref, sems = refs[-2:]
        ranks, groups = lax.axis_size("dp"), lax.axis_size("groups")
        me, group = lax.axis_index("dp"), lax.axis_index("groups")
        for index, (step, turn) in enumerate(places):
            place = lax.rem(me + step, ranks) * (piece_rows * groups)
            if step:
                place = place + lax.rem(group + turn, groups) * piece_rows
            target = pl.ds(pl.multiple_of(place, 16), pieces[index].shape[0])
            copies.append(
                pltpu.make_async_copy(pieces[index], point_ref.at[target], sems.at[index])
            )
            copies[-1].start()
    out_ref[...] = middle_of(own_ref, gain_ref, parts, low, size)
    for copy in copies:
        copy.wait()


def final_kernel(low, size, mine_ref, other_ref, res_ref, point_ref, *refs):
    out_ref = refs[-1]
    total = mine_ref[...].astype(jnp.float32) + other_ref[...].astype(jnp.float32)
    branch = jnp.dot(
        total.astype(jnp.bfloat16), point_ref[...], preferred_element_type=jnp.float32
    )
    value = (0.5 * (branch + rows_of(res_ref, low, size))).astype(jnp.bfloat16)
    out_ref[...] = value.reshape(out_ref.shape)


def cost(kind, share=1.0):
    return pl.CostEstimate(
        flops=int(1e9 * FLOPS[kind] * share), bytes_accessed=2**20, transcendentals=0
    )


def per_device(tokens, stem_table, conv_weight, gain_in, gain_mid, point_weight):
    row_count = tokens.shape[1]
    tap_total, kinds, width = stem_table.shape
    depth, inner = conv_weight.shape[1:]
    count, groups = lax.axis_size("dp"), lax.axis_size("groups")
    me, group, strand = (lax.axis_index(axis) for axis in ("dp", "groups", "strand"))
    half = width // 2
    vmem = pl.BlockSpec(memory_space=pltpu.VMEM)
    anywhere = pl.BlockSpec(memory_space=pl.ANY)
    bf16, f32 = jnp.bfloat16, jnp.float32
    params = pltpu.CompilerParams(vmem_limit_bytes=24 * MIB)

    members = count * lax.axis_size("seq")
    bases = lax.all_to_all(
        jnp.broadcast_to(tokens, (members, row_count)), ("dp", "seq"), 0, 0, tiled=True
    )

    table_rows = 16 * kinds
    flat = jnp.pad(
        stem_table.reshape(tap_total * kinds, width), ((0, table_rows - tap_total * kinds), (0, 0))
    )
    table = lax.dynamic_slice_in_dim(
        jnp.concatenate([flat, flat], axis=1), me * depth, width, axis=1
    )
    plain = lax.dynamic_slice_in_dim(flat, strand * half, half, axis=1)
    gain_here = lax.dynamic_slice_in_dim(gain_in, me * depth, depth)[None]

    columns = lax.dynamic_slice_in_dim(point_weight, strand * half, half, axis=1)
    piece_rows = point_weight.shape[0] // groups
    piece = lax.dynamic_slice_in_dim(columns, group * piece_rows, piece_rows, axis=0)
    crossed = [lax.ppermute(piece, "dp", ring_pairs("dp", -step)) for step in range(1, count)]

    weight = conv_weight
    received = [[] for _ in CHUNKS]
    for step in range(1, count):
        for index, (low, size) in enumerate(CHUNKS):
            first, passing = index == 0, index == 1
            rows = row_count // DILATION * size
            outs = [jax.ShapeDtypeStruct((rows, inner), bf16)]
            operands = [bases, table, gain_here, weight]
            scratch = [pltpu.VMEM((rows + 2 * size, depth), bf16)]
            if first:
                outs.append(jax.ShapeDtypeStruct(conv_weight.shape, bf16))
                scratch.append(pltpu.SemaphoreType.DMA)
                operands[3] = pltpu.with_memory_space_constraint(conv_weight, pltpu.HBM)
            if passing:
                outs.append(jax.ShapeDtypeStruct(piece.shape, bf16))
                operands.append(crossed[step - 1])
            elif index:
                operands.append(part)
            result = pl.pallas_call(
                functools.partial(chunk_kernel, step, low, size, row_count, first, len(operands)),
                out_shape=outs,
                in_specs=[vmem] * 3
                + [pl.BlockSpec(memory_space=pltpu.HBM) if first else vmem]
                + [anywhere] * (len(operands) - 4),
                out_specs=[vmem, anywhere if passing else vmem][: len(outs)],
                scratch_shapes=scratch,
                input_output_aliases={4: 1} if passing else {},
                compiler_params=params,
                cost_estimate=cost('sent' if index else 'early', size / 64),
                name="conv_sent",
            )(*operands)
            part = result[0]
            if first:
                weight = result[1]
            if passing:
                crossed[step - 1] = result[1]
            received[index].append(lax.ppermute(part, "dp", ring_pairs("dp", step)))

    first_rows = row_count // DILATION * CHUNKS[0][1]
    own, res, middle = pl.pallas_call(
        functools.partial(own_kernel, CHUNKS[0]),
        out_shape=[
            jax.ShapeDtypeStruct((row_count, inner), f32),
            jax.ShapeDtypeStruct((row_count, half), f32),
            jax.ShapeDtypeStruct((first_rows, inner), bf16),
        ],
        in_specs=[vmem] * (5 + count),
        out_specs=[vmem] * 3,
        scratch_shapes=[pltpu.VMEM((row_count + 2 * DILATION, depth), bf16)],
        compiler_params=params,
        cost_estimate=cost('own'),
        name="conv_own",
    )(bases, table, plain, gain_here, weight, gain_mid[None], *received[0])

    places, pieces = [(0, 0)], [columns]
    for step in range(1, count):
        for turn in range(groups):
            part = crossed[step - 1]
            if turn:
                part = lax.ppermute(part, "groups", ring_pairs("groups", -turn))
            places.append((step, turn))
            pieces.append(part)

    middles = [middle]
    for index, (low, size) in list(enumerate(CHUNKS))[1:]:
        rows = row_count // DILATION * size
        taken = middles[1:] if index > 1 else pieces
        result = pl.pallas_call(
            functools.partial(
                middle_kernel, low, size, count - 1, [] if index > 1 else places, piece_rows
            ),
            out_shape=[jax.ShapeDtypeStruct((rows, inner), bf16)]
            + [jax.ShapeDtypeStruct((inner, half), bf16)] * (index == 1),
            in_specs=[vmem] * (count + 1) + [anywhere] * len(taken),
            out_specs=[vmem] * (1 + (index == 1)),
            scratch_shapes=[pltpu.SemaphoreType.DMA((len(taken),))] if index == 1 else [],
            compiler_params=params,
            cost_estimate=cost('middle', size / 64),
            name="middle",
        )(own, gain_mid[None], *received[index], *taken)
        if index == 1:
            point = result[1]
        middles.append(result[0])

    out = None
    for middle, (low, size) in zip(middles, CHUNKS):
        other = lax.ppermute(middle, "strand", ring_pairs("strand", 1))
        operands = [middle, other, res, point] + ([] if out is None else [out])
        out = pl.pallas_call(
            functools.partial(final_kernel, low, size),
            grid=(1,),
            out_shape=jax.ShapeDtypeStruct((row_count // DILATION, DILATION, half), bf16),
            in_specs=[vmem] * 4 + [anywhere] * (len(operands) - 4),
            out_specs=pl.BlockSpec(
                (row_count // DILATION, size, half), lambda i, at=low // size: (0, at, 0)
            ),
            input_output_aliases={} if out is None else {4: 0},
            compiler_params=params,
            cost_estimate=cost('final', size / 64),
            name="final",
        )(*operands)
    return out.reshape(1, row_count, half)


def solution(mesh):
    return jax.shard_map(
        per_device,
        mesh=mesh,
        in_specs=(P(("groups", "dp"), "seq"), P(), P(None, "dp", None), P(), P(), P("dp", None)),
        out_specs=P(("groups", "dp"), "seq", "strand"),
        check_vma=False,
    )
```

```python
import functools

import jax
import jax.numpy as jnp
from jax import lax
from jax.experimental import pallas as pl
from jax.experimental.pallas import tpu as pltpu
from jax.sharding import PartitionSpec as P

DILATION = 256
EPS = 1e-06
ROW_STEP = 128
CHUNKS = ((0, 64), (64, 128), (192, 64))
TAILS = ((0, 1), (2,))
KINDS = 4
FLOPS = {'early': 0.1, 'sent0': 1.0, 'sent1': 1.0, 'sent2': 1.0, 'own': 10.0, 'middle0': 5.0, 'middle1': 5.0, 'final0': 1.0, 'final1': 1.0}
MIB = 2**20


def ring_pairs(axis, distance):
    count = lax.axis_size(axis)
    return [(i, (i + distance) % count) for i in range(count)]


def base_taps(tok_ref, step, row_count):
    count, blocks = lax.axis_size("dp"), lax.axis_size("seq")
    here = lax.axis_index("seq")
    first = lax.rem(lax.axis_index("dp") + step, count) * blocks
    sides = [jnp.maximum(here - 1, 0), here, jnp.minimum(here + 1, blocks - 1)]
    bases = jnp.concatenate([tok_ref[first + side] for side in sides], axis=1)
    width, span = 3 * row_count, row_count + 2 * DILATION
    spread = jnp.broadcast_to(bases, (16, width))
    start = width - (row_count - DILATION + 8)
    taps = pltpu.roll(spread, start, 1, stride=1, stride_axis=0)[:, :span]
    place = lax.broadcasted_iota(jnp.int32, (16, span), 1) + (here * row_count - DILATION)
    source = place + 8 - lax.broadcasted_iota(jnp.int32, (16, span), 0)
    length = blocks * row_count
    inside = (place >= 0) & (place < length) & (source >= 0) & (source < length)
    return jnp.where(inside, taps, -1).astype(jnp.float32).astype(jnp.bfloat16)


def one_hot(taps, second, table_rows):
    row = lax.broadcasted_iota(jnp.int32, (table_rows, 16), 0) // KINDS
    column = lax.broadcasted_iota(jnp.int32, (table_rows, 16), 1)
    chosen = (column == 15 - row + second * (2 * row - 14)).astype(jnp.float32)
    values = jnp.dot(chosen.astype(jnp.bfloat16), taps, preferred_element_type=jnp.float32)
    base = lax.broadcasted_iota(jnp.int32, values.shape, 0) % KINDS
    base = base + second * (KINDS - 1 - 2 * base)
    return (values == base.astype(jnp.float32)).astype(jnp.float32).T


def gelu(x):
    inner = x * (0.7978845608028654 + 0.035677408136300125 * (x * x))
    half = 0.5 * x
    return half + half * jnp.tanh(inner)


def activate(hot, table_ref, gain_ref, act_ref):
    depth = gain_ref.shape[1]
    for start in range(0, hot.shape[0], ROW_STEP):
        embedded = jnp.dot(
            hot[start : start + ROW_STEP], table_ref[...], preferred_element_type=jnp.float32
        )
        mean = jnp.mean(embedded * embedded, axis=-1, keepdims=True)
        scaled = embedded[:, :depth] * lax.rsqrt(mean + EPS) * gain_ref[...]
        act_ref[start : start + ROW_STEP] = gelu(scaled).astype(jnp.bfloat16)


def convolve(blocks, w_ref):
    second = lax.axis_index("strand")
    total = None
    for tap, block in enumerate(blocks):
        weight = w_ref[tap + second * (2 - 2 * tap)]
        part = jnp.dot(block, weight, preferred_element_type=jnp.float32)
        total = part if total is None else total + part
    return total


def send_kernel(tok_ref, point_ref, spread_ref, piece_ref, sem):
    rows, columns = piece_ref.shape
    low = pl.multiple_of(lax.axis_index("groups") * rows, 16)
    left = pl.multiple_of(lax.axis_index("strand") * columns, 128)
    copy = pltpu.make_async_copy(
        point_ref.at[pl.ds(low, rows), pl.ds(left, columns)], piece_ref, sem
    )
    copy.start()
    spread_ref[...] = jnp.broadcast_to(tok_ref[...][None], spread_ref.shape)
    copy.wait()


def load_kernel(stem_ref, gain_ref, w_any, table_ref, plain_ref, gain_here_ref, w_ref, flat_ref, sems):
    depth = w_any.shape[1]
    copies = []
    for index, (tap, low, rows) in enumerate(weight_parts(w_any)):
        part = (tap, pl.ds(low, rows))
        copies.append(pltpu.make_async_copy(w_any.at[part], w_ref.at[part], sems.at[index]))
        copies[-1].start()
    taps, kinds, width = stem_ref.shape
    slabs = [stem_ref[tap].astype(jnp.float32) for tap in range(taps)]
    slabs += [jnp.zeros((kinds, width), jnp.float32)] * (16 - taps)
    flat = jnp.concatenate(slabs)
    flat_ref[...] = flat.astype(jnp.bfloat16)
    left = lax.axis_index("dp") * depth
    turn = lax.rem(width - left, width)
    table_ref[...] = pltpu.roll(flat, turn, 1).astype(jnp.bfloat16)
    gain = pltpu.roll(jnp.broadcast_to(gain_ref[...], (8, width)), turn, 1)
    gain_here_ref[...] = gain[:1, :depth]
    half = plain_ref.shape[1]
    column = pl.multiple_of(lax.axis_index("strand") * half, 128)
    plain_ref[...] = flat_ref[:, pl.ds(column, half)]
    for copy in copies:
        copy.wait()


def weight_parts(weight):
    rows = weight.shape[1] // 2
    return [(tap, low, rows) for tap in range(weight.shape[0]) for low in (0, rows)]


def chunk_kernel(step, low, size, row_count, *refs):
    tok_ref, table_ref, gain_ref, w_ref = refs[:4]
    out_ref, act_ref = refs[-2:]
    taps = base_taps(tok_ref, step, row_count)
    hot = one_hot(taps, lax.axis_index("strand"), table_ref.shape[0])
    blocks = row_count // DILATION
    pieces = [hot[b * DILATION + low :][:size] for b in range(blocks + 2)]
    activate(jnp.concatenate(pieces).astype(jnp.bfloat16), table_ref, gain_ref, act_ref)
    parts = [act_ref[t * size : (t + blocks) * size] for t in range(3)]
    out_ref[...] = convolve(parts, w_ref).astype(jnp.bfloat16)


def rows_of(ref, low, size):
    starts = range(low, ref.shape[0], DILATION)
    return jnp.concatenate([ref[start : start + size] for start in starts])


def middle_of(own_ref, gain_ref, parts, low, size):
    total = rows_of(own_ref, low, size)
    for ref in parts:
        total = total + ref[...].astype(jnp.float32)
    mean = jnp.mean(total * total, axis=-1, keepdims=True)
    return gelu(total * lax.rsqrt(mean + EPS) * gain_ref[...]).astype(jnp.bfloat16)


def own_kernel(places, piece_rows, *refs):
    tok_ref, table_ref, plain_ref, gain_ref, w_ref = refs[:5]
    pieces = refs[6 : 6 + len(places)]
    out_ref, res_ref, point_ref, act_ref, sems = refs[6 + len(places) :]
    ranks, groups = lax.axis_size("dp"), lax.axis_size("groups")
    me, group = lax.axis_index("dp"), lax.axis_index("groups")
    copies = []
    for index, (step, turn) in enumerate(places):
        place = lax.rem(me + step, ranks) * (piece_rows * groups)
        if step:
            place = place + lax.rem(group + turn, groups) * piece_rows
        target = pl.ds(pl.multiple_of(place, 16), pieces[index].shape[0])
        copies.append(pltpu.make_async_copy(pieces[index], point_ref.at[target], sems.at[index]))
        copies[-1].start()
    row_count = out_ref.shape[0]
    second = lax.axis_index("strand")
    taps = base_taps(tok_ref, 0, row_count)
    hot = one_hot(taps, second, table_ref.shape[0])
    here = slice(DILATION, DILATION + row_count)
    both = hot[here] + one_hot(taps[:, here], 1 - second, table_ref.shape[0])
    res_ref[...] = jnp.dot(
        both.astype(jnp.bfloat16), plain_ref[...], preferred_element_type=jnp.float32
    )
    activate(hot.astype(jnp.bfloat16), table_ref, gain_ref, act_ref)
    blocks = [act_ref[t * DILATION : t * DILATION + row_count] for t in range(3)]
    out_ref[...] = convolve(blocks, w_ref)
    for copy in copies:
        copy.wait()


def middle_kernel(chunks, count, own_ref, gain_ref, *refs):
    out_ref = refs[-1]
    first, total_size = chunks[0][0], sum(size for _, size in chunks)
    for index, (low, size) in enumerate(chunks):
        parts = refs[index * count : (index + 1) * count]
        value = middle_of(own_ref, gain_ref, parts, low, size)
        for block in range(own_ref.shape[0] // DILATION):
            start = block * total_size + low - first
            out_ref[start : start + size] = value[block * size : (block + 1) * size]


def final_kernel(low, size, mine_ref, other_ref, res_ref, point_ref, *refs):
    out_ref = refs[-1]
    total = mine_ref[...].astype(jnp.float32) + other_ref[...].astype(jnp.float32)
    branch = jnp.dot(
        total.astype(jnp.bfloat16), point_ref[...], preferred_element_type=jnp.float32
    )
    value = (0.5 * (branch + rows_of(res_ref, low, size))).astype(jnp.bfloat16)
    out_ref[...] = value.reshape(out_ref.shape)


def cost(kind):
    return pl.CostEstimate(
        flops=int(1e9 * FLOPS[kind]), bytes_accessed=2**20, transcendentals=0
    )


def per_device(tokens, stem_table, conv_weight, gain_in, gain_mid, point_weight):
    row_count = tokens.shape[1]
    kinds, width = stem_table.shape[1:]
    depth, inner = conv_weight.shape[1:]
    count, groups = lax.axis_size("dp"), lax.axis_size("groups")
    strand = lax.axis_index("strand")
    half = width // 2
    vmem = pl.BlockSpec(memory_space=pltpu.VMEM)
    anywhere = pl.BlockSpec(memory_space=pl.ANY)
    bf16, f32 = jnp.bfloat16, jnp.float32
    params = pltpu.CompilerParams(vmem_limit_bytes=24 * MIB)

    members = count * lax.axis_size("seq")
    piece_rows = point_weight.shape[0] // groups
    spread, piece = pl.pallas_call(
        send_kernel,
        out_shape=[
            jax.ShapeDtypeStruct((members, 1, row_count), tokens.dtype),
            jax.ShapeDtypeStruct((piece_rows, half), bf16),
        ],
        in_specs=[vmem, anywhere],
        out_specs=[vmem] * 2,
        scratch_shapes=[pltpu.SemaphoreType.DMA],
        compiler_params=params,
        cost_estimate=cost("early"),
        name="send",
    )(tokens, pltpu.with_memory_space_constraint(point_weight, pltpu.HBM))
    bases = lax.all_to_all(spread, ("dp", "seq"), 0, 0, tiled=True)
    table_rows = 16 * kinds
    table, plain, gain_here, weight = pl.pallas_call(
        load_kernel,
        out_shape=[
            jax.ShapeDtypeStruct((table_rows, width), bf16),
            jax.ShapeDtypeStruct((table_rows, half), bf16),
            jax.ShapeDtypeStruct((1, depth), f32),
            jax.ShapeDtypeStruct(conv_weight.shape, bf16),
        ],
        in_specs=[vmem, vmem, anywhere],
        out_specs=[vmem] * 4,
        scratch_shapes=[
            pltpu.VMEM((table_rows, width), bf16),
            pltpu.SemaphoreType.DMA((len(weight_parts(conv_weight)),)),
        ],
        compiler_params=params,
        cost_estimate=cost("early"),
        name="load",
    )(stem_table, gain_in[None], pltpu.with_memory_space_constraint(conv_weight, pltpu.HBM))
    columns = lax.dynamic_slice_in_dim(point_weight, strand * half, half, axis=1)
    crossed = [lax.ppermute(piece, "dp", ring_pairs("dp", -step)) for step in range(1, count)]

    received = [[] for _ in CHUNKS]
    part = None
    for step in range(1, count):
        for index, (low, size) in enumerate(CHUNKS):
            rows = row_count // DILATION * size
            operands = [bases, table, gain_here, weight] + ([] if part is None else [part])
            part = pl.pallas_call(
                functools.partial(chunk_kernel, step, low, size, row_count),
                out_shape=jax.ShapeDtypeStruct((rows, inner), bf16),
                in_specs=[vmem] * 4 + [anywhere] * (len(operands) - 4),
                out_specs=vmem,
                scratch_shapes=[pltpu.VMEM((rows + 2 * size, depth), bf16)],
                compiler_params=params,
                cost_estimate=cost(f"sent{index}"),
                name="conv_sent",
            )(*operands)
            received[index].append(lax.ppermute(part, "dp", ring_pairs("dp", step)))

    places, pieces = [(0, 0)], [columns]
    for step in range(1, count):
        for turn in range(groups):
            piece = crossed[step - 1]
            if turn:
                piece = lax.ppermute(piece, "groups", ring_pairs("groups", -turn))
            places.append((step, turn))
            pieces.append(piece)

    own, res, point = pl.pallas_call(
        functools.partial(own_kernel, places, piece_rows),
        out_shape=[
            jax.ShapeDtypeStruct((row_count, inner), f32),
            jax.ShapeDtypeStruct((row_count, half), f32),
            jax.ShapeDtypeStruct((inner, half), bf16),
        ],
        in_specs=[vmem] * 5 + [anywhere] * (1 + len(pieces)),
        out_specs=[vmem] * 3,
        scratch_shapes=[
            pltpu.VMEM((row_count + 2 * DILATION, depth), bf16),
            pltpu.SemaphoreType.DMA((len(pieces),)),
        ],
        compiler_params=params,
        cost_estimate=cost("own"),
        name="conv_own",
    )(bases, table, plain, gain_here, weight, part, *pieces)

    out = None
    blocks = row_count // DILATION
    for index, tail in enumerate(TAILS):
        chunks = [CHUNKS[chunk] for chunk in tail]
        low, size = chunks[0][0], sum(size for _, size in chunks)
        parts = [part for chunk in tail for part in received[chunk]]
        middle = pl.pallas_call(
            functools.partial(middle_kernel, chunks, count - 1),
            out_shape=jax.ShapeDtypeStruct((blocks * size, inner), bf16),
            in_specs=[vmem] * (2 + len(parts)),
            out_specs=vmem,
            compiler_params=params,
            cost_estimate=cost(f"middle{index}"),
            name="middle",
        )(own, gain_mid[None], *parts)
        other = lax.ppermute(middle, "strand", ring_pairs("strand", 1))
        operands = [middle, other, res, point] + ([] if out is None else [out])
        out = pl.pallas_call(
            functools.partial(final_kernel, low, size),
            grid=(1,),
            out_shape=jax.ShapeDtypeStruct((blocks, DILATION, half), bf16),
            in_specs=[vmem] * 4 + [anywhere] * (len(operands) - 4),
            out_specs=pl.BlockSpec((blocks, size, half), lambda i, at=low // size: (0, at, 0)),
            input_output_aliases={} if out is None else {4: 0},
            compiler_params=params,
            cost_estimate=cost(f"final{index}"),
            name="final",
        )(*operands)
    return out.reshape(1, row_count, half)


def solution(mesh):
    return jax.shard_map(
        per_device,
        mesh=mesh,
        in_specs=(P(("groups", "dp"), "seq"), P(), P(None, "dp", None), P(), P(), P("dp", None)),
        out_specs=P(("groups", "dp"), "seq", "strand"),
        check_vma=False,
    )
```

```python
import functools

import jax
import jax.numpy as jnp
from jax import lax
from jax.experimental import pallas as pl
from jax.experimental.pallas import tpu as pltpu
from jax.sharding import PartitionSpec as P

DILATION = 256
EPS = 1e-06
ROW_STEP = 128
CHUNKS = ((0, 64), (64, 128), (192, 64))
TAILS = ((0, 1), (2,))
KINDS = 4
FLOPS = {
    "early": 0.1,
    "sent0": 5.0,
    "sent1": 15.0,
    "sent2": 0.5,
    "own": 15.0,
    "middle0": 5.0,
    "middle1": 5.0,
    "final0": 2.0,
    "final1": 5.0,
}
MIB = 2**20


def ring_pairs(axis, distance):
    count = lax.axis_size(axis)
    return [(i, (i + distance) % count) for i in range(count)]


def base_taps(tok_ref, step, row_count):
    count, blocks = lax.axis_size("dp"), lax.axis_size("seq")
    here = lax.axis_index("seq")
    first = lax.rem(lax.axis_index("dp") + step, count) * blocks
    sides = [jnp.maximum(here - 1, 0), here, jnp.minimum(here + 1, blocks - 1)]
    bases = jnp.concatenate([tok_ref[first + side] for side in sides], axis=1)
    width, span = 3 * row_count, row_count + 2 * DILATION
    spread = jnp.broadcast_to(bases, (16, width))
    start = width - (row_count - DILATION + 8)
    taps = pltpu.roll(spread, start, 1, stride=1, stride_axis=0)[:, :span]
    place = lax.broadcasted_iota(jnp.int32, (16, span), 1) + (here * row_count - DILATION)
    source = place + 8 - lax.broadcasted_iota(jnp.int32, (16, span), 0)
    length = blocks * row_count
    inside = (place >= 0) & (place < length) & (source >= 0) & (source < length)
    return jnp.where(inside, taps, -1).astype(jnp.float32).astype(jnp.bfloat16)


def one_hot(taps, second, table_rows):
    row = lax.broadcasted_iota(jnp.int32, (table_rows, 16), 0) // KINDS
    column = lax.broadcasted_iota(jnp.int32, (table_rows, 16), 1)
    chosen = (column == 15 - row + second * (2 * row - 14)).astype(jnp.float32)
    values = jnp.dot(chosen.astype(jnp.bfloat16), taps, preferred_element_type=jnp.float32)
    base = lax.broadcasted_iota(jnp.int32, values.shape, 0) % KINDS
    base = base + second * (KINDS - 1 - 2 * base)
    return (values == base.astype(jnp.float32)).astype(jnp.float32).T


def gelu(x):
    inner = x * (0.7978845608028654 + 0.035677408136300125 * (x * x))
    half = 0.5 * x
    return half + half * jnp.tanh(inner)


def activate(hot, table_ref, gain_ref, act_ref):
    depth = gain_ref.shape[1]
    for start in range(0, hot.shape[0], ROW_STEP):
        embedded = jnp.dot(
            hot[start : start + ROW_STEP], table_ref[...], preferred_element_type=jnp.float32
        )
        mean = jnp.mean(embedded * embedded, axis=-1, keepdims=True)
        scaled = embedded[:, :depth] * lax.rsqrt(mean + EPS) * gain_ref[...]
        act_ref[start : start + ROW_STEP] = gelu(scaled).astype(jnp.bfloat16)


def convolve(blocks, w_ref):
    second = lax.axis_index("strand")
    total = None
    for tap, block in enumerate(blocks):
        weight = w_ref[tap + second * (2 - 2 * tap)]
        part = jnp.dot(block, weight, preferred_element_type=jnp.float32)
        total = part if total is None else total + part
    return total


def send_kernel(tok_any, point_any, spread_ref, piece_ref, tok_ref, sems):
    rows, columns = piece_ref.shape
    low = pl.multiple_of(lax.axis_index("groups") * rows, 16)
    left = pl.multiple_of(lax.axis_index("strand") * columns, 128)
    part = point_any.at[pl.ds(low, rows), pl.ds(left, columns)]
    copies = [
        pltpu.make_async_copy(tok_any, tok_ref, sems.at[0]),
        pltpu.make_async_copy(part, piece_ref, sems.at[1]),
    ]
    for copy in copies:
        copy.start()
    copies[0].wait()
    spread_ref[...] = jnp.broadcast_to(tok_ref[...][None], spread_ref.shape)
    copies[1].wait()


def load_kernel(stem_any, gain_any, w_any, table_ref, plain_ref, gain_here_ref, w_ref, *scratch):
    stem_ref, gain_ref, flat_ref, sems = scratch
    depth = w_any.shape[1]
    copies = [
        pltpu.make_async_copy(stem_any, stem_ref, sems.at[0]),
        pltpu.make_async_copy(gain_any, gain_ref, sems.at[1]),
    ]
    for index, (tap, low, rows) in enumerate(weight_parts(w_any)):
        part = (tap, pl.ds(low, rows))
        copies.append(pltpu.make_async_copy(w_any.at[part], w_ref.at[part], sems.at[index + 2]))
    for copy in copies:
        copy.start()
    copies[0].wait()
    taps, kinds, width = stem_ref.shape
    slabs = [stem_ref[tap].astype(jnp.float32) for tap in range(taps)]
    slabs += [jnp.zeros((kinds, width), jnp.float32)] * (16 - taps)
    flat = jnp.concatenate(slabs)
    flat_ref[...] = flat.astype(jnp.bfloat16)
    left = lax.axis_index("dp") * depth
    turn = lax.rem(width - left, width)
    table_ref[...] = pltpu.roll(flat, turn, 1).astype(jnp.bfloat16)
    copies[1].wait()
    gain = jnp.broadcast_to(gain_ref[...].reshape(1, width), (8, width))
    gain_here_ref[...] = pltpu.roll(gain, turn, 1)[:1, :depth]
    half = plain_ref.shape[1]
    column = pl.multiple_of(lax.axis_index("strand") * half, 128)
    plain_ref[...] = flat_ref[:, pl.ds(column, half)]
    for copy in copies[2:]:
        copy.wait()


def weight_parts(weight):
    rows = weight.shape[1] // 2
    return [(tap, low, rows) for tap in range(weight.shape[0]) for low in (0, rows)]


def chunk_kernel(step, low, size, row_count, out_index, *refs):
    tok_ref, table_ref, gain_ref, w_ref = refs[:4]
    out_ref, act_ref = refs[out_index], refs[-1]
    taps = base_taps(tok_ref, step, row_count)
    hot = one_hot(taps, lax.axis_index("strand"), table_ref.shape[0])
    blocks = row_count // DILATION
    pieces = [hot[b * DILATION + low :][:size] for b in range(blocks + 2)]
    activate(jnp.concatenate(pieces).astype(jnp.bfloat16), table_ref, gain_ref, act_ref)
    parts = [act_ref[t * size : (t + blocks) * size] for t in range(3)]
    out_ref[...] = convolve(parts, w_ref).astype(jnp.bfloat16)


def rows_of(ref, low, size):
    starts = range(low, ref.shape[0], DILATION)
    return jnp.concatenate([ref[start : start + size] for start in starts])


def middle_of(own_ref, gain_ref, parts, low, size):
    total = rows_of(own_ref, low, size)
    for ref in parts:
        total = total + ref[...].astype(jnp.float32)
    mean = jnp.mean(total * total, axis=-1, keepdims=True)
    return gelu(total * lax.rsqrt(mean + EPS) * gain_ref[...].reshape(1, -1)).astype(
        jnp.bfloat16
    )


def own_kernel(places, piece_rows, *refs):
    tok_ref, table_ref, plain_ref, gain_ref, w_ref = refs[:5]
    pieces = refs[6 : 6 + len(places)]
    out_ref, res_ref, point_ref, act_ref, sems = refs[6 + len(places) :]
    ranks, groups = lax.axis_size("dp"), lax.axis_size("groups")
    me, group = lax.axis_index("dp"), lax.axis_index("groups")
    copies = []
    for index, (step, turn) in enumerate(places):
        place = lax.rem(me + step, ranks) * (piece_rows * groups)
        if step:
            place = place + lax.rem(group + turn, groups) * piece_rows
        source = pieces[index]
        if not step:
            columns = point_ref.shape[1]
            left = pl.multiple_of(lax.axis_index("strand") * columns, 128)
            source = source.at[:, pl.ds(left, columns)]
        target = pl.ds(pl.multiple_of(place, 16), source.shape[0])
        copies.append(pltpu.make_async_copy(source, point_ref.at[target], sems.at[index]))
        copies[-1].start()
    row_count = out_ref.shape[0]
    second = lax.axis_index("strand")
    taps = base_taps(tok_ref, 0, row_count)
    hot = one_hot(taps, second, table_ref.shape[0])
    here = slice(DILATION, DILATION + row_count)
    both = hot[here] + one_hot(taps[:, here], 1 - second, table_ref.shape[0])
    res_ref[...] = jnp.dot(
        both.astype(jnp.bfloat16), plain_ref[...], preferred_element_type=jnp.float32
    )
    activate(hot.astype(jnp.bfloat16), table_ref, gain_ref, act_ref)
    blocks = [act_ref[t * DILATION : t * DILATION + row_count] for t in range(3)]
    out_ref[...] = convolve(blocks, w_ref)
    for copy in copies:
        copy.wait()


def middle_kernel(chunks, count, own_ref, gain_ref, *refs):
    out_ref = refs[-1]
    first, total_size = chunks[0][0], sum(size for _, size in chunks)
    for index, (low, size) in enumerate(chunks):
        parts = refs[index * count : (index + 1) * count]
        value = middle_of(own_ref, gain_ref, parts, low, size)
        for block in range(own_ref.shape[0] // DILATION):
            start = block * total_size + low - first
            out_ref[start : start + size] = value[block * size : (block + 1) * size]


def final_kernel(low, size, mine_ref, other_ref, res_ref, point_ref, *refs):
    out_ref = refs[-1]
    total = mine_ref[...].astype(jnp.float32) + other_ref[...].astype(jnp.float32)
    branch = jnp.dot(
        total.astype(jnp.bfloat16), point_ref[...], preferred_element_type=jnp.float32
    )
    value = (0.5 * (branch + rows_of(res_ref, low, size))).astype(jnp.bfloat16)
    out_ref[...] = value.reshape(out_ref.shape)


def pinned(x):
    return pltpu.with_memory_space_constraint(x, pltpu.VMEM)


def in_hbm(x):
    return pltpu.with_memory_space_constraint(x, pltpu.HBM)


def cost(kind):
    return pl.CostEstimate(
        flops=int(1e9 * FLOPS[kind]), bytes_accessed=2**20, transcendentals=0
    )


def per_device(tokens, stem_table, conv_weight, gain_in, gain_mid, point_weight):
    row_count = tokens.shape[1]
    kinds, width = stem_table.shape[1:]
    depth, inner = conv_weight.shape[1:]
    count, groups = lax.axis_size("dp"), lax.axis_size("groups")
    strand = lax.axis_index("strand")
    half = width // 2
    vmem = pl.BlockSpec(memory_space=pltpu.VMEM)
    anywhere = pl.BlockSpec(memory_space=pl.ANY)
    bf16, f32 = jnp.bfloat16, jnp.float32
    params = pltpu.CompilerParams(vmem_limit_bytes=24 * MIB)

    members = count * lax.axis_size("seq")
    piece_rows = point_weight.shape[0] // groups
    spread, piece = pl.pallas_call(
        send_kernel,
        out_shape=[
            jax.ShapeDtypeStruct((members, 1, row_count), tokens.dtype),
            jax.ShapeDtypeStruct((piece_rows, half), bf16),
        ],
        in_specs=[anywhere] * 2,
        out_specs=[vmem] * 2,
        scratch_shapes=[pltpu.VMEM(tokens.shape, tokens.dtype), pltpu.SemaphoreType.DMA((2,))],
        compiler_params=params,
        cost_estimate=cost("early"),
        name="send",
    )(in_hbm(tokens), in_hbm(point_weight))
    bases = lax.all_to_all(spread, ("dp", "seq"), 0, 0, tiled=True)
    table_rows = 16 * kinds
    table, plain, gain_here, weight = pl.pallas_call(
        load_kernel,
        out_shape=[
            pltpu.VMEM((table_rows, width), bf16),
            pltpu.VMEM((table_rows, half), bf16),
            pltpu.VMEM((1, depth), f32),
            pltpu.VMEM(conv_weight.shape, bf16),
        ],
        in_specs=[anywhere] * 3,
        out_specs=[vmem] * 4,
        scratch_shapes=[
            pltpu.VMEM(stem_table.shape, bf16),
            pltpu.VMEM(gain_in.shape, f32),
            pltpu.VMEM((table_rows, width), bf16),
            pltpu.SemaphoreType.DMA((2 + len(weight_parts(conv_weight)),)),
        ],
        compiler_params=params,
        cost_estimate=cost("early"),
        name="load",
    )(in_hbm(stem_table), in_hbm(gain_in), in_hbm(conv_weight))
    crossed = [lax.ppermute(piece, "dp", ring_pairs("dp", -step)) for step in range(1, count)]

    received = [[] for _ in CHUNKS]
    part = None
    for step in range(1, count):
        for index, (low, size) in enumerate(CHUNKS):
            rows = row_count // DILATION * size
            operands = [bases] + [pinned(x) for x in (table, gain_here, weight)]
            shapes = [jax.ShapeDtypeStruct((rows, inner), bf16)]
            if not index:
                operands.append(crossed[step - 1])
                shapes.append(jax.ShapeDtypeStruct(crossed[step - 1].shape, bf16))
            if part is not None:
                operands.append(part)
            part, *passed = pl.pallas_call(
                functools.partial(chunk_kernel, step, low, size, row_count, len(operands)),
                out_shape=shapes,
                in_specs=[vmem] * 4 + [anywhere] * (len(operands) - 4),
                out_specs=[vmem, anywhere][: len(shapes)],
                scratch_shapes=[pltpu.VMEM((rows + 2 * size, depth), bf16)],
                input_output_aliases={} if index else {4: 1},
                compiler_params=params,
                cost_estimate=cost(f"sent{index}"),
                name="conv_sent",
            )(*operands)
            if passed:
                crossed[step - 1] = passed[0]
            received[index].append(lax.ppermute(part, "dp", ring_pairs("dp", step)))

    places, pieces = [(0, 0)], [in_hbm(point_weight)]
    for step in range(1, count):
        for turn in range(groups):
            piece = crossed[step - 1]
            if turn:
                piece = lax.ppermute(piece, "groups", ring_pairs("groups", -turn))
            places.append((step, turn))
            pieces.append(piece)

    own, res, point = pl.pallas_call(
        functools.partial(own_kernel, places, piece_rows),
        out_shape=[
            jax.ShapeDtypeStruct((row_count, inner), f32),
            jax.ShapeDtypeStruct((row_count, half), f32),
            jax.ShapeDtypeStruct((inner, half), bf16),
        ],
        in_specs=[vmem] * 5 + [anywhere] * (1 + len(pieces)),
        out_specs=[vmem] * 3,
        scratch_shapes=[
            pltpu.VMEM((row_count + 2 * DILATION, depth), bf16),
            pltpu.SemaphoreType.DMA((len(pieces),)),
        ],
        compiler_params=params,
        cost_estimate=cost("own"),
        name="conv_own",
    )(bases, *[pinned(x) for x in (table, plain, gain_here, weight)], part, *pieces)

    out = None
    blocks = row_count // DILATION
    for index, tail in enumerate(TAILS):
        chunks = [CHUNKS[chunk] for chunk in tail]
        low, size = chunks[0][0], sum(size for _, size in chunks)
        parts = [part for chunk in tail for part in received[chunk]]
        middle = pl.pallas_call(
            functools.partial(middle_kernel, chunks, count - 1),
            out_shape=jax.ShapeDtypeStruct((blocks * size, inner), bf16),
            in_specs=[vmem] * (2 + len(parts)),
            out_specs=vmem,
            compiler_params=params,
            cost_estimate=cost(f"middle{index}"),
            name="middle",
        )(own, gain_mid, *parts)
        other = lax.ppermute(middle, "strand", ring_pairs("strand", 1))
        operands = [middle, other, res, point] + ([] if out is None else [out])
        out = pl.pallas_call(
            functools.partial(final_kernel, low, size),
            grid=(1,),
            out_shape=jax.ShapeDtypeStruct((blocks, DILATION, half), bf16),
            in_specs=[vmem] * 4 + [anywhere] * (len(operands) - 4),
            out_specs=pl.BlockSpec((blocks, size, half), lambda i, at=low // size: (0, at, 0)),
            input_output_aliases={} if out is None else {4: 0},
            compiler_params=params,
            cost_estimate=cost(f"final{index}"),
            name="final",
        )(*operands)
    return out.reshape(1, row_count, half)


def solution(mesh):
    return jax.shard_map(
        per_device,
        mesh=mesh,
        in_specs=(P(("groups", "dp"), "seq"), P(), P(None, "dp", None), P(), P(), P("dp", None)),
        out_specs=P(("groups", "dp"), "seq", "strand"),
        check_vma=False,
    )
```

```python
import functools

import jax
import jax.numpy as jnp
from jax import lax
from jax.experimental import pallas as pl
from jax.experimental.pallas import tpu as pltpu
from jax.sharding import PartitionSpec as P

DILATION = 256
EPS = 1e-06
ROW_STEP = 128
CHUNKS = ((0, 96), (96, 96), (192, 64))
TAILS = ((0, 1), (2,))
KINDS = 4
TABLE = 16 * KINDS
FLOPS = {
    "early": 0.1,
    "load": 0.1,
    "sent0": 15.0,
    "sent1": 0.5,
    "sent2": 15.0,
    "own": 15.0,
    "middle0": 0.05,
    "middle1": 5.0,
    "final0": 0.5,
    "final1": 15.0,
}
MIB = 2**20


def line_pairs(axis, distance):
    count = lax.axis_size(axis)
    return [(i, i + distance) for i in range(count) if 0 <= i + distance < count]


def ring_pairs(axis, distance):
    count = lax.axis_size(axis)
    return [(i, (i + distance) % count) for i in range(count)]


def base_taps(sides, step, row_count):
    blocks, here = lax.axis_size("seq"), lax.axis_index("seq")
    low = step * row_count
    bases = jnp.concatenate([ref[:, low : low + row_count] for ref in sides], axis=1)
    width, span = 3 * row_count, row_count + 2 * DILATION
    spread = jnp.broadcast_to(bases, (16, width))
    start = width - (row_count - DILATION + 8)
    taps = pltpu.roll(spread, start, 1, stride=1, stride_axis=0)[:, :span]
    place = lax.broadcasted_iota(jnp.int32, (16, span), 1) + (here * row_count - DILATION)
    source = place + 8 - lax.broadcasted_iota(jnp.int32, (16, span), 0)
    length = blocks * row_count
    inside = (place >= 0) & (place < length) & (source >= 0) & (source < length)
    return jnp.where(inside, taps, -1).astype(jnp.float32).astype(jnp.bfloat16)


def one_hot(taps, second):
    row = lax.broadcasted_iota(jnp.int32, (TABLE, 16), 0) // KINDS
    column = lax.broadcasted_iota(jnp.int32, (TABLE, 16), 1)
    chosen = (column == 15 - row + second * (2 * row - 14)).astype(jnp.float32)
    values = jnp.dot(chosen.astype(jnp.bfloat16), taps, preferred_element_type=jnp.float32)
    base = lax.broadcasted_iota(jnp.int32, values.shape, 0) % KINDS
    base = base + second * (KINDS - 1 - 2 * base)
    return (values == base.astype(jnp.float32)).astype(jnp.float32).T


def gelu(x):
    inner = x * (0.7978845608028654 + 0.035677408136300125 * (x * x))
    half = 0.5 * x
    return half + half * jnp.tanh(inner)


def activate(hot, gain_ref, pack_ref, act_ref):
    depth, width = act_ref.shape[1], gain_ref.shape[0]
    turn = lax.rem(width - lax.axis_index("dp") * depth, width)
    gain = jnp.broadcast_to(gain_ref[...].reshape(1, width), (8, width))
    gain = pltpu.roll(gain, turn, 1)[:1, :depth]
    tables = [pack_ref[rows] for rows in table_rows(depth, width, pack_ref.shape[1])]
    for start in range(0, hot.shape[0], ROW_STEP):
        rows = hot[start : start + ROW_STEP]
        parts = [jnp.dot(rows, table, preferred_element_type=jnp.float32) for table in tables]
        mean = sum(jnp.sum(part * part, axis=-1, keepdims=True) for part in parts) * (1.0 / width)
        scaled = parts[0][:, :depth] * lax.rsqrt(mean + EPS) * gain
        act_ref[start : start + ROW_STEP] = gelu(scaled).astype(jnp.bfloat16)


def convolve(blocks, pack_ref):
    second = lax.axis_index("strand")
    total = None
    for tap, block in enumerate(blocks):
        depth = block.shape[1]
        row = pl.multiple_of((tap + second * (2 - 2 * tap)) * depth, 16)
        weight = pack_ref[pl.ds(row, depth), :]
        part = jnp.dot(block, weight, preferred_element_type=jnp.float32)
        total = part if total is None else total + part
    return total


def table_rows(depth, width, columns):
    first = 3 * depth
    count = width // columns
    return [slice(first + i * TABLE, first + (i + 1) * TABLE) for i in range(count)]


def plain_rows(depth, width, columns):
    first = 3 * depth + width // columns * TABLE
    return slice(first, first + TABLE)


def slice_kernel(point_any, tok_any, piece_ref, tok_ref, sems):
    rows, columns = piece_ref.shape
    low = pl.multiple_of(lax.axis_index("groups") * rows, 16)
    left = pl.multiple_of(lax.axis_index("strand") * columns, 128)
    part = point_any.at[pl.ds(low, rows), pl.ds(left, columns)]
    copies = [
        pltpu.make_async_copy(part, piece_ref, sems.at[0]),
        pltpu.make_async_copy(tok_any, tok_ref, sems.at[1]),
    ]
    for copy in copies:
        copy.start()
    for copy in copies:
        copy.wait()


def join_kernel(*refs):
    refs[-1][...] = jnp.concatenate([ref[...] for ref in refs[:-1]], axis=1)


def load_kernel(stem_any, w_any, pack_ref, stem_ref, flat_ref, sems):
    depth, columns = w_any.shape[1:]
    copies = [pltpu.make_async_copy(stem_any, stem_ref, sems.at[0])]
    for index, (tap, low, rows) in enumerate(weight_parts(w_any)):
        source = w_any.at[tap, pl.ds(low, rows)]
        target = pack_ref.at[pl.ds(tap * depth + low, rows)]
        copies.append(pltpu.make_async_copy(source, target, sems.at[index + 1]))
    for copy in copies:
        copy.start()
    copies[0].wait()
    taps, kinds, width = stem_ref.shape
    slabs = [stem_ref[tap].astype(jnp.float32) for tap in range(taps)]
    slabs += [jnp.zeros((kinds, width), jnp.float32)] * (16 - taps)
    flat = jnp.concatenate(slabs)
    flat_ref[...] = flat.astype(jnp.bfloat16)
    turn = lax.rem(width - lax.axis_index("dp") * depth, width)
    turned = pltpu.roll(flat, turn, 1).astype(jnp.bfloat16)
    for index, rows in enumerate(table_rows(depth, width, columns)):
        pack_ref[rows] = turned[:, index * columns : (index + 1) * columns]
    column = pl.multiple_of(lax.axis_index("strand") * columns, 128)
    pack_ref[plain_rows(depth, width, columns)] = flat_ref[:, pl.ds(column, columns)]
    for copy in copies[1:]:
        copy.wait()


def weight_parts(weight):
    rows = weight.shape[1] // 2
    return [(tap, low, rows) for tap in range(weight.shape[0]) for low in (0, rows)]


def chunk_kernel(step, low, size, row_count, out_index, *refs):
    gain_ref, pack_ref = refs[3:5]
    out_ref, act_ref = refs[out_index], refs[-1]
    hot = one_hot(base_taps(refs[:3], step, row_count), lax.axis_index("strand"))
    blocks = row_count // DILATION
    pieces = [hot[b * DILATION + low :][:size] for b in range(blocks + 2)]
    activate(jnp.concatenate(pieces).astype(jnp.bfloat16), gain_ref, pack_ref, act_ref)
    parts = [act_ref[t * size : (t + blocks) * size] for t in range(3)]
    out_ref[...] = convolve(parts, pack_ref).astype(jnp.bfloat16)


def rows_of(ref, low, size):
    starts = range(low, ref.shape[0], DILATION)
    return jnp.concatenate([ref[start : start + size] for start in starts])


def middle_of(own_ref, gain_ref, parts, low, size):
    total = rows_of(own_ref, low, size)
    for ref in parts:
        total = total + ref[...].astype(jnp.float32)
    mean = jnp.mean(total * total, axis=-1, keepdims=True)
    return gelu(total * lax.rsqrt(mean + EPS) * gain_ref[...].reshape(1, -1)).astype(
        jnp.bfloat16
    )


def own_kernel(places, piece_rows, *refs):
    gain_ref, pack_ref = refs[3:5]
    pieces = refs[6 : 6 + len(places)]
    out_ref, res_ref, point_ref, act_ref, sems = refs[6 + len(places) :]
    ranks, groups = lax.axis_size("dp"), lax.axis_size("groups")
    me, group = lax.axis_index("dp"), lax.axis_index("groups")
    copies = []
    for index, (step, turn) in enumerate(places):
        place = lax.rem(me + step, ranks) * (piece_rows * groups)
        if step:
            place = place + lax.rem(group + turn, groups) * piece_rows
        source = pieces[index]
        if not step:
            columns = point_ref.shape[1]
            left = pl.multiple_of(lax.axis_index("strand") * columns, 128)
            source = source.at[:, pl.ds(left, columns)]
        target = pl.ds(pl.multiple_of(place, 16), source.shape[0])
        copies.append(pltpu.make_async_copy(source, point_ref.at[target], sems.at[index]))
        copies[-1].start()
    row_count = out_ref.shape[0]
    second = lax.axis_index("strand")
    taps = base_taps(refs[:3], 0, row_count)
    hot = one_hot(taps, second)
    here = slice(DILATION, DILATION + row_count)
    both = (hot[here] + one_hot(taps[:, here], 1 - second)).astype(jnp.bfloat16)
    plain = pack_ref[plain_rows(act_ref.shape[1], gain_ref.shape[0], pack_ref.shape[1])]
    res_ref[...] = jnp.dot(both, plain, preferred_element_type=jnp.float32)
    activate(hot.astype(jnp.bfloat16), gain_ref, pack_ref, act_ref)
    blocks = [act_ref[t * DILATION : t * DILATION + row_count] for t in range(3)]
    out_ref[...] = convolve(blocks, pack_ref)
    for copy in copies:
        copy.wait()


def middle_kernel(chunks, count, own_ref, gain_ref, *refs):
    out_ref = refs[-1]
    first, total_size = chunks[0][0], sum(size for _, size in chunks)
    for index, (low, size) in enumerate(chunks):
        parts = refs[index * count : (index + 1) * count]
        value = middle_of(own_ref, gain_ref, parts, low, size)
        for block in range(own_ref.shape[0] // DILATION):
            start = block * total_size + low - first
            out_ref[start : start + size] = value[block * size : (block + 1) * size]


def final_kernel(low, size, mine_ref, other_ref, res_ref, point_ref, *refs):
    out_ref = refs[-1]
    total = mine_ref[...].astype(jnp.float32) + other_ref[...].astype(jnp.float32)
    branch = jnp.dot(
        total.astype(jnp.bfloat16), point_ref[...], preferred_element_type=jnp.float32
    )
    value = (0.5 * (branch + rows_of(res_ref, low, size))).astype(jnp.bfloat16)
    out_ref[...] = value.reshape(out_ref.shape)


def in_hbm(x):
    return pltpu.with_memory_space_constraint(x, pltpu.HBM)


def cost(kind):
    return pl.CostEstimate(
        flops=int(1e9 * FLOPS[kind]), bytes_accessed=2**20, transcendentals=0
    )


def per_device(tokens, stem_table, conv_weight, gain_in, gain_mid, point_weight):
    row_count = tokens.shape[1]
    width = stem_table.shape[2]
    depth, inner = conv_weight.shape[1:]
    count, groups = lax.axis_size("dp"), lax.axis_size("groups")
    half = width // 2
    vmem = pl.BlockSpec(memory_space=pltpu.VMEM)
    anywhere = pl.BlockSpec(memory_space=pl.ANY)
    bf16, f32 = jnp.bfloat16, jnp.float32
    params = pltpu.CompilerParams(vmem_limit_bytes=24 * MIB)

    others = [lax.ppermute(tokens, "dp", ring_pairs("dp", -step)) for step in range(1, count)]
    piece_rows = point_weight.shape[0] // groups
    piece, here = pl.pallas_call(
        slice_kernel,
        out_shape=[
            jax.ShapeDtypeStruct((piece_rows, half), bf16),
            jax.ShapeDtypeStruct(tokens.shape, tokens.dtype),
        ],
        in_specs=[anywhere] * 2,
        out_specs=[vmem] * 2,
        scratch_shapes=[pltpu.SemaphoreType.DMA((2,))],
        compiler_params=params,
        cost_estimate=cost("early"),
        name="point_slice",
    )(in_hbm(point_weight), in_hbm(tokens))
    joined = pl.pallas_call(
        join_kernel,
        out_shape=jax.ShapeDtypeStruct((1, count * row_count), tokens.dtype),
        in_specs=[vmem] * count,
        out_specs=vmem,
        compiler_params=params,
        cost_estimate=cost("early"),
        name="join",
    )(here, *others)
    below = lax.ppermute(joined, "seq", line_pairs("seq", 1))
    above = lax.ppermute(joined, "seq", line_pairs("seq", -1))
    pack_rows = 3 * depth + (width // inner + 1) * TABLE
    pack = pl.pallas_call(
        load_kernel,
        out_shape=jax.ShapeDtypeStruct((pack_rows, inner), bf16),
        in_specs=[anywhere] * 2,
        out_specs=vmem,
        scratch_shapes=[
            pltpu.VMEM(stem_table.shape, bf16),
            pltpu.VMEM((TABLE, width), bf16),
            pltpu.SemaphoreType.DMA((1 + len(weight_parts(conv_weight)),)),
        ],
        compiler_params=params,
        cost_estimate=cost("load"),
        name="load",
    )(in_hbm(stem_table), in_hbm(conv_weight))
    shared = [below, joined, above, gain_in, pack]
    crossed = [lax.ppermute(piece, "dp", ring_pairs("dp", -step)) for step in range(1, count)]

    received = [[] for _ in CHUNKS]
    for step in range(1, count):
        for index, (low, size) in enumerate(CHUNKS):
            rows = row_count // DILATION * size
            operands = list(shared)
            shapes = [jax.ShapeDtypeStruct((rows, inner), bf16)]
            if index == 1:
                operands.append(crossed[step - 1])
                shapes.append(jax.ShapeDtypeStruct(crossed[step - 1].shape, bf16))
            if index:
                operands.append(part)
            part, *passed = pl.pallas_call(
                functools.partial(chunk_kernel, step, low, size, row_count, len(operands)),
                out_shape=shapes,
                in_specs=[vmem] * 5 + [anywhere] * (len(operands) - 5),
                out_specs=[vmem, anywhere][: len(shapes)],
                scratch_shapes=[pltpu.VMEM((rows + 2 * size, depth), bf16)],
                input_output_aliases={5: 1} if index == 1 else {},
                compiler_params=params,
                cost_estimate=cost(f"sent{index}"),
                name="conv_sent",
            )(*operands)
            if passed:
                crossed[step - 1] = passed[0]
            received[index].append(lax.ppermute(part, "dp", ring_pairs("dp", step)))

    places, pieces = [(0, 0)], [in_hbm(point_weight)]
    for step in range(1, count):
        for turn in range(groups):
            piece = crossed[step - 1]
            if turn:
                piece = lax.ppermute(piece, "groups", ring_pairs("groups", -turn))
            places.append((step, turn))
            pieces.append(piece)

    own, res, point = pl.pallas_call(
        functools.partial(own_kernel, places, piece_rows),
        out_shape=[
            jax.ShapeDtypeStruct((row_count, inner), f32),
            jax.ShapeDtypeStruct((row_count, half), f32),
            jax.ShapeDtypeStruct((inner, half), bf16),
        ],
        in_specs=[vmem] * 5 + [anywhere] * (1 + len(pieces)),
        out_specs=[vmem] * 3,
        scratch_shapes=[
            pltpu.VMEM((row_count + 2 * DILATION, depth), bf16),
            pltpu.SemaphoreType.DMA((len(pieces),)),
        ],
        compiler_params=params,
        cost_estimate=cost("own"),
        name="conv_own",
    )(*shared, part, *pieces)

    out = None
    blocks = row_count // DILATION
    for index, tail in enumerate(TAILS):
        chunks = [CHUNKS[chunk] for chunk in tail]
        low, size = chunks[0][0], sum(size for _, size in chunks)
        parts = [part for chunk in tail for part in received[chunk]]
        middle = pl.pallas_call(
            functools.partial(middle_kernel, chunks, count - 1),
            out_shape=jax.ShapeDtypeStruct((blocks * size, inner), bf16),
            in_specs=[vmem] * (2 + len(parts)),
            out_specs=vmem,
            compiler_params=params,
            cost_estimate=cost(f"middle{index}"),
            name="middle",
        )(own, gain_mid, *parts)
        other = lax.ppermute(middle, "strand", ring_pairs("strand", 1))
        operands = [middle, other, res, point] + ([] if out is None else [out])
        out = pl.pallas_call(
            functools.partial(final_kernel, low, size),
            grid=(1,),
            out_shape=jax.ShapeDtypeStruct((blocks, DILATION, half), bf16),
            in_specs=[vmem] * 4 + [anywhere] * (len(operands) - 4),
            out_specs=pl.BlockSpec((blocks, size, half), lambda i, at=low // size: (0, at, 0)),
            input_output_aliases={} if out is None else {4: 0},
            compiler_params=params,
            cost_estimate=cost(f"final{index}"),
            name="final",
        )(*operands)
    return out.reshape(1, row_count, half)


def solution(mesh):
    return jax.shard_map(
        per_device,
        mesh=mesh,
        in_specs=(P(("groups", "dp"), "seq"), P(), P(None, "dp", None), P(), P(), P("dp", None)),
        out_specs=P(("groups", "dp"), "seq", "strand"),
        check_vma=False,
    )
```

```python
import functools

import jax
import jax.numpy as jnp
from jax import lax
from jax.experimental import pallas as pl
from jax.experimental.pallas import tpu as pltpu
from jax.sharding import PartitionSpec as P

DILATION = 256
EPS = 1e-06
ROW_STEP = 128
CHUNKS = ((0, 96), (96, 96), (192, 64))
TAILS = ((0, 1), (2,))
KINDS = 4
TABLE = 16 * KINDS
FLOPS = {
    "early": 0.1,
    "load": 0.1,
    "sent0": 15.0,
    "sent1": 0.5,
    "sent2": 15.0,
    "own": 15.0,
    "middle0": 0.05,
    "middle1": 5.0,
    "final0": 0.5,
    "final1": 15.0,
}
MIB = 2**20


def pair_pairs(axis, first):
    count = lax.axis_size(axis)
    pairs = [(i, i + 1) for i in range(first, count - 1, 2)]
    return pairs + [(target, source) for source, target in pairs]


def ring_pairs(axis, distance):
    count = lax.axis_size(axis)
    return [(i, (i + distance) % count) for i in range(count)]


def base_taps(sides, step, row_count):
    blocks, here = lax.axis_size("seq"), lax.axis_index("seq")
    low = step * row_count
    even, middle, odd = [ref[:, low : low + row_count] for ref in sides]
    second = lax.rem(here, 2) == 1
    below, above = jnp.where(second, even, odd), jnp.where(second, odd, even)
    bases = jnp.concatenate([below, middle, above], axis=1)
    width, span = 3 * row_count, row_count + 2 * DILATION
    spread = jnp.broadcast_to(bases, (16, width))
    start = width - (row_count - DILATION + 8)
    taps = pltpu.roll(spread, start, 1, stride=1, stride_axis=0)[:, :span]
    place = lax.broadcasted_iota(jnp.int32, (16, span), 1) + (here * row_count - DILATION)
    source = place + 8 - lax.broadcasted_iota(jnp.int32, (16, span), 0)
    length = blocks * row_count
    inside = (place >= 0) & (place < length) & (source >= 0) & (source < length)
    return jnp.where(inside, taps, -1).astype(jnp.float32).astype(jnp.bfloat16)


def one_hot(taps, second):
    row = lax.broadcasted_iota(jnp.int32, (TABLE, 16), 0) // KINDS
    column = lax.broadcasted_iota(jnp.int32, (TABLE, 16), 1)
    chosen = (column == 15 - row + second * (2 * row - 14)).astype(jnp.float32)
    values = jnp.dot(chosen.astype(jnp.bfloat16), taps, preferred_element_type=jnp.float32)
    base = lax.broadcasted_iota(jnp.int32, values.shape, 0) % KINDS
    base = base + second * (KINDS - 1 - 2 * base)
    return (values == base.astype(jnp.float32)).astype(jnp.float32).T


def gelu(x):
    inner = x * (0.7978845608028654 + 0.035677408136300125 * (x * x))
    half = 0.5 * x
    return half + half * jnp.tanh(inner)


def activate(hot, gain_ref, pack_ref, act_ref):
    depth, width = act_ref.shape[1], gain_ref.shape[0]
    turn = lax.rem(width - lax.axis_index("dp") * depth, width)
    gain = jnp.broadcast_to(gain_ref[...].reshape(1, width), (8, width))
    gain = pltpu.roll(gain, turn, 1)[:1, :depth]
    tables = [pack_ref[rows] for rows in table_rows(depth, width, pack_ref.shape[1])]
    for start in range(0, hot.shape[0], ROW_STEP):
        rows = hot[start : start + ROW_STEP]
        parts = [jnp.dot(rows, table, preferred_element_type=jnp.float32) for table in tables]
        mean = sum(jnp.sum(part * part, axis=-1, keepdims=True) for part in parts) * (1.0 / width)
        scaled = parts[0][:, :depth] * lax.rsqrt(mean + EPS) * gain
        act_ref[start : start + ROW_STEP] = gelu(scaled).astype(jnp.bfloat16)


def convolve(blocks, pack_ref):
    second = lax.axis_index("strand")
    total = None
    for tap, block in enumerate(blocks):
        depth = block.shape[1]
        row = pl.multiple_of((tap + second * (2 - 2 * tap)) * depth, 16)
        weight = pack_ref[pl.ds(row, depth), :]
        part = jnp.dot(block, weight, preferred_element_type=jnp.float32)
        total = part if total is None else total + part
    return total


def table_rows(depth, width, columns):
    first = 3 * depth
    count = width // columns
    return [slice(first + i * TABLE, first + (i + 1) * TABLE) for i in range(count)]


def plain_rows(depth, width, columns):
    first = 3 * depth + width // columns * TABLE
    return slice(first, first + TABLE)


def slice_kernel(point_any, tok_any, piece_ref, tok_ref, sems):
    rows, columns = piece_ref.shape
    low = pl.multiple_of(lax.axis_index("groups") * rows, 16)
    left = pl.multiple_of(lax.axis_index("strand") * columns, 128)
    part = point_any.at[pl.ds(low, rows), pl.ds(left, columns)]
    copies = [
        pltpu.make_async_copy(part, piece_ref, sems.at[0]),
        pltpu.make_async_copy(tok_any, tok_ref, sems.at[1]),
    ]
    for copy in copies:
        copy.start()
    for copy in copies:
        copy.wait()


def join_kernel(*refs):
    refs[-1][...] = jnp.concatenate([ref[...] for ref in refs[:-1]], axis=1)


def load_kernel(stem_any, w_any, pack_ref, stem_ref, flat_ref, sems):
    depth, columns = w_any.shape[1:]
    copies = [pltpu.make_async_copy(stem_any, stem_ref, sems.at[0])]
    for index, (tap, low, rows) in enumerate(weight_parts(w_any)):
        source = w_any.at[tap, pl.ds(low, rows)]
        target = pack_ref.at[pl.ds(tap * depth + low, rows)]
        copies.append(pltpu.make_async_copy(source, target, sems.at[index + 1]))
    for copy in copies:
        copy.start()
    copies[0].wait()
    taps, kinds, width = stem_ref.shape
    slabs = [stem_ref[tap].astype(jnp.float32) for tap in range(taps)]
    slabs += [jnp.zeros((kinds, width), jnp.float32)] * (16 - taps)
    flat = jnp.concatenate(slabs)
    flat_ref[...] = flat.astype(jnp.bfloat16)
    turn = lax.rem(width - lax.axis_index("dp") * depth, width)
    turned = pltpu.roll(flat, turn, 1).astype(jnp.bfloat16)
    for index, rows in enumerate(table_rows(depth, width, columns)):
        pack_ref[rows] = turned[:, index * columns : (index + 1) * columns]
    column = pl.multiple_of(lax.axis_index("strand") * columns, 128)
    pack_ref[plain_rows(depth, width, columns)] = flat_ref[:, pl.ds(column, columns)]
    for copy in copies[1:]:
        copy.wait()


def weight_parts(weight):
    rows = weight.shape[1] // 2
    return [(tap, low, rows) for tap in range(weight.shape[0]) for low in (0, rows)]


def chunk_kernel(step, low, size, row_count, out_index, *refs):
    gain_ref, pack_ref = refs[3:5]
    out_ref, act_ref = refs[out_index], refs[-1]
    taps = base_taps(refs[:3], step, row_count)
    blocks = row_count // DILATION
    starts = [block * DILATION + low for block in range(blocks + 2)]
    taps = jnp.concatenate([taps[:, start : start + size] for start in starts], axis=1)
    hot = one_hot(taps, lax.axis_index("strand")).astype(jnp.bfloat16)
    activate(hot, gain_ref, pack_ref, act_ref)
    parts = [act_ref[t * size : (t + blocks) * size] for t in range(3)]
    out_ref[...] = convolve(parts, pack_ref).astype(jnp.bfloat16)


def rows_of(ref, low, size):
    starts = range(low, ref.shape[0], DILATION)
    return jnp.concatenate([ref[start : start + size] for start in starts])


def middle_of(own_ref, gain_ref, parts, low, size):
    total = rows_of(own_ref, low, size)
    for ref in parts:
        total = total + ref[...].astype(jnp.float32)
    mean = jnp.mean(total * total, axis=-1, keepdims=True)
    return gelu(total * lax.rsqrt(mean + EPS) * gain_ref[...].reshape(1, -1)).astype(
        jnp.bfloat16
    )


def own_kernel(places, piece_rows, *refs):
    gain_ref, pack_ref = refs[3:5]
    pieces = refs[6 : 6 + len(places)]
    out_ref, res_ref, point_ref, act_ref, sems = refs[6 + len(places) :]
    ranks, groups = lax.axis_size("dp"), lax.axis_size("groups")
    me, group = lax.axis_index("dp"), lax.axis_index("groups")
    copies = []
    for index, (step, turn) in enumerate(places):
        place = lax.rem(me + step, ranks) * (piece_rows * groups)
        if step:
            place = place + lax.rem(group + turn, groups) * piece_rows
        source = pieces[index]
        if not step:
            columns = point_ref.shape[1]
            left = pl.multiple_of(lax.axis_index("strand") * columns, 128)
            source = source.at[:, pl.ds(left, columns)]
        target = pl.ds(pl.multiple_of(place, 16), source.shape[0])
        copies.append(pltpu.make_async_copy(source, point_ref.at[target], sems.at[index]))
        copies[-1].start()
    row_count = out_ref.shape[0]
    second = lax.axis_index("strand")
    taps = base_taps(refs[:3], 0, row_count)
    hot = one_hot(taps, second)
    here = slice(DILATION, DILATION + row_count)
    both = (hot[here] + one_hot(taps[:, here], 1 - second)).astype(jnp.bfloat16)
    plain = pack_ref[plain_rows(act_ref.shape[1], gain_ref.shape[0], pack_ref.shape[1])]
    res_ref[...] = jnp.dot(both, plain, preferred_element_type=jnp.float32)
    activate(hot.astype(jnp.bfloat16), gain_ref, pack_ref, act_ref)
    blocks = [act_ref[t * DILATION : t * DILATION + row_count] for t in range(3)]
    out_ref[...] = convolve(blocks, pack_ref)
    for copy in copies:
        copy.wait()


def middle_kernel(chunks, count, own_ref, gain_ref, *refs):
    out_ref = refs[-1]
    first, total_size = chunks[0][0], sum(size for _, size in chunks)
    for index, (low, size) in enumerate(chunks):
        parts = refs[index * count : (index + 1) * count]
        value = middle_of(own_ref, gain_ref, parts, low, size)
        for block in range(own_ref.shape[0] // DILATION):
            start = block * total_size + low - first
            out_ref[start : start + size] = value[block * size : (block + 1) * size]


def final_kernel(low, size, mine_ref, other_ref, res_ref, point_ref, *refs):
    out_ref = refs[-1]
    total = mine_ref[...].astype(jnp.float32) + other_ref[...].astype(jnp.float32)
    branch = jnp.dot(
        total.astype(jnp.bfloat16), point_ref[...], preferred_element_type=jnp.float32
    )
    value = (0.5 * (branch + rows_of(res_ref, low, size))).astype(jnp.bfloat16)
    out_ref[...] = value.reshape(out_ref.shape)


def in_hbm(x):
    return pltpu.with_memory_space_constraint(x, pltpu.HBM)


def cost(kind):
    return pl.CostEstimate(
        flops=int(1e9 * FLOPS[kind]), bytes_accessed=2**20, transcendentals=0
    )


def per_device(tokens, stem_table, conv_weight, gain_in, gain_mid, point_weight):
    row_count = tokens.shape[1]
    width = stem_table.shape[2]
    depth, inner = conv_weight.shape[1:]
    count, groups = lax.axis_size("dp"), lax.axis_size("groups")
    half = width // 2
    vmem = pl.BlockSpec(memory_space=pltpu.VMEM)
    anywhere = pl.BlockSpec(memory_space=pl.ANY)
    bf16, f32 = jnp.bfloat16, jnp.float32
    params = pltpu.CompilerParams(vmem_limit_bytes=24 * MIB)

    others = [lax.ppermute(tokens, "dp", ring_pairs("dp", -step)) for step in range(1, count)]
    piece_rows = point_weight.shape[0] // groups
    piece, here = pl.pallas_call(
        slice_kernel,
        out_shape=[
            jax.ShapeDtypeStruct((piece_rows, half), bf16),
            jax.ShapeDtypeStruct(tokens.shape, tokens.dtype),
        ],
        in_specs=[anywhere] * 2,
        out_specs=[vmem] * 2,
        scratch_shapes=[pltpu.SemaphoreType.DMA((2,))],
        compiler_params=params,
        cost_estimate=cost("early"),
        name="point_slice",
    )(in_hbm(point_weight), in_hbm(tokens))
    joined = pl.pallas_call(
        join_kernel,
        out_shape=jax.ShapeDtypeStruct((1, count * row_count), tokens.dtype),
        in_specs=[vmem] * count,
        out_specs=vmem,
        compiler_params=params,
        cost_estimate=cost("early"),
        name="join",
    )(here, *others)
    even = lax.ppermute(joined, "seq", pair_pairs("seq", 0))
    odd = lax.ppermute(joined, "seq", pair_pairs("seq", 1))
    pack_rows = 3 * depth + (width // inner + 1) * TABLE
    pack = pl.pallas_call(
        load_kernel,
        out_shape=jax.ShapeDtypeStruct((pack_rows, inner), bf16),
        in_specs=[anywhere] * 2,
        out_specs=vmem,
        scratch_shapes=[
            pltpu.VMEM(stem_table.shape, bf16),
            pltpu.VMEM((TABLE, width), bf16),
            pltpu.SemaphoreType.DMA((1 + len(weight_parts(conv_weight)),)),
        ],
        compiler_params=params,
        cost_estimate=cost("load"),
        name="load",
    )(in_hbm(stem_table), in_hbm(conv_weight))
    shared = [even, joined, odd, gain_in, pack]
    crossed = [lax.ppermute(piece, "dp", ring_pairs("dp", -step)) for step in range(1, count)]

    received = [[] for _ in CHUNKS]
    for step in range(1, count):
        for index, (low, size) in enumerate(CHUNKS):
            rows = row_count // DILATION * size
            operands = list(shared)
            shapes = [jax.ShapeDtypeStruct((rows, inner), bf16)]
            if index == 1:
                operands.append(crossed[step - 1])
                shapes.append(jax.ShapeDtypeStruct(crossed[step - 1].shape, bf16))
            if index:
                operands.append(part)
            part, *passed = pl.pallas_call(
                functools.partial(chunk_kernel, step, low, size, row_count, len(operands)),
                out_shape=shapes,
                in_specs=[vmem] * 5 + [anywhere] * (len(operands) - 5),
                out_specs=[vmem, anywhere][: len(shapes)],
                scratch_shapes=[pltpu.VMEM((rows + 2 * size, depth), bf16)],
                input_output_aliases={5: 1} if index == 1 else {},
                compiler_params=params,
                cost_estimate=cost(f"sent{index}"),
                name="conv_sent",
            )(*operands)
            if passed:
                crossed[step - 1] = passed[0]
            received[index].append(lax.ppermute(part, "dp", ring_pairs("dp", step)))

    places, pieces = [(0, 0)], [in_hbm(point_weight)]
    for step in range(1, count):
        for turn in range(groups):
            piece = crossed[step - 1]
            if turn:
                piece = lax.ppermute(piece, "groups", ring_pairs("groups", -turn))
            places.append((step, turn))
            pieces.append(piece)

    own, res, point = pl.pallas_call(
        functools.partial(own_kernel, places, piece_rows),
        out_shape=[
            jax.ShapeDtypeStruct((row_count, inner), f32),
            jax.ShapeDtypeStruct((row_count, half), f32),
            jax.ShapeDtypeStruct((inner, half), bf16),
        ],
        in_specs=[vmem] * 5 + [anywhere] * (1 + len(pieces)),
        out_specs=[vmem] * 3,
        scratch_shapes=[
            pltpu.VMEM((row_count + 2 * DILATION, depth), bf16),
            pltpu.SemaphoreType.DMA((len(pieces),)),
        ],
        compiler_params=params,
        cost_estimate=cost("own"),
        name="conv_own",
    )(*shared, part, *pieces)

    out = None
    blocks = row_count // DILATION
    for index, tail in enumerate(TAILS):
        chunks = [CHUNKS[chunk] for chunk in tail]
        low, size = chunks[0][0], sum(size for _, size in chunks)
        parts = [part for chunk in tail for part in received[chunk]]
        middle = pl.pallas_call(
            functools.partial(middle_kernel, chunks, count - 1),
            out_shape=jax.ShapeDtypeStruct((blocks * size, inner), bf16),
            in_specs=[vmem] * (2 + len(parts)),
            out_specs=vmem,
            compiler_params=params,
            cost_estimate=cost(f"middle{index}"),
            name="middle",
        )(own, gain_mid, *parts)
        other = lax.ppermute(middle, "strand", ring_pairs("strand", 1))
        operands = [middle, other, res, point] + ([] if out is None else [out])
        out = pl.pallas_call(
            functools.partial(final_kernel, low, size),
            grid=(1,),
            out_shape=jax.ShapeDtypeStruct((blocks, DILATION, half), bf16),
            in_specs=[vmem] * 4 + [anywhere] * (len(operands) - 4),
            out_specs=pl.BlockSpec((blocks, size, half), lambda i, at=low // size: (0, at, 0)),
            input_output_aliases={} if out is None else {4: 0},
            compiler_params=params,
            cost_estimate=cost(f"final{index}"),
            name="final",
        )(*operands)
    return out.reshape(1, row_count, half)


def solution(mesh):
    return jax.shard_map(
        per_device,
        mesh=mesh,
        in_specs=(P(("groups", "dp"), "seq"), P(), P(None, "dp", None), P(), P(), P("dp", None)),
        out_specs=P(("groups", "dp"), "seq", "strand"),
        check_vma=False,
    )
```

```python
import functools

import jax
import jax.numpy as jnp
from jax import lax
from jax.experimental import pallas as pl
from jax.experimental.pallas import tpu as pltpu
from jax.sharding import PartitionSpec as P

DILATION = 256
EPS = 1e-06
ROW_STEP = 128
CHUNKS = ((0, 96), (96, 96), (192, 64))
TAILS = ((0, 1), (2,))
EARLY_TAPS, LATE_TAPS = (0, 1), (2,)
KINDS = 4
TABLE = 16 * KINDS
FLOPS = {
    "early": 0.1,
    "load": 0.1,
    "sent0": 15.0,
    "sent1": 0.5,
    "sent2": 15.0,
    "own": 15.0,
    "middle0": 0.05,
    "middle1": 5.0,
    "final0": 0.5,
    "final1": 15.0,
}
MIB = 2**20


def pair_pairs(axis, first):
    count = lax.axis_size(axis)
    pairs = [(i, i + 1) for i in range(first, count - 1, 2)]
    return pairs + [(target, source) for source, target in pairs]


def ring_pairs(axis, distance):
    count = lax.axis_size(axis)
    return [(i, (i + distance) % count) for i in range(count)]


def base_taps(joined_ref, row_count):
    blocks, here = lax.axis_size("seq"), lax.axis_index("seq")
    bases = joined_ref[...]
    width, span = 3 * row_count, row_count + 2 * DILATION
    spread = jnp.broadcast_to(bases, (16, width))
    start = width - (row_count - DILATION + 8)
    taps = pltpu.roll(spread, start, 1, stride=1, stride_axis=0)[:, :span]
    place = lax.broadcasted_iota(jnp.int32, (16, span), 1) + (here * row_count - DILATION)
    source = place + 8 - lax.broadcasted_iota(jnp.int32, (16, span), 0)
    length = blocks * row_count
    inside = (place >= 0) & (place < length) & (source >= 0) & (source < length)
    return jnp.where(inside, taps, -1).astype(jnp.float32).astype(jnp.bfloat16)


def one_hot(taps, second):
    row = lax.broadcasted_iota(jnp.int32, (TABLE, 16), 0) // KINDS
    column = lax.broadcasted_iota(jnp.int32, (TABLE, 16), 1)
    chosen = (column == 15 - row + second * (2 * row - 14)).astype(jnp.float32)
    values = jnp.dot(chosen.astype(jnp.bfloat16), taps, preferred_element_type=jnp.float32)
    base = lax.broadcasted_iota(jnp.int32, values.shape, 0) % KINDS
    base = base + second * (KINDS - 1 - 2 * base)
    return (values == base.astype(jnp.float32)).astype(jnp.float32).T


def gelu(x):
    inner = x * (0.7978845608028654 + 0.035677408136300125 * (x * x))
    half = 0.5 * x
    return half + half * jnp.tanh(inner)


def activate(hot, gain_ref, pack_ref, act_ref):
    depth, width = act_ref.shape[1], gain_ref.shape[0]
    turn = lax.rem(width - lax.axis_index("dp") * depth, width)
    gain = jnp.broadcast_to(gain_ref[...].reshape(1, width), (8, width))
    gain = pltpu.roll(gain, turn, 1)[:1, :depth]
    tables = [pack_ref[rows] for rows in table_rows(depth, width, pack_ref.shape[1])]
    for start in range(0, hot.shape[0], ROW_STEP):
        rows = hot[start : start + ROW_STEP]
        parts = [jnp.dot(rows, table, preferred_element_type=jnp.float32) for table in tables]
        mean = sum(jnp.sum(part * part, axis=-1, keepdims=True) for part in parts) * (1.0 / width)
        scaled = parts[0][:, :depth] * lax.rsqrt(mean + EPS) * gain
        act_ref[start : start + ROW_STEP] = gelu(scaled).astype(jnp.bfloat16)


def convolve(blocks, pack_ref, copies=()):
    second = lax.axis_index("strand")
    depth = blocks[0].shape[1]
    total = None
    for row_block in EARLY_TAPS + LATE_TAPS:
        if row_block in LATE_TAPS:
            for copy in copies:
                copy.wait()
            copies = ()
        weight = pack_ref[row_block * depth : (row_block + 1) * depth]
        if row_block == 1:
            block = blocks[1]
        else:
            block = jnp.where(second == 1, blocks[2 - row_block], blocks[row_block])
        part = jnp.dot(block, weight, preferred_element_type=jnp.float32)
        total = part if total is None else total + part
    return total


def table_rows(depth, width, columns):
    first = 3 * depth
    count = width // columns
    return [slice(first + i * TABLE, first + (i + 1) * TABLE) for i in range(count)]


def plain_rows(depth, width, columns):
    first = 3 * depth + width // columns * TABLE
    return slice(first, first + TABLE)


def slice_kernel(point_any, tok_any, piece_ref, tok_ref, sems):
    rows, columns = piece_ref.shape
    low = pl.multiple_of(lax.axis_index("groups") * rows, 16)
    left = pl.multiple_of(lax.axis_index("strand") * columns, 128)
    part = point_any.at[pl.ds(low, rows), pl.ds(left, columns)]
    copies = [
        pltpu.make_async_copy(part, piece_ref, sems.at[0]),
        pltpu.make_async_copy(tok_any, tok_ref, sems.at[1]),
    ]
    for copy in copies:
        copy.start()
    for copy in copies:
        copy.wait()


def join_kernel(even_ref, here_ref, odd_ref, joined_ref):
    even, odd = even_ref[...], odd_ref[...]
    second = lax.rem(lax.axis_index("seq"), 2) == 1
    below, above = jnp.where(second, even, odd), jnp.where(second, odd, even)
    joined_ref[...] = jnp.concatenate([below, here_ref[...], above], axis=1)


def load_kernel(stem_any, w_any, pack_ref, stem_ref, flat_ref, sem, sems):
    depth, columns = w_any.shape[1:]
    copies = [pltpu.make_async_copy(stem_any, stem_ref, sem)]
    copies += weight_copies(w_any, pack_ref, EARLY_TAPS, sems)
    for copy in copies:
        copy.start()
    copies[0].wait()
    taps, kinds, width = stem_ref.shape
    slabs = [stem_ref[tap].astype(jnp.float32) for tap in range(taps)]
    slabs += [jnp.zeros((kinds, width), jnp.float32)] * (16 - taps)
    flat = jnp.concatenate(slabs)
    flat_ref[...] = flat.astype(jnp.bfloat16)
    turn = lax.rem(width - lax.axis_index("dp") * depth, width)
    turned = pltpu.roll(flat, turn, 1).astype(jnp.bfloat16)
    for index, rows in enumerate(table_rows(depth, width, columns)):
        pack_ref[rows] = turned[:, index * columns : (index + 1) * columns]
    column = pl.multiple_of(lax.axis_index("strand") * columns, 128)
    pack_ref[plain_rows(depth, width, columns)] = flat_ref[:, pl.ds(column, columns)]
    for copy in copies[1:]:
        copy.wait()


def weight_parts(weight, taps):
    rows = weight.shape[1] // 2
    return [(tap, low, rows) for tap in taps for low in (0, rows)]


def weight_copies(w_any, pack_ref, taps, sems):
    depth = w_any.shape[1]
    return [
        pltpu.make_async_copy(
            w_any.at[tap, pl.ds(low, rows)],
            pack_ref.at[pl.ds(tap * depth + low, rows)],
            sems.at[index],
        )
        for index, (tap, low, rows) in enumerate(weight_parts(w_any, taps))
    ]


def chunk_kernel(low, size, row_count, out_index, loading, *refs):
    tok_ref, gain_ref, pack_ref = refs[:3]
    out_ref, act_ref = refs[out_index], refs[out_index + 2 if loading else -1]
    copies = []
    if loading:
        pack_ref = refs[out_index + 1]
        copies = weight_copies(refs[3], pack_ref, LATE_TAPS, refs[-1])
    for copy in copies:
        copy.start()
    taps = base_taps(tok_ref, row_count)
    hot = one_hot(taps, lax.axis_index("strand"))
    blocks = row_count // DILATION
    pieces = [hot[b * DILATION + low :][:size] for b in range(blocks + 2)]
    activate(jnp.concatenate(pieces).astype(jnp.bfloat16), gain_ref, pack_ref, act_ref)
    parts = [act_ref[t * size : (t + blocks) * size] for t in range(3)]
    out_ref[...] = convolve(parts, pack_ref, copies).astype(jnp.bfloat16)


def rows_of(ref, low, size):
    starts = range(low, ref.shape[0], DILATION)
    return jnp.concatenate([ref[start : start + size] for start in starts])


def middle_of(own_ref, gain_ref, parts, low, size):
    total = rows_of(own_ref, low, size)
    for ref in parts:
        total = total + ref[...].astype(jnp.float32)
    mean = jnp.mean(total * total, axis=-1, keepdims=True)
    return gelu(total * lax.rsqrt(mean + EPS) * gain_ref[...].reshape(1, -1)).astype(
        jnp.bfloat16
    )


def own_kernel(places, piece_rows, *refs):
    tok_ref, gain_ref, pack_ref = refs[:3]
    pieces = refs[4 : 4 + len(places)]
    out_ref, res_ref, point_ref, act_ref, sems = refs[4 + len(places) :]
    ranks, groups = lax.axis_size("dp"), lax.axis_size("groups")
    me, group = lax.axis_index("dp"), lax.axis_index("groups")
    copies = []
    for index, (step, turn) in enumerate(places):
        place = lax.rem(me + step, ranks) * (piece_rows * groups)
        if step:
            place = place + lax.rem(group + turn, groups) * piece_rows
        source = pieces[index]
        if not step:
            columns = point_ref.shape[1]
            left = pl.multiple_of(lax.axis_index("strand") * columns, 128)
            source = source.at[:, pl.ds(left, columns)]
        target = pl.ds(pl.multiple_of(place, 16), source.shape[0])
        copies.append(pltpu.make_async_copy(source, point_ref.at[target], sems.at[index]))
        copies[-1].start()
    row_count = out_ref.shape[0]
    second = lax.axis_index("strand")
    taps = base_taps(tok_ref, row_count)
    hot = one_hot(taps, second)
    here = slice(DILATION, DILATION + row_count)
    both = (hot[here] + one_hot(taps[:, here], 1 - second)).astype(jnp.bfloat16)
    plain = pack_ref[plain_rows(act_ref.shape[1], gain_ref.shape[0], pack_ref.shape[1])]
    res_ref[...] = jnp.dot(both, plain, preferred_element_type=jnp.float32)
    activate(hot.astype(jnp.bfloat16), gain_ref, pack_ref, act_ref)
    blocks = [act_ref[t * DILATION : t * DILATION + row_count] for t in range(3)]
    out_ref[...] = convolve(blocks, pack_ref)
    for copy in copies:
        copy.wait()


def middle_kernel(chunks, count, own_ref, gain_ref, *refs):
    out_ref = refs[-1]
    first, total_size = chunks[0][0], sum(size for _, size in chunks)
    for index, (low, size) in enumerate(chunks):
        parts = refs[index * count : (index + 1) * count]
        value = middle_of(own_ref, gain_ref, parts, low, size)
        for block in range(own_ref.shape[0] // DILATION):
            start = block * total_size + low - first
            out_ref[start : start + size] = value[block * size : (block + 1) * size]


def final_kernel(low, size, mine_ref, other_ref, res_ref, point_ref, *refs):
    out_ref = refs[-1]
    total = mine_ref[...].astype(jnp.float32) + other_ref[...].astype(jnp.float32)
    branch = jnp.dot(
        total.astype(jnp.bfloat16), point_ref[...], preferred_element_type=jnp.float32
    )
    value = (0.5 * (branch + rows_of(res_ref, low, size))).astype(jnp.bfloat16)
    out_ref[...] = value.reshape(out_ref.shape)


def in_hbm(x):
    return pltpu.with_memory_space_constraint(x, pltpu.HBM)


def cost(kind):
    return pl.CostEstimate(
        flops=int(1e9 * FLOPS[kind]), bytes_accessed=2**20, transcendentals=0
    )


def per_device(tokens, stem_table, conv_weight, gain_in, gain_mid, point_weight):
    row_count = tokens.shape[1]
    width = stem_table.shape[2]
    depth, inner = conv_weight.shape[1:]
    count, groups = lax.axis_size("dp"), lax.axis_size("groups")
    half = width // 2
    vmem = pl.BlockSpec(memory_space=pltpu.VMEM)
    anywhere = pl.BlockSpec(memory_space=pl.ANY)
    bf16, f32 = jnp.bfloat16, jnp.float32
    params = pltpu.CompilerParams(vmem_limit_bytes=24 * MIB)

    even = lax.ppermute(tokens, "seq", pair_pairs("seq", 0))
    odd = lax.ppermute(tokens, "seq", pair_pairs("seq", 1))
    piece_rows = point_weight.shape[0] // groups
    piece, here = pl.pallas_call(
        slice_kernel,
        out_shape=[
            jax.ShapeDtypeStruct((piece_rows, half), bf16),
            jax.ShapeDtypeStruct(tokens.shape, tokens.dtype),
        ],
        in_specs=[anywhere] * 2,
        out_specs=[vmem] * 2,
        scratch_shapes=[pltpu.SemaphoreType.DMA((2,))],
        compiler_params=params,
        cost_estimate=cost("early"),
        name="point_slice",
    )(in_hbm(point_weight), in_hbm(tokens))
    joined = pl.pallas_call(
        join_kernel,
        out_shape=jax.ShapeDtypeStruct((1, 3 * row_count), tokens.dtype),
        in_specs=[vmem] * 3,
        out_specs=vmem,
        compiler_params=params,
        cost_estimate=cost("early"),
        name="join",
    )(even, here, odd)
    sequences = [joined] + [
        lax.ppermute(joined, "dp", ring_pairs("dp", -step)) for step in range(1, count)
    ]
    pack_rows = 3 * depth + (width // inner + 1) * TABLE
    pack = pl.pallas_call(
        load_kernel,
        out_shape=jax.ShapeDtypeStruct((pack_rows, inner), bf16),
        in_specs=[anywhere] * 2,
        out_specs=vmem,
        scratch_shapes=[
            pltpu.VMEM(stem_table.shape, bf16),
            pltpu.VMEM((TABLE, width), bf16),
            pltpu.SemaphoreType.DMA,
            pltpu.SemaphoreType.DMA((len(weight_parts(conv_weight, EARLY_TAPS)),)),
        ],
        compiler_params=params,
        cost_estimate=cost("load"),
        name="load",
    )(in_hbm(stem_table), in_hbm(conv_weight))
    crossed = [lax.ppermute(piece, "dp", ring_pairs("dp", -step)) for step in range(1, count)]

    received = [[] for _ in CHUNKS]
    for step in range(1, count):
        for index, (low, size) in enumerate(CHUNKS):
            rows = row_count // DILATION * size
            loading, passing = step == 1 and index == 0, index == 1
            operands = [sequences[step], gain_in, pack]
            shapes = [jax.ShapeDtypeStruct((rows, inner), bf16)]
            scratch = [pltpu.VMEM((rows + 2 * size, depth), bf16)]
            aliases = {}
            if loading:
                operands.append(in_hbm(conv_weight))
                shapes.append(jax.ShapeDtypeStruct(pack.shape, bf16))
                late = len(weight_parts(conv_weight, LATE_TAPS))
                scratch.append(pltpu.SemaphoreType.DMA((late,)))
                aliases = {2: 1}
            if passing:
                operands.append(crossed[step - 1])
                shapes.append(jax.ShapeDtypeStruct(crossed[step - 1].shape, bf16))
                aliases = {3: 1}
            if index:
                operands.append(part)
            part, *passed = pl.pallas_call(
                functools.partial(chunk_kernel, low, size, row_count, len(operands), loading),
                out_shape=shapes,
                in_specs=[vmem] * 3 + [anywhere] * (len(operands) - 3),
                out_specs=[vmem, vmem if loading else anywhere][: len(shapes)],
                scratch_shapes=scratch,
                input_output_aliases=aliases,
                compiler_params=params,
                cost_estimate=cost(f"sent{index}"),
                name="conv_sent",
            )(*operands)
            if loading:
                pack = passed.pop()
            if passed:
                crossed[step - 1] = passed[0]
            received[index].append(lax.ppermute(part, "dp", ring_pairs("dp", step)))

    places, pieces = [(0, 0)], [in_hbm(point_weight)]
    for step in range(1, count):
        for turn in range(groups):
            piece = crossed[step - 1]
            if turn:
                piece = lax.ppermute(piece, "groups", ring_pairs("groups", -turn))
            places.append((step, turn))
            pieces.append(piece)

    own, res, point = pl.pallas_call(
        functools.partial(own_kernel, places, piece_rows),
        out_shape=[
            jax.ShapeDtypeStruct((row_count, inner), f32),
            jax.ShapeDtypeStruct((row_count, half), f32),
            jax.ShapeDtypeStruct((inner, half), bf16),
        ],
        in_specs=[vmem] * 3 + [anywhere] * (1 + len(pieces)),
        out_specs=[vmem] * 3,
        scratch_shapes=[
            pltpu.VMEM((row_count + 2 * DILATION, depth), bf16),
            pltpu.SemaphoreType.DMA((len(pieces),)),
        ],
        compiler_params=params,
        cost_estimate=cost("own"),
        name="conv_own",
    )(joined, gain_in, pack, part, *pieces)

    out = None
    blocks = row_count // DILATION
    for index, tail in enumerate(TAILS):
        chunks = [CHUNKS[chunk] for chunk in tail]
        low, size = chunks[0][0], sum(size for _, size in chunks)
        parts = [part for chunk in tail for part in received[chunk]]
        middle = pl.pallas_call(
            functools.partial(middle_kernel, chunks, count - 1),
            out_shape=jax.ShapeDtypeStruct((blocks * size, inner), bf16),
            in_specs=[vmem] * (2 + len(parts)),
            out_specs=vmem,
            compiler_params=params,
            cost_estimate=cost(f"middle{index}"),
            name="middle",
        )(own, gain_mid, *parts)
        other = lax.ppermute(middle, "strand", ring_pairs("strand", 1))
        operands = [middle, other, res, point] + ([] if out is None else [out])
        out = pl.pallas_call(
            functools.partial(final_kernel, low, size),
            grid=(1,),
            out_shape=jax.ShapeDtypeStruct((blocks, DILATION, half), bf16),
            in_specs=[vmem] * 4 + [anywhere] * (len(operands) - 4),
            out_specs=pl.BlockSpec((blocks, size, half), lambda i, at=low // size: (0, at, 0)),
            input_output_aliases={} if out is None else {4: 0},
            compiler_params=params,
            cost_estimate=cost(f"final{index}"),
            name="final",
        )(*operands)
    return out.reshape(1, row_count, half)


def solution(mesh):
    return jax.shard_map(
        per_device,
        mesh=mesh,
        in_specs=(P(("groups", "dp"), "seq"), P(), P(None, "dp", None), P(), P(), P("dp", None)),
        out_specs=P(("groups", "dp"), "seq", "strand"),
        check_vma=False,
    )
```

```python
import functools

import jax
import jax.numpy as jnp
from jax import lax
from jax.experimental import pallas as pl
from jax.experimental.pallas import tpu as pltpu
from jax.sharding import PartitionSpec as P

DILATION = 256
EPS = 1e-06
ROW_STEP = 128
CHUNKS = ((0, 96), (96, 96), (192, 64))
TAILS = ((0, 1), (2,))
EARLY_TAPS, LATE_TAPS = (0, 1), (2,)
KINDS = 4
TABLE = 16 * KINDS
FLOPS = {
    "early": 0.1,
    "load": 0.1,
    "sent0": 15.0,
    "sent1": 0.5,
    "sent2": 15.0,
    "own": 15.0,
    "middle0": 0.05,
    "middle1": 5.0,
    "final0": 0.5,
    "final1": 15.0,
}
MIB = 2**20


def pair_pairs(axis, first):
    count = lax.axis_size(axis)
    pairs = [(i, i + 1) for i in range(first, count - 1, 2)]
    return pairs + [(target, source) for source, target in pairs]


def ring_pairs(axis, distance):
    count = lax.axis_size(axis)
    return [(i, (i + distance) % count) for i in range(count)]


def base_taps(sides, step, row_count):
    blocks, here = lax.axis_size("seq"), lax.axis_index("seq")
    low = step * row_count
    even, middle, odd = [ref[:, low : low + row_count] for ref in sides]
    second = lax.rem(here, 2) == 1
    below, above = jnp.where(second, even, odd), jnp.where(second, odd, even)
    bases = jnp.concatenate([below, middle, above], axis=1)
    width, span = 3 * row_count, row_count + 2 * DILATION
    spread = jnp.broadcast_to(bases, (16, width))
    start = width - (row_count - DILATION + 8)
    taps = pltpu.roll(spread, start, 1, stride=1, stride_axis=0)[:, :span]
    place = lax.broadcasted_iota(jnp.int32, (16, span), 1) + (here * row_count - DILATION)
    source = place + 8 - lax.broadcasted_iota(jnp.int32, (16, span), 0)
    length = blocks * row_count
    inside = (place >= 0) & (place < length) & (source >= 0) & (source < length)
    return jnp.where(inside, taps, -1).astype(jnp.float32).astype(jnp.bfloat16)


def one_hot(taps, second):
    row = lax.broadcasted_iota(jnp.int32, (TABLE, 16), 0) // KINDS
    column = lax.broadcasted_iota(jnp.int32, (TABLE, 16), 1)
    chosen = (column == 15 - row + second * (2 * row - 14)).astype(jnp.float32)
    values = jnp.dot(chosen.astype(jnp.bfloat16), taps, preferred_element_type=jnp.float32)
    base = lax.broadcasted_iota(jnp.int32, values.shape, 0) % KINDS
    base = base + second * (KINDS - 1 - 2 * base)
    return (values == base.astype(jnp.float32)).astype(jnp.float32).T


def gelu(x):
    inner = x * (0.7978845608028654 + 0.035677408136300125 * (x * x))
    half = 0.5 * x
    return half + half * jnp.tanh(inner)


def activate(hot, gain_ref, pack_ref, act_ref):
    depth, width = act_ref.shape[1], gain_ref.shape[0]
    turn = lax.rem(width - lax.axis_index("dp") * depth, width)
    gain = jnp.broadcast_to(gain_ref[...].reshape(1, width), (8, width))
    gain = pltpu.roll(gain, turn, 1)[:1, :depth]
    tables = [pack_ref[rows] for rows in table_rows(depth, width, pack_ref.shape[1])]
    for start in range(0, hot.shape[0], ROW_STEP):
        rows = hot[start : start + ROW_STEP]
        parts = [jnp.dot(rows, table, preferred_element_type=jnp.float32) for table in tables]
        mean = sum(jnp.sum(part * part, axis=-1, keepdims=True) for part in parts) * (1.0 / width)
        scaled = parts[0][:, :depth] * lax.rsqrt(mean + EPS) * gain
        act_ref[start : start + ROW_STEP] = gelu(scaled).astype(jnp.bfloat16)


def convolve(blocks, pack_ref, copies=()):
    second = lax.axis_index("strand")
    depth = blocks[0].shape[1]
    total = None
    for row_block in EARLY_TAPS + LATE_TAPS:
        if row_block in LATE_TAPS:
            for copy in copies:
                copy.wait()
            copies = ()
        weight = pack_ref[row_block * depth : (row_block + 1) * depth]
        if row_block == 1:
            block = blocks[1]
        else:
            block = jnp.where(second == 1, blocks[2 - row_block], blocks[row_block])
        part = jnp.dot(block, weight, preferred_element_type=jnp.float32)
        total = part if total is None else total + part
    return total


def table_rows(depth, width, columns):
    first = 3 * depth
    count = width // columns
    return [slice(first + i * TABLE, first + (i + 1) * TABLE) for i in range(count)]


def plain_rows(depth, width, columns):
    first = 3 * depth + width // columns * TABLE
    return slice(first, first + TABLE)


def slice_kernel(point_any, tok_any, piece_ref, tok_ref, sems):
    rows, columns = piece_ref.shape
    low = pl.multiple_of(lax.axis_index("groups") * rows, 16)
    left = pl.multiple_of(lax.axis_index("strand") * columns, 128)
    part = point_any.at[pl.ds(low, rows), pl.ds(left, columns)]
    copies = [
        pltpu.make_async_copy(part, piece_ref, sems.at[0]),
        pltpu.make_async_copy(tok_any, tok_ref, sems.at[1]),
    ]
    for copy in copies:
        copy.start()
    for copy in copies:
        copy.wait()


def join_kernel(*refs):
    refs[-1][...] = jnp.concatenate([ref[...] for ref in refs[:-1]], axis=1)


def load_kernel(stem_any, w_any, pack_ref, stem_ref, flat_ref, sem, sems):
    depth, columns = w_any.shape[1:]
    copies = [pltpu.make_async_copy(stem_any, stem_ref, sem)]
    copies += weight_copies(w_any, pack_ref, EARLY_TAPS, sems)
    for copy in copies:
        copy.start()
    copies[0].wait()
    taps, kinds, width = stem_ref.shape
    slabs = [stem_ref[tap].astype(jnp.float32) for tap in range(taps)]
    slabs += [jnp.zeros((kinds, width), jnp.float32)] * (16 - taps)
    flat = jnp.concatenate(slabs)
    flat_ref[...] = flat.astype(jnp.bfloat16)
    me = lax.axis_index("dp")
    if depth == columns:
        parts = [lax.rem(me + index, width // columns) for index in range(width // columns)]
        starts = [pl.multiple_of(part * columns, 128) for part in parts]
        turned = [flat_ref[:, pl.ds(start, columns)] for start in starts]
    else:
        whole = pltpu.roll(flat, lax.rem(width - me * depth, width), 1).astype(jnp.bfloat16)
        turned = jnp.split(whole, width // columns, axis=1)
    for rows, part in zip(table_rows(depth, width, columns), turned):
        pack_ref[rows] = part
    column = pl.multiple_of(lax.axis_index("strand") * columns, 128)
    pack_ref[plain_rows(depth, width, columns)] = flat_ref[:, pl.ds(column, columns)]
    for copy in copies[1:]:
        copy.wait()


def weight_parts(weight, taps):
    rows = weight.shape[1] // 2
    return [(tap, low, rows) for tap in taps for low in (0, rows)]


def weight_copies(w_any, pack_ref, taps, sems):
    depth = w_any.shape[1]
    return [
        pltpu.make_async_copy(
            w_any.at[tap, pl.ds(low, rows)],
            pack_ref.at[pl.ds(tap * depth + low, rows)],
            sems.at[index],
        )
        for index, (tap, low, rows) in enumerate(weight_parts(w_any, taps))
    ]


def chunk_kernel(step, low, size, row_count, out_index, loading, *refs):
    gain_ref, pack_ref = refs[3:5]
    out_ref, act_ref = refs[out_index], refs[out_index + 2 if loading else -1]
    copies = []
    if loading:
        pack_ref = refs[out_index + 1]
        copies = weight_copies(refs[5], pack_ref, LATE_TAPS, refs[-1])
    for copy in copies:
        copy.start()
    taps = base_taps(refs[:3], step, row_count)
    hot = one_hot(taps, lax.axis_index("strand"))
    blocks = row_count // DILATION
    pieces = [hot[b * DILATION + low :][:size] for b in range(blocks + 2)]
    activate(jnp.concatenate(pieces).astype(jnp.bfloat16), gain_ref, pack_ref, act_ref)
    parts = [act_ref[t * size : (t + blocks) * size] for t in range(3)]
    out_ref[...] = convolve(parts, pack_ref, copies).astype(jnp.bfloat16)


def rows_of(ref, low, size):
    starts = range(low, ref.shape[0], DILATION)
    return jnp.concatenate([ref[start : start + size] for start in starts])


def middle_of(own_ref, gain_ref, parts, low, size):
    total = rows_of(own_ref, low, size)
    for ref in parts:
        total = total + ref[...].astype(jnp.float32)
    mean = jnp.mean(total * total, axis=-1, keepdims=True)
    return gelu(total * lax.rsqrt(mean + EPS) * gain_ref[...].reshape(1, -1)).astype(
        jnp.bfloat16
    )


def own_kernel(places, piece_rows, *refs):
    gain_ref, pack_ref = refs[3:5]
    pieces = refs[6 : 6 + len(places)]
    out_ref, res_ref, point_ref, act_ref, sems = refs[6 + len(places) :]
    ranks, groups = lax.axis_size("dp"), lax.axis_size("groups")
    me, group = lax.axis_index("dp"), lax.axis_index("groups")
    copies = []
    for index, (step, turn) in enumerate(places):
        place = lax.rem(me + step, ranks) * (piece_rows * groups)
        if step:
            place = place + lax.rem(group + turn, groups) * piece_rows
        source = pieces[index]
        if not step:
            columns = point_ref.shape[1]
            left = pl.multiple_of(lax.axis_index("strand") * columns, 128)
            source = source.at[:, pl.ds(left, columns)]
        target = pl.ds(pl.multiple_of(place, 16), source.shape[0])
        copies.append(pltpu.make_async_copy(source, point_ref.at[target], sems.at[index]))
        copies[-1].start()
    row_count = out_ref.shape[0]
    second = lax.axis_index("strand")
    taps = base_taps(refs[:3], 0, row_count)
    hot = one_hot(taps, second)
    here = slice(DILATION, DILATION + row_count)
    both = (hot[here] + one_hot(taps[:, here], 1 - second)).astype(jnp.bfloat16)
    plain = pack_ref[plain_rows(act_ref.shape[1], gain_ref.shape[0], pack_ref.shape[1])]
    res_ref[...] = jnp.dot(both, plain, preferred_element_type=jnp.float32)
    activate(hot.astype(jnp.bfloat16), gain_ref, pack_ref, act_ref)
    blocks = [act_ref[t * DILATION : t * DILATION + row_count] for t in range(3)]
    out_ref[...] = convolve(blocks, pack_ref)
    for copy in copies:
        copy.wait()


def middle_kernel(chunks, count, own_ref, gain_ref, *refs):
    out_ref = refs[-1]
    first, total_size = chunks[0][0], sum(size for _, size in chunks)
    for index, (low, size) in enumerate(chunks):
        parts = refs[index * count : (index + 1) * count]
        value = middle_of(own_ref, gain_ref, parts, low, size)
        for block in range(own_ref.shape[0] // DILATION):
            start = block * total_size + low - first
            out_ref[start : start + size] = value[block * size : (block + 1) * size]


def final_kernel(low, size, mine_ref, other_ref, res_ref, point_ref, *refs):
    out_ref = refs[-1]
    total = mine_ref[...].astype(jnp.float32) + other_ref[...].astype(jnp.float32)
    branch = jnp.dot(
        total.astype(jnp.bfloat16), point_ref[...], preferred_element_type=jnp.float32
    )
    value = (0.5 * (branch + rows_of(res_ref, low, size))).astype(jnp.bfloat16)
    out_ref[...] = value.reshape(out_ref.shape)


def in_hbm(x):
    return pltpu.with_memory_space_constraint(x, pltpu.HBM)


def cost(kind):
    return pl.CostEstimate(
        flops=int(1e9 * FLOPS[kind]), bytes_accessed=2**20, transcendentals=0
    )


def per_device(tokens, stem_table, conv_weight, gain_in, gain_mid, point_weight):
    row_count = tokens.shape[1]
    width = stem_table.shape[2]
    depth, inner = conv_weight.shape[1:]
    count, groups = lax.axis_size("dp"), lax.axis_size("groups")
    half = width // 2
    vmem = pl.BlockSpec(memory_space=pltpu.VMEM)
    anywhere = pl.BlockSpec(memory_space=pl.ANY)
    bf16, f32 = jnp.bfloat16, jnp.float32
    params = pltpu.CompilerParams(vmem_limit_bytes=24 * MIB)

    others = [lax.ppermute(tokens, "dp", ring_pairs("dp", -step)) for step in range(1, count)]
    piece_rows = point_weight.shape[0] // groups
    piece, here = pl.pallas_call(
        slice_kernel,
        out_shape=[
            jax.ShapeDtypeStruct((piece_rows, half), bf16),
            jax.ShapeDtypeStruct(tokens.shape, tokens.dtype),
        ],
        in_specs=[anywhere] * 2,
        out_specs=[vmem] * 2,
        scratch_shapes=[pltpu.SemaphoreType.DMA((2,))],
        compiler_params=params,
        cost_estimate=cost("early"),
        name="point_slice",
    )(in_hbm(point_weight), in_hbm(tokens))
    joined = pl.pallas_call(
        join_kernel,
        out_shape=jax.ShapeDtypeStruct((1, count * row_count), tokens.dtype),
        in_specs=[vmem] * count,
        out_specs=vmem,
        compiler_params=params,
        cost_estimate=cost("early"),
        name="join",
    )(here, *others)
    even = lax.ppermute(joined, "seq", pair_pairs("seq", 0))
    odd = lax.ppermute(joined, "seq", pair_pairs("seq", 1))
    pack_rows = 3 * depth + (width // inner + 1) * TABLE
    pack = pl.pallas_call(
        load_kernel,
        out_shape=jax.ShapeDtypeStruct((pack_rows, inner), bf16),
        in_specs=[anywhere] * 2,
        out_specs=vmem,
        scratch_shapes=[
            pltpu.VMEM(stem_table.shape, bf16),
            pltpu.VMEM((TABLE, width), bf16),
            pltpu.SemaphoreType.DMA,
            pltpu.SemaphoreType.DMA((len(weight_parts(conv_weight, EARLY_TAPS)),)),
        ],
        compiler_params=params,
        cost_estimate=cost("load"),
        name="load",
    )(in_hbm(stem_table), in_hbm(conv_weight))
    crossed = [lax.ppermute(piece, "dp", ring_pairs("dp", -step)) for step in range(1, count)]

    received = [[] for _ in CHUNKS]
    for step in range(1, count):
        for index, (low, size) in enumerate(CHUNKS):
            rows = row_count // DILATION * size
            loading, passing = step == 1 and index == 0, index == 1
            operands = [even, joined, odd, gain_in, pack]
            shapes = [jax.ShapeDtypeStruct((rows, inner), bf16)]
            scratch = [pltpu.VMEM((rows + 2 * size, depth), bf16)]
            aliases = {}
            if loading:
                operands.append(in_hbm(conv_weight))
                shapes.append(jax.ShapeDtypeStruct(pack.shape, bf16))
                late = len(weight_parts(conv_weight, LATE_TAPS))
                scratch.append(pltpu.SemaphoreType.DMA((late,)))
                aliases = {4: 1}
            if passing:
                operands.append(crossed[step - 1])
                shapes.append(jax.ShapeDtypeStruct(crossed[step - 1].shape, bf16))
                aliases = {5: 1}
            if index:
                operands.append(part)
            part, *passed = pl.pallas_call(
                functools.partial(
                    chunk_kernel, step, low, size, row_count, len(operands), loading
                ),
                out_shape=shapes,
                in_specs=[vmem] * 5 + [anywhere] * (len(operands) - 5),
                out_specs=[vmem, vmem if loading else anywhere][: len(shapes)],
                scratch_shapes=scratch,
                input_output_aliases=aliases,
                compiler_params=params,
                cost_estimate=cost(f"sent{index}"),
                name="conv_sent",
            )(*operands)
            if loading:
                pack = passed.pop()
            if passed:
                crossed[step - 1] = passed[0]
            received[index].append(lax.ppermute(part, "dp", ring_pairs("dp", step)))

    places, pieces = [(0, 0)], [in_hbm(point_weight)]
    for step in range(1, count):
        for turn in range(groups):
            piece = crossed[step - 1]
            if turn:
                piece = lax.ppermute(piece, "groups", ring_pairs("groups", -turn))
            places.append((step, turn))
            pieces.append(piece)

    own, res, point = pl.pallas_call(
        functools.partial(own_kernel, places, piece_rows),
        out_shape=[
            jax.ShapeDtypeStruct((row_count, inner), f32),
            jax.ShapeDtypeStruct((row_count, half), f32),
            jax.ShapeDtypeStruct((inner, half), bf16),
        ],
        in_specs=[vmem] * 5 + [anywhere] * (1 + len(pieces)),
        out_specs=[vmem] * 3,
        scratch_shapes=[
            pltpu.VMEM((row_count + 2 * DILATION, depth), bf16),
            pltpu.SemaphoreType.DMA((len(pieces),)),
        ],
        compiler_params=params,
        cost_estimate=cost("own"),
        name="conv_own",
    )(even, joined, odd, gain_in, pack, part, *pieces)

    out = None
    blocks = row_count // DILATION
    for index, tail in enumerate(TAILS):
        chunks = [CHUNKS[chunk] for chunk in tail]
        low, size = chunks[0][0], sum(size for _, size in chunks)
        parts = [part for chunk in tail for part in received[chunk]]
        middle = pl.pallas_call(
            functools.partial(middle_kernel, chunks, count - 1),
            out_shape=jax.ShapeDtypeStruct((blocks * size, inner), bf16),
            in_specs=[vmem] * (2 + len(parts)),
            out_specs=vmem,
            compiler_params=params,
            cost_estimate=cost(f"middle{index}"),
            name="middle",
        )(own, gain_mid, *parts)
        other = lax.ppermute(middle, "strand", ring_pairs("strand", 1))
        operands = [middle, other, res, point] + ([] if out is None else [out])
        out = pl.pallas_call(
            functools.partial(final_kernel, low, size),
            grid=(1,),
            out_shape=jax.ShapeDtypeStruct((blocks, DILATION, half), bf16),
            in_specs=[vmem] * 4 + [anywhere] * (len(operands) - 4),
            out_specs=pl.BlockSpec((blocks, size, half), lambda i, at=low // size: (0, at, 0)),
            input_output_aliases={} if out is None else {4: 0},
            compiler_params=params,
            cost_estimate=cost(f"final{index}"),
            name="final",
        )(*operands)
    return out.reshape(1, row_count, half)


def solution(mesh):
    return jax.shard_map(
        per_device,
        mesh=mesh,
        in_specs=(P(("groups", "dp"), "seq"), P(), P(None, "dp", None), P(), P(), P("dp", None)),
        out_specs=P(("groups", "dp"), "seq", "strand"),
        check_vma=False,
    )
```

```python
import functools

import jax
import jax.numpy as jnp
from jax import lax
from jax.experimental import pallas as pl
from jax.experimental.pallas import tpu as pltpu
from jax.sharding import PartitionSpec as P

DILATION = 256
EPS = 1e-06
ROW_STEPS = (256, 192, 64)
CHUNKS = ((0, 96), (96, 96), (192, 64))
TAILS = ((0, 1), (2,))
EARLY_TAPS, LATE_TAPS = (0, 1), (2,)
KINDS = 4
TABLE = 16 * KINDS
FLOPS = {
    "early": 0.1,
    "load": 0.1,
    "sent0": 15.0,
    "sent1": 0.5,
    "sent2": 15.0,
    "own": 15.0,
    "middle0": 0.05,
    "middle1": 5.0,
    "final0": 0.5,
    "final1": 15.0,
}
MIB = 2**20


def pair_pairs(axis, first):
    count = lax.axis_size(axis)
    pairs = [(i, i + 1) for i in range(first, count - 1, 2)]
    return pairs + [(target, source) for source, target in pairs]


def ring_pairs(axis, distance):
    count = lax.axis_size(axis)
    return [(i, (i + distance) % count) for i in range(count)]


def base_taps(sides, step, row_count):
    blocks, here = lax.axis_size("seq"), lax.axis_index("seq")
    low = step * row_count
    even, middle, odd = [ref[:, low : low + row_count] for ref in sides]
    second = lax.rem(here, 2) == 1
    below, above = jnp.where(second, even, odd), jnp.where(second, odd, even)
    bases = jnp.concatenate([below, middle, above], axis=1)
    width, span = 3 * row_count, row_count + 2 * DILATION
    spread = jnp.broadcast_to(bases, (16, width))
    start = width - (row_count - DILATION + 8)
    taps = pltpu.roll(spread, start, 1, stride=1, stride_axis=0)[:, :span]
    place = lax.broadcasted_iota(jnp.int32, (16, span), 1) + (here * row_count - DILATION)
    source = place + 8 - lax.broadcasted_iota(jnp.int32, (16, span), 0)
    length = blocks * row_count
    inside = (place >= 0) & (place < length) & (source >= 0) & (source < length)
    return jnp.where(inside, taps, -1).astype(jnp.float32).astype(jnp.bfloat16)


def one_hot(taps, second):
    row = lax.broadcasted_iota(jnp.int32, (TABLE, 16), 0) // KINDS
    column = lax.broadcasted_iota(jnp.int32, (TABLE, 16), 1)
    chosen = (column == 15 - row + second * (2 * row - 14)).astype(jnp.float32)
    values = jnp.dot(chosen.astype(jnp.bfloat16), taps, preferred_element_type=jnp.float32)
    base = lax.broadcasted_iota(jnp.int32, values.shape, 0) % KINDS
    base = base + second * (KINDS - 1 - 2 * base)
    return (values == base.astype(jnp.float32)).astype(jnp.float32).T


def gelu(x):
    inner = x * (0.7978845608028654 + 0.035677408136300125 * (x * x))
    half = 0.5 * x
    return half + half * jnp.tanh(inner)


def activate(hot, gain_ref, pack_ref, act_ref):
    depth, width = act_ref.shape[1], gain_ref.shape[0]
    turn = lax.rem(width - lax.axis_index("dp") * depth, width)
    gain = jnp.broadcast_to(gain_ref[...].reshape(1, width), (8, width))
    gain = pltpu.roll(gain, turn, 1)[:1, :depth]
    tables = [pack_ref[rows] for rows in table_rows(depth, width, pack_ref.shape[1])]
    step = next(step for step in ROW_STEPS if hot.shape[0] % step == 0)
    for start in range(0, hot.shape[0], step):
        rows = hot[start : start + step]
        parts = [jnp.dot(rows, table, preferred_element_type=jnp.float32) for table in tables]
        square = sum(part * part for part in parts)
        mean = jnp.sum(square, axis=-1, keepdims=True) * (1.0 / width)
        scaled = parts[0][:, :depth] * lax.rsqrt(mean + EPS) * gain
        act_ref[start : start + step] = gelu(scaled).astype(jnp.bfloat16)


def convolve(act_ref, size, rows, pack_ref, copies=()):
    second = lax.axis_index("strand")
    depth = act_ref.shape[1]
    total = None
    for tap in EARLY_TAPS + LATE_TAPS:
        if tap in LATE_TAPS:
            for copy in copies:
                copy.wait()
        start = pl.multiple_of((tap + second * (2 - 2 * tap)) * size, 16)
        block = act_ref[pl.ds(start, rows), :]
        weight = pack_ref[tap * depth : (tap + 1) * depth]
        part = jnp.dot(block, weight, preferred_element_type=jnp.float32)
        total = part if total is None else total + part
    return total


def table_rows(depth, width, columns):
    first = 3 * depth
    count = width // columns
    return [slice(first + i * TABLE, first + (i + 1) * TABLE) for i in range(count)]


def plain_rows(depth, width, columns):
    first = 3 * depth + width // columns * TABLE
    return slice(first, first + TABLE)


def slice_kernel(point_any, tok_any, piece_ref, tok_ref, sems):
    rows, columns = piece_ref.shape
    low = pl.multiple_of(lax.axis_index("groups") * rows, 16)
    left = pl.multiple_of(lax.axis_index("strand") * columns, 128)
    part = point_any.at[pl.ds(low, rows), pl.ds(left, columns)]
    copies = [
        pltpu.make_async_copy(part, piece_ref, sems.at[0]),
        pltpu.make_async_copy(tok_any, tok_ref, sems.at[1]),
    ]
    for copy in copies:
        copy.start()
    for copy in copies:
        copy.wait()


def join_kernel(*refs):
    refs[-1][...] = jnp.concatenate([ref[...] for ref in refs[:-1]], axis=1)


def load_kernel(stem_any, w_any, pack_ref, stem_ref, flat_ref, sem, sems):
    depth, columns = w_any.shape[1:]
    copies = [pltpu.make_async_copy(stem_any, stem_ref, sem)]
    copies += weight_copies(w_any, pack_ref, EARLY_TAPS, sems)
    for copy in copies:
        copy.start()
    copies[0].wait()
    taps, kinds, width = stem_ref.shape
    slabs = [stem_ref[tap].astype(jnp.float32) for tap in range(taps)]
    slabs += [jnp.zeros((kinds, width), jnp.float32)] * (16 - taps)
    flat = jnp.concatenate(slabs)
    flat_ref[...] = flat.astype(jnp.bfloat16)
    me = lax.axis_index("dp")
    if depth == columns:
        parts = [lax.rem(me + index, width // columns) for index in range(width // columns)]
        starts = [pl.multiple_of(part * columns, 128) for part in parts]
        turned = [flat_ref[:, pl.ds(start, columns)] for start in starts]
    else:
        whole = pltpu.roll(flat, lax.rem(width - me * depth, width), 1).astype(jnp.bfloat16)
        turned = jnp.split(whole, width // columns, axis=1)
    for rows, part in zip(table_rows(depth, width, columns), turned):
        pack_ref[rows] = part
    column = pl.multiple_of(lax.axis_index("strand") * columns, 128)
    pack_ref[plain_rows(depth, width, columns)] = flat_ref[:, pl.ds(column, columns)]
    for copy in copies[1:]:
        copy.wait()


def weight_parts(weight, taps):
    rows = weight.shape[1] // 2
    return [(tap, low, rows) for tap in taps for low in (0, rows)]


def weight_copies(w_any, pack_ref, taps, sems):
    depth = w_any.shape[1]
    return [
        pltpu.make_async_copy(
            w_any.at[tap, pl.ds(low, rows)],
            pack_ref.at[pl.ds(tap * depth + low, rows)],
            sems.at[index],
        )
        for index, (tap, low, rows) in enumerate(weight_parts(w_any, taps))
    ]


def chunk_kernel(step, low, size, row_count, out_index, loading, *refs):
    gain_ref, pack_ref = refs[3:5]
    out_ref, act_ref = refs[out_index], refs[out_index + 2 if loading else -1]
    copies = []
    if loading:
        pack_ref = refs[out_index + 1]
        copies = weight_copies(refs[5], pack_ref, LATE_TAPS, refs[-1])
    for copy in copies:
        copy.start()
    taps = base_taps(refs[:3], step, row_count)
    hot = one_hot(taps, lax.axis_index("strand"))
    blocks = row_count // DILATION
    pieces = [hot[b * DILATION + low :][:size] for b in range(blocks + 2)]
    activate(jnp.concatenate(pieces).astype(jnp.bfloat16), gain_ref, pack_ref, act_ref)
    total = convolve(act_ref, size, blocks * size, pack_ref, copies)
    out_ref[...] = total.astype(jnp.bfloat16)


def rows_of(ref, low, size):
    starts = range(low, ref.shape[0], DILATION)
    return jnp.concatenate([ref[start : start + size] for start in starts])


def middle_of(own_ref, gain_ref, parts, low, size):
    total = rows_of(own_ref, low, size)
    for ref in parts:
        total = total + ref[...].astype(jnp.float32)
    mean = jnp.mean(total * total, axis=-1, keepdims=True)
    return gelu(total * lax.rsqrt(mean + EPS) * gain_ref[...].reshape(1, -1)).astype(
        jnp.bfloat16
    )


def own_kernel(places, piece_rows, *refs):
    gain_ref, pack_ref = refs[3:5]
    pieces = refs[6 : 6 + len(places)]
    out_ref, res_ref, point_ref, act_ref, sems = refs[6 + len(places) :]
    ranks, groups = lax.axis_size("dp"), lax.axis_size("groups")
    me, group = lax.axis_index("dp"), lax.axis_index("groups")
    copies = []
    for index, (step, turn) in enumerate(places):
        place = lax.rem(me + step, ranks) * (piece_rows * groups)
        if step:
            place = place + lax.rem(group + turn, groups) * piece_rows
        source = pieces[index]
        if not step:
            columns = point_ref.shape[1]
            left = pl.multiple_of(lax.axis_index("strand") * columns, 128)
            source = source.at[:, pl.ds(left, columns)]
        target = pl.ds(pl.multiple_of(place, 16), source.shape[0])
        copies.append(pltpu.make_async_copy(source, point_ref.at[target], sems.at[index]))
        copies[-1].start()
    row_count = out_ref.shape[0]
    second = lax.axis_index("strand")
    taps = base_taps(refs[:3], 0, row_count)
    hot = one_hot(taps, second)
    here = slice(DILATION, DILATION + row_count)
    both = (hot[here] + one_hot(taps[:, here], 1 - second)).astype(jnp.bfloat16)
    plain = pack_ref[plain_rows(act_ref.shape[1], gain_ref.shape[0], pack_ref.shape[1])]
    res_ref[...] = jnp.dot(both, plain, preferred_element_type=jnp.float32)
    activate(hot.astype(jnp.bfloat16), gain_ref, pack_ref, act_ref)
    out_ref[...] = convolve(act_ref, DILATION, row_count, pack_ref)
    for copy in copies:
        copy.wait()


def middle_kernel(chunks, count, own_ref, gain_ref, *refs):
    out_ref = refs[-1]
    first, total_size = chunks[0][0], sum(size for _, size in chunks)
    for index, (low, size) in enumerate(chunks):
        parts = refs[index * count : (index + 1) * count]
        value = middle_of(own_ref, gain_ref, parts, low, size)
        for block in range(own_ref.shape[0] // DILATION):
            start = block * total_size + low - first
            out_ref[start : start + size] = value[block * size : (block + 1) * size]


def final_kernel(low, size, mine_ref, other_ref, res_ref, point_ref, *refs):
    out_ref = refs[-1]
    total = mine_ref[...].astype(jnp.float32) + other_ref[...].astype(jnp.float32)
    branch = jnp.dot(
        total.astype(jnp.bfloat16), point_ref[...], preferred_element_type=jnp.float32
    )
    value = (0.5 * (branch + rows_of(res_ref, low, size))).astype(jnp.bfloat16)
    out_ref[...] = value.reshape(out_ref.shape)


def in_hbm(x):
    return pltpu.with_memory_space_constraint(x, pltpu.HBM)


def cost(kind):
    return pl.CostEstimate(
        flops=int(1e9 * FLOPS[kind]), bytes_accessed=2**20, transcendentals=0
    )


def per_device(tokens, stem_table, conv_weight, gain_in, gain_mid, point_weight):
    row_count = tokens.shape[1]
    width = stem_table.shape[2]
    depth, inner = conv_weight.shape[1:]
    count, groups = lax.axis_size("dp"), lax.axis_size("groups")
    half = width // 2
    vmem = pl.BlockSpec(memory_space=pltpu.VMEM)
    anywhere = pl.BlockSpec(memory_space=pl.ANY)
    bf16, f32 = jnp.bfloat16, jnp.float32
    params = pltpu.CompilerParams(vmem_limit_bytes=24 * MIB)

    others = [lax.ppermute(tokens, "dp", ring_pairs("dp", -step)) for step in range(1, count)]
    piece_rows = point_weight.shape[0] // groups
    piece, here = pl.pallas_call(
        slice_kernel,
        out_shape=[
            jax.ShapeDtypeStruct((piece_rows, half), bf16),
            jax.ShapeDtypeStruct(tokens.shape, tokens.dtype),
        ],
        in_specs=[anywhere] * 2,
        out_specs=[vmem] * 2,
        scratch_shapes=[pltpu.SemaphoreType.DMA((2,))],
        compiler_params=params,
        cost_estimate=cost("early"),
        name="point_slice",
    )(in_hbm(point_weight), in_hbm(tokens))
    joined = pl.pallas_call(
        join_kernel,
        out_shape=jax.ShapeDtypeStruct((1, count * row_count), tokens.dtype),
        in_specs=[vmem] * count,
        out_specs=vmem,
        compiler_params=params,
        cost_estimate=cost("early"),
        name="join",
    )(here, *others)
    even = lax.ppermute(joined, "seq", pair_pairs("seq", 0))
    odd = lax.ppermute(joined, "seq", pair_pairs("seq", 1))
    pack_rows = 3 * depth + (width // inner + 1) * TABLE
    pack = pl.pallas_call(
        load_kernel,
        out_shape=jax.ShapeDtypeStruct((pack_rows, inner), bf16),
        in_specs=[anywhere] * 2,
        out_specs=vmem,
        scratch_shapes=[
            pltpu.VMEM(stem_table.shape, bf16),
            pltpu.VMEM((TABLE, width), bf16),
            pltpu.SemaphoreType.DMA,
            pltpu.SemaphoreType.DMA((len(weight_parts(conv_weight, EARLY_TAPS)),)),
        ],
        compiler_params=params,
        cost_estimate=cost("load"),
        name="load",
    )(in_hbm(stem_table), in_hbm(conv_weight))
    crossed = [lax.ppermute(piece, "dp", ring_pairs("dp", -step)) for step in range(1, count)]

    received = [[] for _ in CHUNKS]
    for step in range(1, count):
        for index, (low, size) in enumerate(CHUNKS):
            rows = row_count // DILATION * size
            loading, passing = step == 1 and index == 0, index == 1
            operands = [even, joined, odd, gain_in, pack]
            shapes = [jax.ShapeDtypeStruct((rows, inner), bf16)]
            scratch = [pltpu.VMEM((rows + 2 * size, depth), bf16)]
            aliases = {}
            if loading:
                operands.append(in_hbm(conv_weight))
                shapes.append(jax.ShapeDtypeStruct(pack.shape, bf16))
                late = len(weight_parts(conv_weight, LATE_TAPS))
                scratch.append(pltpu.SemaphoreType.DMA((late,)))
                aliases = {4: 1}
            if passing:
                operands.append(crossed[step - 1])
                shapes.append(jax.ShapeDtypeStruct(crossed[step - 1].shape, bf16))
                aliases = {5: 1}
            if index:
                operands.append(part)
            part, *passed = pl.pallas_call(
                functools.partial(
                    chunk_kernel, step, low, size, row_count, len(operands), loading
                ),
                out_shape=shapes,
                in_specs=[vmem] * 5 + [anywhere] * (len(operands) - 5),
                out_specs=[vmem, vmem if loading else anywhere][: len(shapes)],
                scratch_shapes=scratch,
                input_output_aliases=aliases,
                compiler_params=params,
                cost_estimate=cost(f"sent{index}"),
                name="conv_sent",
            )(*operands)
            if loading:
                pack = passed.pop()
            if passed:
                crossed[step - 1] = passed[0]
            received[index].append(lax.ppermute(part, "dp", ring_pairs("dp", step)))

    places, pieces = [(0, 0)], [in_hbm(point_weight)]
    for step in range(1, count):
        for turn in range(groups):
            piece = crossed[step - 1]
            if turn:
                piece = lax.ppermute(piece, "groups", ring_pairs("groups", -turn))
            places.append((step, turn))
            pieces.append(piece)

    own, res, point = pl.pallas_call(
        functools.partial(own_kernel, places, piece_rows),
        out_shape=[
            jax.ShapeDtypeStruct((row_count, inner), f32),
            jax.ShapeDtypeStruct((row_count, half), f32),
            jax.ShapeDtypeStruct((inner, half), bf16),
        ],
        in_specs=[vmem] * 5 + [anywhere] * (1 + len(pieces)),
        out_specs=[vmem] * 3,
        scratch_shapes=[
            pltpu.VMEM((row_count + 2 * DILATION, depth), bf16),
            pltpu.SemaphoreType.DMA((len(pieces),)),
        ],
        compiler_params=params,
        cost_estimate=cost("own"),
        name="conv_own",
    )(even, joined, odd, gain_in, pack, part, *pieces)

    out = None
    blocks = row_count // DILATION
    for index, tail in enumerate(TAILS):
        chunks = [CHUNKS[chunk] for chunk in tail]
        low, size = chunks[0][0], sum(size for _, size in chunks)
        parts = [part for chunk in tail for part in received[chunk]]
        middle = pl.pallas_call(
            functools.partial(middle_kernel, chunks, count - 1),
            out_shape=jax.ShapeDtypeStruct((blocks * size, inner), bf16),
            in_specs=[vmem] * (2 + len(parts)),
            out_specs=vmem,
            compiler_params=params,
            cost_estimate=cost(f"middle{index}"),
            name="middle",
        )(own, gain_mid, *parts)
        other = lax.ppermute(middle, "strand", ring_pairs("strand", 1))
        operands = [middle, other, res, point] + ([] if out is None else [out])
        out = pl.pallas_call(
            functools.partial(final_kernel, low, size),
            grid=(1,),
            out_shape=jax.ShapeDtypeStruct((blocks, DILATION, half), bf16),
            in_specs=[vmem] * 4 + [anywhere] * (len(operands) - 4),
            out_specs=pl.BlockSpec((blocks, size, half), lambda i, at=low // size: (0, at, 0)),
            input_output_aliases={} if out is None else {4: 0},
            compiler_params=params,
            cost_estimate=cost(f"final{index}"),
            name="final",
        )(*operands)
    return out.reshape(1, row_count, half)


def solution(mesh):
    return jax.shard_map(
        per_device,
        mesh=mesh,
        in_specs=(P(("groups", "dp"), "seq"), P(), P(None, "dp", None), P(), P(), P("dp", None)),
        out_specs=P(("groups", "dp"), "seq", "strand"),
        check_vma=False,
    )
```

```python
import functools

import jax
import jax.numpy as jnp
from jax import lax
from jax.experimental import pallas as pl
from jax.experimental.pallas import tpu as pltpu
from jax.sharding import PartitionSpec as P

DILATION = 256
EPS = 1e-06
ROW_STEP = 32
CHUNKS = ((0, 96), (96, 96), (192, 64))
TAILS = ((0, 1), (2,))
EARLY_TAPS, LATE_TAPS = (0, 1), (2,)
KINDS = 4
TABLE = 16 * KINDS
FLOPS = {
    "early": 0.1,
    "load": 0.1,
    "sent0": 15.0,
    "sent1": 0.5,
    "sent2": 15.0,
    "own": 15.0,
    "middle0": 0.05,
    "middle1": 5.0,
    "final0": 0.5,
    "final1": 15.0,
}
MIB = 2**20


def pair_pairs(axis, first):
    count = lax.axis_size(axis)
    pairs = [(i, i + 1) for i in range(first, count - 1, 2)]
    return pairs + [(target, source) for source, target in pairs]


def ring_pairs(axis, distance):
    count = lax.axis_size(axis)
    return [(i, (i + distance) % count) for i in range(count)]


def base_taps(sides, step, row_count):
    blocks, here = lax.axis_size("seq"), lax.axis_index("seq")
    low = step * row_count
    even, middle, odd = [ref[:, low : low + row_count] for ref in sides]
    second = lax.rem(here, 2) == 1
    below, above = jnp.where(second, even, odd), jnp.where(second, odd, even)
    bases = jnp.concatenate([below, middle, above], axis=1)
    width, span = 3 * row_count, row_count + 2 * DILATION
    spread = jnp.broadcast_to(bases, (16, width))
    start = width - (row_count - DILATION + 8)
    taps = pltpu.roll(spread, start, 1, stride=1, stride_axis=0)[:, :span]
    place = lax.broadcasted_iota(jnp.int32, (16, span), 1) + (here * row_count - DILATION)
    source = place + 8 - lax.broadcasted_iota(jnp.int32, (16, span), 0)
    length = blocks * row_count
    inside = (place >= 0) & (place < length) & (source >= 0) & (source < length)
    return jnp.where(inside, taps, -1).astype(jnp.float32).astype(jnp.bfloat16)


def one_hot(taps, second):
    row = lax.broadcasted_iota(jnp.int32, (TABLE, 16), 0) // KINDS
    column = lax.broadcasted_iota(jnp.int32, (TABLE, 16), 1)
    chosen = (column == 15 - row + second * (2 * row - 14)).astype(jnp.float32)
    values = jnp.dot(chosen.astype(jnp.bfloat16), taps, preferred_element_type=jnp.float32)
    base = lax.broadcasted_iota(jnp.int32, values.shape, 0) % KINDS
    base = base + second * (KINDS - 1 - 2 * base)
    return (values == base.astype(jnp.float32)).astype(jnp.float32).T


def gelu(x):
    inner = x * (0.7978845608028654 + 0.035677408136300125 * (x * x))
    half = 0.5 * x
    return half + half * jnp.tanh(inner)


def activate(hot, gain_ref, pack_ref, act_ref):
    depth, width = act_ref.shape[1], gain_ref.shape[0]
    turn = lax.rem(width - lax.axis_index("dp") * depth, width)
    gain = jnp.broadcast_to(gain_ref[...].reshape(1, width), (8, width))
    gain = pltpu.roll(gain, turn, 1)[:1, :depth]
    tables = [pack_ref[rows] for rows in table_rows(depth, width, pack_ref.shape[1])]
    for start in range(0, hot.shape[0], ROW_STEP):
        rows = hot[start : start + ROW_STEP]
        parts = [jnp.dot(rows, table, preferred_element_type=jnp.float32) for table in tables]
        square = sum(part * part for part in parts)
        mean = jnp.sum(square, axis=-1, keepdims=True) * (1.0 / width)
        scaled = parts[0][:, :depth] * lax.rsqrt(mean + EPS) * gain
        act_ref[start : start + ROW_STEP] = gelu(scaled).astype(jnp.bfloat16)


def convolve(act_ref, size, rows, pack_ref, copies=()):
    second = lax.axis_index("strand")
    depth = act_ref.shape[1]
    total = None
    for tap in EARLY_TAPS + LATE_TAPS:
        if tap in LATE_TAPS:
            for copy in copies:
                copy.wait()
        start = pl.multiple_of((tap + second * (2 - 2 * tap)) * size, 16)
        block = act_ref[pl.ds(start, rows), :]
        weight = pack_ref[tap * depth : (tap + 1) * depth]
        part = jnp.dot(block, weight, preferred_element_type=jnp.float32)
        total = part if total is None else total + part
    return total


def table_rows(depth, width, columns):
    first = 3 * depth
    count = width // columns
    return [slice(first + i * TABLE, first + (i + 1) * TABLE) for i in range(count)]


def plain_rows(depth, width, columns):
    first = 3 * depth + width // columns * TABLE
    return slice(first, first + TABLE)


def slice_kernel(point_any, tok_any, piece_ref, tok_ref, sems):
    rows, columns = piece_ref.shape
    low = pl.multiple_of(lax.axis_index("groups") * rows, 16)
    left = pl.multiple_of(lax.axis_index("strand") * columns, 128)
    part = point_any.at[pl.ds(low, rows), pl.ds(left, columns)]
    copies = [
        pltpu.make_async_copy(part, piece_ref, sems.at[0]),
        pltpu.make_async_copy(tok_any, tok_ref, sems.at[1]),
    ]
    for copy in copies:
        copy.start()
    for copy in copies:
        copy.wait()


def join_kernel(*refs):
    refs[-1][...] = jnp.concatenate([ref[...] for ref in refs[:-1]], axis=1)


def load_kernel(stem_any, w_any, pack_ref, stem_ref, flat_ref, sem, sems):
    depth, columns = w_any.shape[1:]
    copies = [pltpu.make_async_copy(stem_any, stem_ref, sem)]
    copies += weight_copies(w_any, pack_ref, EARLY_TAPS, sems)
    for copy in copies:
        copy.start()
    copies[0].wait()
    taps, kinds, width = stem_ref.shape
    slabs = [stem_ref[tap].astype(jnp.float32) for tap in range(taps)]
    slabs += [jnp.zeros((kinds, width), jnp.float32)] * (16 - taps)
    flat = jnp.concatenate(slabs)
    flat_ref[...] = flat.astype(jnp.bfloat16)
    me = lax.axis_index("dp")
    if depth == columns:
        parts = [lax.rem(me + index, width // columns) for index in range(width // columns)]
        starts = [pl.multiple_of(part * columns, 128) for part in parts]
        turned = [flat_ref[:, pl.ds(start, columns)] for start in starts]
    else:
        whole = pltpu.roll(flat, lax.rem(width - me * depth, width), 1).astype(jnp.bfloat16)
        turned = jnp.split(whole, width // columns, axis=1)
    for rows, part in zip(table_rows(depth, width, columns), turned):
        pack_ref[rows] = part
    column = pl.multiple_of(lax.axis_index("strand") * columns, 128)
    pack_ref[plain_rows(depth, width, columns)] = flat_ref[:, pl.ds(column, columns)]
    for copy in copies[1:]:
        copy.wait()


def weight_parts(weight, taps):
    rows = weight.shape[1] // 2
    return [(tap, low, rows) for tap in taps for low in (0, rows)]


def weight_copies(w_any, pack_ref, taps, sems):
    depth = w_any.shape[1]
    return [
        pltpu.make_async_copy(
            w_any.at[tap, pl.ds(low, rows)],
            pack_ref.at[pl.ds(tap * depth + low, rows)],
            sems.at[index],
        )
        for index, (tap, low, rows) in enumerate(weight_parts(w_any, taps))
    ]


def chunk_kernel(step, low, size, row_count, out_index, loading, *refs):
    gain_ref, pack_ref = refs[3:5]
    out_ref, act_ref = refs[out_index], refs[out_index + 2 if loading else -1]
    copies = []
    if loading:
        pack_ref = refs[out_index + 1]
        copies = weight_copies(refs[5], pack_ref, LATE_TAPS, refs[-1])
    for copy in copies:
        copy.start()
    taps = base_taps(refs[:3], step, row_count)
    hot = one_hot(taps, lax.axis_index("strand"))
    blocks = row_count // DILATION
    pieces = [hot[b * DILATION + low :][:size] for b in range(blocks + 2)]
    activate(jnp.concatenate(pieces).astype(jnp.bfloat16), gain_ref, pack_ref, act_ref)
    total = convolve(act_ref, size, blocks * size, pack_ref, copies)
    out_ref[...] = total.astype(jnp.bfloat16)


def rows_of(ref, low, size):
    starts = range(low, ref.shape[0], DILATION)
    return jnp.concatenate([ref[start : start + size] for start in starts])


def own_kernel(places, piece_rows, *refs):
    gain_ref, pack_ref = refs[3:5]
    pieces = refs[6 : 6 + len(places)]
    out_ref, res_ref, point_ref, act_ref, sems = refs[6 + len(places) :]
    ranks, groups = lax.axis_size("dp"), lax.axis_size("groups")
    me, group = lax.axis_index("dp"), lax.axis_index("groups")
    copies = []
    for index, (step, turn) in enumerate(places):
        place = lax.rem(me + step, ranks) * (piece_rows * groups)
        if step:
            place = place + lax.rem(group + turn, groups) * piece_rows
        source = pieces[index]
        if not step:
            columns = point_ref.shape[1]
            left = pl.multiple_of(lax.axis_index("strand") * columns, 128)
            source = source.at[:, pl.ds(left, columns)]
        target = pl.ds(pl.multiple_of(place, 16), source.shape[0])
        copies.append(pltpu.make_async_copy(source, point_ref.at[target], sems.at[index]))
        copies[-1].start()
    row_count = out_ref.shape[0]
    second = lax.axis_index("strand")
    taps = base_taps(refs[:3], 0, row_count)
    hot = one_hot(taps, second)
    here = slice(DILATION, DILATION + row_count)
    both = (hot[here] + one_hot(taps[:, here], 1 - second)).astype(jnp.bfloat16)
    plain = pack_ref[plain_rows(act_ref.shape[1], gain_ref.shape[0], pack_ref.shape[1])]
    res_ref[...] = jnp.dot(both, plain, preferred_element_type=jnp.float32)
    activate(hot.astype(jnp.bfloat16), gain_ref, pack_ref, act_ref)
    out_ref[...] = convolve(act_ref, DILATION, row_count, pack_ref)
    for copy in copies:
        copy.wait()


def middle_kernel(chunks, count, own_ref, gain_ref, *refs):
    out_ref = refs[-1]
    gain = gain_ref[...].reshape(1, -1)
    first, total_size = chunks[0][0], sum(size for _, size in chunks)
    for index, (low, size) in enumerate(chunks):
        parts = refs[index * count : (index + 1) * count]
        for block in range(own_ref.shape[0] // DILATION):
            for row in range(0, size, ROW_STEP):
                start = block * DILATION + low + row
                total = own_ref[start : start + ROW_STEP]
                start = block * size + row
                for ref in parts:
                    total = total + ref[start : start + ROW_STEP].astype(jnp.float32)
                mean = jnp.mean(total * total, axis=-1, keepdims=True)
                value = gelu(total * lax.rsqrt(mean + EPS) * gain)
                start = block * total_size + low - first + row
                out_ref[start : start + ROW_STEP] = value.astype(jnp.bfloat16)


def final_kernel(low, size, mine_ref, other_ref, res_ref, point_ref, *refs):
    out_ref = refs[-1]
    total = mine_ref[...].astype(jnp.float32) + other_ref[...].astype(jnp.float32)
    branch = jnp.dot(
        total.astype(jnp.bfloat16), point_ref[...], preferred_element_type=jnp.float32
    )
    value = (0.5 * (branch + rows_of(res_ref, low, size))).astype(jnp.bfloat16)
    out_ref[...] = value.reshape(out_ref.shape)


def in_hbm(x):
    return pltpu.with_memory_space_constraint(x, pltpu.HBM)


def cost(kind):
    return pl.CostEstimate(
        flops=int(1e9 * FLOPS[kind]), bytes_accessed=2**20, transcendentals=0
    )


def per_device(tokens, stem_table, conv_weight, gain_in, gain_mid, point_weight):
    row_count = tokens.shape[1]
    width = stem_table.shape[2]
    depth, inner = conv_weight.shape[1:]
    count, groups = lax.axis_size("dp"), lax.axis_size("groups")
    half = width // 2
    vmem = pl.BlockSpec(memory_space=pltpu.VMEM)
    anywhere = pl.BlockSpec(memory_space=pl.ANY)
    bf16, f32 = jnp.bfloat16, jnp.float32
    params = pltpu.CompilerParams(vmem_limit_bytes=24 * MIB)

    others = [lax.ppermute(tokens, "dp", ring_pairs("dp", -step)) for step in range(1, count)]
    piece_rows = point_weight.shape[0] // groups
    piece, here = pl.pallas_call(
        slice_kernel,
        out_shape=[
            jax.ShapeDtypeStruct((piece_rows, half), bf16),
            jax.ShapeDtypeStruct(tokens.shape, tokens.dtype),
        ],
        in_specs=[anywhere] * 2,
        out_specs=[vmem] * 2,
        scratch_shapes=[pltpu.SemaphoreType.DMA((2,))],
        compiler_params=params,
        cost_estimate=cost("early"),
        name="point_slice",
    )(in_hbm(point_weight), in_hbm(tokens))
    joined = pl.pallas_call(
        join_kernel,
        out_shape=jax.ShapeDtypeStruct((1, count * row_count), tokens.dtype),
        in_specs=[vmem] * count,
        out_specs=vmem,
        compiler_params=params,
        cost_estimate=cost("early"),
        name="join",
    )(here, *others)
    even = lax.ppermute(joined, "seq", pair_pairs("seq", 0))
    odd = lax.ppermute(joined, "seq", pair_pairs("seq", 1))
    pack_rows = 3 * depth + (width // inner + 1) * TABLE
    pack = pl.pallas_call(
        load_kernel,
        out_shape=jax.ShapeDtypeStruct((pack_rows, inner), bf16),
        in_specs=[anywhere] * 2,
        out_specs=vmem,
        scratch_shapes=[
            pltpu.VMEM(stem_table.shape, bf16),
            pltpu.VMEM((TABLE, width), bf16),
            pltpu.SemaphoreType.DMA,
            pltpu.SemaphoreType.DMA((len(weight_parts(conv_weight, EARLY_TAPS)),)),
        ],
        compiler_params=params,
        cost_estimate=cost("load"),
        name="load",
    )(in_hbm(stem_table), in_hbm(conv_weight))
    crossed = [lax.ppermute(piece, "dp", ring_pairs("dp", -step)) for step in range(1, count)]

    received = [[] for _ in CHUNKS]
    for step in range(1, count):
        for index, (low, size) in enumerate(CHUNKS):
            rows = row_count // DILATION * size
            loading, passing = step == 1 and index == 0, index == 1
            operands = [even, joined, odd, gain_in, pack]
            shapes = [jax.ShapeDtypeStruct((rows, inner), bf16)]
            scratch = [pltpu.VMEM((rows + 2 * size, depth), bf16)]
            aliases = {}
            if loading:
                operands.append(in_hbm(conv_weight))
                shapes.append(jax.ShapeDtypeStruct(pack.shape, bf16))
                late = len(weight_parts(conv_weight, LATE_TAPS))
                scratch.append(pltpu.SemaphoreType.DMA((late,)))
                aliases = {4: 1}
            if passing:
                operands.append(crossed[step - 1])
                shapes.append(jax.ShapeDtypeStruct(crossed[step - 1].shape, bf16))
                aliases = {5: 1}
            if index:
                operands.append(part)
            part, *passed = pl.pallas_call(
                functools.partial(
                    chunk_kernel, step, low, size, row_count, len(operands), loading
                ),
                out_shape=shapes,
                in_specs=[vmem] * 5 + [anywhere] * (len(operands) - 5),
                out_specs=[vmem, vmem if loading else anywhere][: len(shapes)],
                scratch_shapes=scratch,
                input_output_aliases=aliases,
                compiler_params=params,
                cost_estimate=cost(f"sent{index}"),
                name="conv_sent",
            )(*operands)
            if loading:
                pack = passed.pop()
            if passed:
                crossed[step - 1] = passed[0]
            received[index].append(lax.ppermute(part, "dp", ring_pairs("dp", step)))

    places, pieces = [(0, 0)], [in_hbm(point_weight)]
    for step in range(1, count):
        for turn in range(groups):
            piece = crossed[step - 1]
            if turn:
                piece = lax.ppermute(piece, "groups", ring_pairs("groups", -turn))
            places.append((step, turn))
            pieces.append(piece)

    own, res, point = pl.pallas_call(
        functools.partial(own_kernel, places, piece_rows),
        out_shape=[
            jax.ShapeDtypeStruct((row_count, inner), f32),
            jax.ShapeDtypeStruct((row_count, half), f32),
            jax.ShapeDtypeStruct((inner, half), bf16),
        ],
        in_specs=[vmem] * 5 + [anywhere] * (1 + len(pieces)),
        out_specs=[vmem] * 3,
        scratch_shapes=[
            pltpu.VMEM((row_count + 2 * DILATION, depth), bf16),
            pltpu.SemaphoreType.DMA((len(pieces),)),
        ],
        compiler_params=params,
        cost_estimate=cost("own"),
        name="conv_own",
    )(even, joined, odd, gain_in, pack, part, *pieces)

    out = None
    blocks = row_count // DILATION
    for index, tail in enumerate(TAILS):
        chunks = [CHUNKS[chunk] for chunk in tail]
        low, size = chunks[0][0], sum(size for _, size in chunks)
        parts = [part for chunk in tail for part in received[chunk]]
        middle = pl.pallas_call(
            functools.partial(middle_kernel, chunks, count - 1),
            out_shape=jax.ShapeDtypeStruct((blocks * size, inner), bf16),
            in_specs=[vmem] * (2 + len(parts)),
            out_specs=vmem,
            compiler_params=params,
            cost_estimate=cost(f"middle{index}"),
            name="middle",
        )(own, gain_mid, *parts)
        other = lax.ppermute(middle, "strand", ring_pairs("strand", 1))
        operands = [middle, other, res, point] + ([] if out is None else [out])
        out = pl.pallas_call(
            functools.partial(final_kernel, low, size),
            grid=(1,),
            out_shape=jax.ShapeDtypeStruct((blocks, DILATION, half), bf16),
            in_specs=[vmem] * 4 + [anywhere] * (len(operands) - 4),
            out_specs=pl.BlockSpec((blocks, size, half), lambda i, at=low // size: (0, at, 0)),
            input_output_aliases={} if out is None else {4: 0},
            compiler_params=params,
            cost_estimate=cost(f"final{index}"),
            name="final",
        )(*operands)
    return out.reshape(1, row_count, half)


def solution(mesh):
    return jax.shard_map(
        per_device,
        mesh=mesh,
        in_specs=(P(("groups", "dp"), "seq"), P(), P(None, "dp", None), P(), P(), P("dp", None)),
        out_specs=P(("groups", "dp"), "seq", "strand"),
        check_vma=False,
    )
```

```python
import functools

import jax
import jax.numpy as jnp
from jax import lax
from jax.experimental import pallas as pl
from jax.experimental.pallas import tpu as pltpu
from jax.sharding import PartitionSpec as P

DILATION = 256
EPS = 1e-06
ROW_STEP = 32
CHUNKS = ((0, 64), (64, 128), (192, 64))
TAILS = ((0, 1), (2,))
EARLY_TAPS, LATE_TAPS = (0, 1), (2,)
KINDS = 4
TABLE = 16 * KINDS
FLOPS = {
    "early": 0.1,
    "load": 0.1,
    "sent0": 15.0,
    "sent1": 0.5,
    "sent2": 15.0,
    "own": 15.0,
    "middle0": 0.05,
    "middle1": 5.0,
    "final0": 0.5,
    "final1": 15.0,
}
MIB = 2**20


def pair_pairs(axis, first):
    count = lax.axis_size(axis)
    pairs = [(i, i + 1) for i in range(first, count - 1, 2)]
    return pairs + [(target, source) for source, target in pairs]


def ring_pairs(axis, distance):
    count = lax.axis_size(axis)
    return [(i, (i + distance) % count) for i in range(count)]


def base_taps(sides, step, row_count):
    blocks, here = lax.axis_size("seq"), lax.axis_index("seq")
    low = step * row_count
    odd, middle, even = [ref[:, low : low + row_count] for ref in sides]
    second = lax.rem(here, 2) == 1
    below, above = jnp.where(second, even, odd), jnp.where(second, odd, even)
    bases = jnp.concatenate([below, middle, above], axis=1)
    width, span = 3 * row_count, row_count + 2 * DILATION
    spread = jnp.broadcast_to(bases, (16, width))
    start = width - (row_count - DILATION + 8)
    taps = pltpu.roll(spread, start, 1, stride=1, stride_axis=0)[:, :span]
    place = lax.broadcasted_iota(jnp.int32, (16, span), 1) + (here * row_count - DILATION)
    source = place + 8 - lax.broadcasted_iota(jnp.int32, (16, span), 0)
    length = blocks * row_count
    inside = (place >= 0) & (place < length) & (source >= 0) & (source < length)
    return jnp.where(inside, taps, -1).astype(jnp.float32).astype(jnp.bfloat16)


def one_hot(taps, second):
    row = lax.broadcasted_iota(jnp.int32, (TABLE, 16), 0) // KINDS
    column = lax.broadcasted_iota(jnp.int32, (TABLE, 16), 1)
    chosen = (column == 15 - row + second * (2 * row - 14)).astype(jnp.float32)
    values = jnp.dot(chosen.astype(jnp.bfloat16), taps, preferred_element_type=jnp.float32)
    base = lax.broadcasted_iota(jnp.int32, values.shape, 0) % KINDS
    base = base + second * (KINDS - 1 - 2 * base)
    return (values == base.astype(jnp.float32)).astype(jnp.float32).T


def gelu(x):
    inner = x * (0.7978845608028654 + 0.035677408136300125 * (x * x))
    half = 0.5 * x
    return half + half * jnp.tanh(inner)


def activate(hot, gain_ref, pack_ref, act_ref):
    depth, width = act_ref.shape[1], gain_ref.shape[0]
    turn = lax.rem(width - lax.axis_index("dp") * depth, width)
    gain = jnp.broadcast_to(gain_ref[...].reshape(1, width), (8, width))
    gain = pltpu.roll(gain, turn, 1)[:1, :depth]
    tables = [pack_ref[rows] for rows in table_rows(depth, width, pack_ref.shape[1])]
    for start in range(0, hot.shape[0], ROW_STEP):
        rows = hot[start : start + ROW_STEP]
        parts = [jnp.dot(rows, table, preferred_element_type=jnp.float32) for table in tables]
        square = sum(part * part for part in parts)
        mean = jnp.sum(square, axis=-1, keepdims=True) * (1.0 / width)
        scaled = parts[0][:, :depth] * lax.rsqrt(mean + EPS) * gain
        act_ref[start : start + ROW_STEP] = gelu(scaled).astype(jnp.bfloat16)


def convolve(act_ref, size, rows, pack_ref, copies=()):
    second = lax.axis_index("strand")
    depth = act_ref.shape[1]
    total = None
    for tap in EARLY_TAPS + LATE_TAPS:
        if tap in LATE_TAPS:
            for copy in copies:
                copy.wait()
        start = pl.multiple_of((tap + second * (2 - 2 * tap)) * size, 16)
        block = act_ref[pl.ds(start, rows), :]
        weight = pack_ref[tap * depth : (tap + 1) * depth]
        part = jnp.dot(block, weight, preferred_element_type=jnp.float32)
        total = part if total is None else total + part
    return total


def table_rows(depth, width, columns):
    first = 3 * depth
    count = width // columns
    return [slice(first + i * TABLE, first + (i + 1) * TABLE) for i in range(count)]


def plain_rows(depth, width, columns):
    first = 3 * depth + width // columns * TABLE
    return slice(first, first + TABLE)


def slice_kernel(point_any, tok_any, piece_ref, tok_ref, sems):
    rows, columns = piece_ref.shape
    low = pl.multiple_of(lax.axis_index("groups") * rows, 16)
    left = pl.multiple_of(lax.axis_index("strand") * columns, 128)
    part = point_any.at[pl.ds(low, rows), pl.ds(left, columns)]
    copies = [
        pltpu.make_async_copy(part, piece_ref, sems.at[0]),
        pltpu.make_async_copy(tok_any, tok_ref, sems.at[1]),
    ]
    for copy in copies:
        copy.start()
    for copy in copies:
        copy.wait()


def join_kernel(*refs):
    refs[-1][...] = jnp.concatenate([ref[...] for ref in refs[:-1]], axis=1)


def load_kernel(stem_any, w_any, pack_ref, stem_ref, flat_ref, sem, sems):
    depth, columns = w_any.shape[1:]
    copies = [pltpu.make_async_copy(stem_any, stem_ref, sem)]
    copies += weight_copies(w_any, pack_ref, EARLY_TAPS, sems)
    for copy in copies:
        copy.start()
    copies[0].wait()
    taps, kinds, width = stem_ref.shape
    slabs = [stem_ref[tap].astype(jnp.float32) for tap in range(taps)]
    slabs += [jnp.zeros((kinds, width), jnp.float32)] * (16 - taps)
    flat = jnp.concatenate(slabs)
    flat_ref[...] = flat.astype(jnp.bfloat16)
    me = lax.axis_index("dp")
    if depth == columns:
        parts = [lax.rem(me + index, width // columns) for index in range(width // columns)]
        starts = [pl.multiple_of(part * columns, 128) for part in parts]
        turned = [flat_ref[:, pl.ds(start, columns)] for start in starts]
    else:
        whole = pltpu.roll(flat, lax.rem(width - me * depth, width), 1).astype(jnp.bfloat16)
        turned = jnp.split(whole, width // columns, axis=1)
    for rows, part in zip(table_rows(depth, width, columns), turned):
        pack_ref[rows] = part
    column = pl.multiple_of(lax.axis_index("strand") * columns, 128)
    pack_ref[plain_rows(depth, width, columns)] = flat_ref[:, pl.ds(column, columns)]
    for copy in copies[1:]:
        copy.wait()


def weight_parts(weight, taps):
    rows = weight.shape[1] // 2
    return [(tap, low, rows) for tap in taps for low in (0, rows)]


def weight_copies(w_any, pack_ref, taps, sems):
    depth = w_any.shape[1]
    return [
        pltpu.make_async_copy(
            w_any.at[tap, pl.ds(low, rows)],
            pack_ref.at[pl.ds(tap * depth + low, rows)],
            sems.at[index],
        )
        for index, (tap, low, rows) in enumerate(weight_parts(w_any, taps))
    ]


def chunk_kernel(step, low, size, row_count, out_index, loading, *refs):
    gain_ref, pack_ref = refs[3:5]
    out_ref, act_ref = refs[out_index], refs[out_index + 2 if loading else -1]
    copies = []
    if loading:
        pack_ref = refs[out_index + 1]
        copies = weight_copies(refs[5], pack_ref, LATE_TAPS, refs[-1])
    for copy in copies:
        copy.start()
    taps = base_taps(refs[:3], step, row_count)
    hot = one_hot(taps, lax.axis_index("strand"))
    blocks = row_count // DILATION
    pieces = [hot[b * DILATION + low :][:size] for b in range(blocks + 2)]
    activate(jnp.concatenate(pieces).astype(jnp.bfloat16), gain_ref, pack_ref, act_ref)
    total = convolve(act_ref, size, blocks * size, pack_ref, copies)
    out_ref[...] = total.astype(jnp.bfloat16)


def rows_of(ref, low, size):
    starts = range(low, ref.shape[0], DILATION)
    return jnp.concatenate([ref[start : start + size] for start in starts])


def own_kernel(places, piece_rows, *refs):
    gain_ref, pack_ref = refs[3:5]
    pieces = refs[6 : 6 + len(places)]
    out_ref, res_ref, point_ref, act_ref, sems = refs[6 + len(places) :]
    ranks, groups = lax.axis_size("dp"), lax.axis_size("groups")
    me, group = lax.axis_index("dp"), lax.axis_index("groups")
    copies = []
    for index, (step, turn) in enumerate(places):
        place = lax.rem(me + step, ranks) * (piece_rows * groups)
        if step:
            place = place + lax.rem(group + turn, groups) * piece_rows
        source = pieces[index]
        if not step:
            columns = point_ref.shape[1]
            left = pl.multiple_of(lax.axis_index("strand") * columns, 128)
            source = source.at[:, pl.ds(left, columns)]
        target = pl.ds(pl.multiple_of(place, 16), source.shape[0])
        copies.append(pltpu.make_async_copy(source, point_ref.at[target], sems.at[index]))
        copies[-1].start()
    row_count = out_ref.shape[0]
    second = lax.axis_index("strand")
    taps = base_taps(refs[:3], 0, row_count)
    hot = one_hot(taps, second)
    here = slice(DILATION, DILATION + row_count)
    both = (hot[here] + one_hot(taps[:, here], 1 - second)).astype(jnp.bfloat16)
    plain = pack_ref[plain_rows(act_ref.shape[1], gain_ref.shape[0], pack_ref.shape[1])]
    res_ref[...] = jnp.dot(both, plain, preferred_element_type=jnp.float32)
    activate(hot.astype(jnp.bfloat16), gain_ref, pack_ref, act_ref)
    out_ref[...] = convolve(act_ref, DILATION, row_count, pack_ref)
    for copy in copies:
        copy.wait()


def middle_kernel(chunks, count, own_ref, gain_ref, *refs):
    out_ref = refs[-1]
    gain = gain_ref[...].reshape(1, -1)
    first, total_size = chunks[0][0], sum(size for _, size in chunks)
    for index, (low, size) in enumerate(chunks):
        parts = refs[index * count : (index + 1) * count]
        for block in range(own_ref.shape[0] // DILATION):
            for row in range(0, size, ROW_STEP):
                start = block * DILATION + low + row
                total = own_ref[start : start + ROW_STEP]
                start = block * size + row
                for ref in parts:
                    total = total + ref[start : start + ROW_STEP].astype(jnp.float32)
                mean = jnp.mean(total * total, axis=-1, keepdims=True)
                value = gelu(total * lax.rsqrt(mean + EPS) * gain)
                start = block * total_size + low - first + row
                out_ref[start : start + ROW_STEP] = value.astype(jnp.bfloat16)


def final_kernel(low, size, mine_ref, other_ref, res_ref, point_ref, *refs):
    out_ref = refs[-1]
    total = mine_ref[...].astype(jnp.float32) + other_ref[...].astype(jnp.float32)
    branch = jnp.dot(
        total.astype(jnp.bfloat16), point_ref[...], preferred_element_type=jnp.float32
    )
    value = (0.5 * (branch + rows_of(res_ref, low, size))).astype(jnp.bfloat16)
    out_ref[...] = value.reshape(out_ref.shape)


def in_hbm(x):
    return pltpu.with_memory_space_constraint(x, pltpu.HBM)


def cost(kind):
    return pl.CostEstimate(
        flops=int(1e9 * FLOPS[kind]), bytes_accessed=2**20, transcendentals=0
    )


def per_device(tokens, stem_table, conv_weight, gain_in, gain_mid, point_weight):
    row_count = tokens.shape[1]
    width = stem_table.shape[2]
    depth, inner = conv_weight.shape[1:]
    count, groups = lax.axis_size("dp"), lax.axis_size("groups")
    half = width // 2
    vmem = pl.BlockSpec(memory_space=pltpu.VMEM)
    anywhere = pl.BlockSpec(memory_space=pl.ANY)
    bf16, f32 = jnp.bfloat16, jnp.float32
    params = pltpu.CompilerParams(vmem_limit_bytes=24 * MIB)

    others = [lax.ppermute(tokens, "dp", ring_pairs("dp", -step)) for step in range(1, count)]
    piece_rows = point_weight.shape[0] // groups
    piece, here = pl.pallas_call(
        slice_kernel,
        out_shape=[
            jax.ShapeDtypeStruct((piece_rows, half), bf16),
            jax.ShapeDtypeStruct(tokens.shape, tokens.dtype),
        ],
        in_specs=[anywhere] * 2,
        out_specs=[vmem] * 2,
        scratch_shapes=[pltpu.SemaphoreType.DMA((2,))],
        compiler_params=params,
        cost_estimate=cost("early"),
        name="point_slice",
    )(in_hbm(point_weight), in_hbm(tokens))
    joined = pl.pallas_call(
        join_kernel,
        out_shape=jax.ShapeDtypeStruct((1, count * row_count), tokens.dtype),
        in_specs=[vmem] * count,
        out_specs=vmem,
        compiler_params=params,
        cost_estimate=cost("early"),
        name="join",
    )(here, *others)
    odd = lax.ppermute(joined, "seq", pair_pairs("seq", 1))
    even = lax.ppermute(joined, "seq", pair_pairs("seq", 0))
    pack_rows = 3 * depth + (width // inner + 1) * TABLE
    pack = pl.pallas_call(
        load_kernel,
        out_shape=jax.ShapeDtypeStruct((pack_rows, inner), bf16),
        in_specs=[anywhere] * 2,
        out_specs=vmem,
        scratch_shapes=[
            pltpu.VMEM(stem_table.shape, bf16),
            pltpu.VMEM((TABLE, width), bf16),
            pltpu.SemaphoreType.DMA,
            pltpu.SemaphoreType.DMA((len(weight_parts(conv_weight, EARLY_TAPS)),)),
        ],
        compiler_params=params,
        cost_estimate=cost("load"),
        name="load",
    )(in_hbm(stem_table), in_hbm(conv_weight))
    crossed = [lax.ppermute(piece, "dp", ring_pairs("dp", -step)) for step in range(1, count)]

    received = [[] for _ in CHUNKS]
    for step in range(1, count):
        for index, (low, size) in enumerate(CHUNKS):
            rows = row_count // DILATION * size
            loading, passing = step == 1 and index == 0, index == 1
            operands = [odd, joined, even, gain_in, pack]
            shapes = [jax.ShapeDtypeStruct((rows, inner), bf16)]
            scratch = [pltpu.VMEM((rows + 2 * size, depth), bf16)]
            aliases = {}
            if loading:
                operands.append(in_hbm(conv_weight))
                shapes.append(jax.ShapeDtypeStruct(pack.shape, bf16))
                late = len(weight_parts(conv_weight, LATE_TAPS))
                scratch.append(pltpu.SemaphoreType.DMA((late,)))
                aliases = {4: 1}
            if passing:
                operands.append(crossed[step - 1])
                shapes.append(jax.ShapeDtypeStruct(crossed[step - 1].shape, bf16))
                aliases = {5: 1}
            if index:
                operands.append(part)
            part, *passed = pl.pallas_call(
                functools.partial(
                    chunk_kernel, step, low, size, row_count, len(operands), loading
                ),
                out_shape=shapes,
                in_specs=[vmem] * 5 + [anywhere] * (len(operands) - 5),
                out_specs=[vmem, vmem if loading else anywhere][: len(shapes)],
                scratch_shapes=scratch,
                input_output_aliases=aliases,
                compiler_params=params,
                cost_estimate=cost(f"sent{index}"),
                name="conv_sent",
            )(*operands)
            if loading:
                pack = passed.pop()
            if passed:
                crossed[step - 1] = passed[0]
            received[index].append(lax.ppermute(part, "dp", ring_pairs("dp", step)))

    places, pieces = [(0, 0)], [in_hbm(point_weight)]
    for step in range(1, count):
        for turn in range(groups):
            piece = crossed[step - 1]
            if turn:
                piece = lax.ppermute(piece, "groups", ring_pairs("groups", -turn))
            places.append((step, turn))
            pieces.append(piece)

    own, res, point = pl.pallas_call(
        functools.partial(own_kernel, places, piece_rows),
        out_shape=[
            jax.ShapeDtypeStruct((row_count, inner), f32),
            jax.ShapeDtypeStruct((row_count, half), f32),
            jax.ShapeDtypeStruct((inner, half), bf16),
        ],
        in_specs=[vmem] * 5 + [anywhere] * (1 + len(pieces)),
        out_specs=[vmem] * 3,
        scratch_shapes=[
            pltpu.VMEM((row_count + 2 * DILATION, depth), bf16),
            pltpu.SemaphoreType.DMA((len(pieces),)),
        ],
        compiler_params=params,
        cost_estimate=cost("own"),
        name="conv_own",
    )(odd, joined, even, gain_in, pack, part, *pieces)

    out = None
    blocks = row_count // DILATION
    for index, tail in enumerate(TAILS):
        chunks = [CHUNKS[chunk] for chunk in tail]
        low, size = chunks[0][0], sum(size for _, size in chunks)
        parts = [part for chunk in tail for part in received[chunk]]
        middle = pl.pallas_call(
            functools.partial(middle_kernel, chunks, count - 1),
            out_shape=jax.ShapeDtypeStruct((blocks * size, inner), bf16),
            in_specs=[vmem] * (2 + len(parts)),
            out_specs=vmem,
            compiler_params=params,
            cost_estimate=cost(f"middle{index}"),
            name="middle",
        )(own, gain_mid, *parts)
        other = lax.ppermute(middle, "strand", ring_pairs("strand", 1))
        operands = [middle, other, res, point] + ([] if out is None else [out])
        out = pl.pallas_call(
            functools.partial(final_kernel, low, size),
            grid=(1,),
            out_shape=jax.ShapeDtypeStruct((blocks, DILATION, half), bf16),
            in_specs=[vmem] * 4 + [anywhere] * (len(operands) - 4),
            out_specs=pl.BlockSpec((blocks, size, half), lambda i, at=low // size: (0, at, 0)),
            input_output_aliases={} if out is None else {4: 0},
            compiler_params=params,
            cost_estimate=cost(f"final{index}"),
            name="final",
        )(*operands)
    return out.reshape(1, row_count, half)


def solution(mesh):
    return jax.shard_map(
        per_device,
        mesh=mesh,
        in_specs=(P(("groups", "dp"), "seq"), P(), P(None, "dp", None), P(), P(), P("dp", None)),
        out_specs=P(("groups", "dp"), "seq", "strand"),
        check_vma=False,
    )
```

```python
import functools

import jax
import jax.numpy as jnp
from jax import lax
from jax.experimental import pallas as pl
from jax.experimental.pallas import tpu as pltpu
from jax.sharding import PartitionSpec as P

DILATION = 256
EPS = 1e-06
ROW_STEP = 32
CHUNKS = ((0, 96), (96, 96), (192, 64))
TAILS = ((0,), (1,), (2,))
EARLY_TAPS, LATE_TAPS = (0, 1), (2,)
KINDS = 4
TABLE = 16 * KINDS
WEIGHTS = {
    "early": 0.1,
    "load": 0.1,
    "sent0": 15.0,
    "sent1": 0.5,
    "sent2": 5.0,
    "own": 15.0,
    "middle0": 0.05,
    "middle1": 5.0,
    "middle2": 5.0,
    "final0": 0.05,
    "final1": 0.5,
    "final2": 15.0,
}
MIB = 2**20


def pair_pairs(axis, first):
    count = lax.axis_size(axis)
    pairs = [(i, i + 1) for i in range(first, count - 1, 2)]
    return pairs + [(target, source) for source, target in pairs]


def ring_pairs(axis, distance):
    count = lax.axis_size(axis)
    return [(i, (i + distance) % count) for i in range(count)]


def base_taps(sides, step, row_count):
    blocks, here = lax.axis_size("seq"), lax.axis_index("seq")
    low = step * row_count
    even, middle, odd = [ref[:, low : low + row_count] for ref in sides]
    second = lax.rem(here, 2) == 1
    below, above = jnp.where(second, even, odd), jnp.where(second, odd, even)
    bases = jnp.concatenate([below, middle, above], axis=1)
    width, span = 3 * row_count, row_count + 2 * DILATION
    spread = jnp.broadcast_to(bases, (16, width))
    start = width - (row_count - DILATION + 8)
    taps = pltpu.roll(spread, start, 1, stride=1, stride_axis=0)[:, :span]
    place = lax.broadcasted_iota(jnp.int32, (16, span), 1) + (here * row_count - DILATION)
    source = place + 8 - lax.broadcasted_iota(jnp.int32, (16, span), 0)
    length = blocks * row_count
    inside = (place >= 0) & (place < length) & (source >= 0) & (source < length)
    return jnp.where(inside, taps, -1).astype(jnp.float32).astype(jnp.bfloat16)


def one_hot(taps, second):
    row = lax.broadcasted_iota(jnp.int32, (TABLE, 16), 0) // KINDS
    column = lax.broadcasted_iota(jnp.int32, (TABLE, 16), 1)
    chosen = (column == 15 - row + second * (2 * row - 14)).astype(jnp.float32)
    values = jnp.dot(chosen.astype(jnp.bfloat16), taps, preferred_element_type=jnp.float32)
    base = lax.broadcasted_iota(jnp.int32, values.shape, 0) % KINDS
    base = base + second * (KINDS - 1 - 2 * base)
    return (values == base.astype(jnp.float32)).astype(jnp.float32).T


def gelu(x):
    inner = x * (0.7978845608028654 + 0.035677408136300125 * (x * x))
    half = 0.5 * x
    return half + half * jnp.tanh(inner)


def activate(hot, gain_ref, pack_ref, act_ref):
    depth, width = act_ref.shape[1], gain_ref.shape[0]
    turn = lax.rem(width - lax.axis_index("dp") * depth, width)
    gain = jnp.broadcast_to(gain_ref[...].reshape(1, width), (8, width))
    gain = pltpu.roll(gain, turn, 1)[:1, :depth]
    tables = [pack_ref[rows] for rows in table_rows(depth, width, pack_ref.shape[1])]
    for start in range(0, hot.shape[0], ROW_STEP):
        rows = hot[start : start + ROW_STEP]
        parts = [jnp.dot(rows, table, preferred_element_type=jnp.float32) for table in tables]
        square = sum(part * part for part in parts)
        mean = jnp.sum(square, axis=-1, keepdims=True) * (1.0 / width)
        scaled = parts[0][:, :depth] * lax.rsqrt(mean + EPS) * gain
        act_ref[start : start + ROW_STEP] = gelu(scaled).astype(jnp.bfloat16)


def convolve(act_ref, size, rows, pack_ref, copies=()):
    second = lax.axis_index("strand")
    depth = act_ref.shape[1]
    total = None
    for tap in EARLY_TAPS + LATE_TAPS:
        if tap in LATE_TAPS:
            for copy in copies:
                copy.wait()
        start = pl.multiple_of((tap + second * (2 - 2 * tap)) * size, 16)
        block = act_ref[pl.ds(start, rows), :]
        weight = pack_ref[tap * depth : (tap + 1) * depth]
        part = jnp.dot(block, weight, preferred_element_type=jnp.float32)
        total = part if total is None else total + part
    return total


def table_rows(depth, width, columns):
    first = 3 * depth
    count = width // columns
    return [slice(first + i * TABLE, first + (i + 1) * TABLE) for i in range(count)]


def plain_rows(depth, width, columns):
    first = 3 * depth + width // columns * TABLE
    return slice(first, first + TABLE)


def slice_kernel(point_any, tok_any, piece_ref, tok_ref, sems):
    rows, columns = piece_ref.shape
    low = pl.multiple_of(lax.axis_index("groups") * rows, 16)
    left = pl.multiple_of(lax.axis_index("strand") * columns, 128)
    part = point_any.at[pl.ds(low, rows), pl.ds(left, columns)]
    copies = [
        pltpu.make_async_copy(part, piece_ref, sems.at[0]),
        pltpu.make_async_copy(tok_any, tok_ref, sems.at[1]),
    ]
    for copy in copies:
        copy.start()
    for copy in copies:
        copy.wait()


def join_kernel(*refs):
    refs[-1][...] = jnp.concatenate([ref[...] for ref in refs[:-1]], axis=1)


def load_kernel(stem_any, w_any, pack_ref, stem_ref, flat_ref, sem, sems):
    depth, columns = w_any.shape[1:]
    copies = [pltpu.make_async_copy(stem_any, stem_ref, sem)]
    copies += weight_copies(w_any, pack_ref, EARLY_TAPS, sems)
    for copy in copies:
        copy.start()
    copies[0].wait()
    taps, kinds, width = stem_ref.shape
    slabs = [stem_ref[tap].astype(jnp.float32) for tap in range(taps)]
    slabs += [jnp.zeros((kinds, width), jnp.float32)] * (16 - taps)
    flat = jnp.concatenate(slabs)
    flat_ref[...] = flat.astype(jnp.bfloat16)
    me = lax.axis_index("dp")
    if depth == columns:
        parts = [lax.rem(me + index, width // columns) for index in range(width // columns)]
        starts = [pl.multiple_of(part * columns, 128) for part in parts]
        turned = [flat_ref[:, pl.ds(start, columns)] for start in starts]
    else:
        whole = pltpu.roll(flat, lax.rem(width - me * depth, width), 1).astype(jnp.bfloat16)
        turned = jnp.split(whole, width // columns, axis=1)
    for rows, part in zip(table_rows(depth, width, columns), turned):
        pack_ref[rows] = part
    column = pl.multiple_of(lax.axis_index("strand") * columns, 128)
    pack_ref[plain_rows(depth, width, columns)] = flat_ref[:, pl.ds(column, columns)]
    for copy in copies[1:]:
        copy.wait()


def weight_parts(weight, taps):
    rows = weight.shape[1] // 2
    return [(tap, low, rows) for tap in taps for low in (0, rows)]


def weight_copies(w_any, pack_ref, taps, sems):
    depth = w_any.shape[1]
    return [
        pltpu.make_async_copy(
            w_any.at[tap, pl.ds(low, rows)],
            pack_ref.at[pl.ds(tap * depth + low, rows)],
            sems.at[index],
        )
        for index, (tap, low, rows) in enumerate(weight_parts(w_any, taps))
    ]


def chunk_kernel(step, low, size, row_count, out_index, loading, *refs):
    gain_ref, pack_ref = refs[3:5]
    out_ref, act_ref = refs[out_index], refs[out_index + 2 if loading else -1]
    copies = []
    if loading:
        pack_ref = refs[out_index + 1]
        copies = weight_copies(refs[5], pack_ref, LATE_TAPS, refs[-1])
    for copy in copies:
        copy.start()
    taps = base_taps(refs[:3], step, row_count)
    hot = one_hot(taps, lax.axis_index("strand"))
    blocks = row_count // DILATION
    pieces = [hot[b * DILATION + low :][:size] for b in range(blocks + 2)]
    activate(jnp.concatenate(pieces).astype(jnp.bfloat16), gain_ref, pack_ref, act_ref)
    total = convolve(act_ref, size, blocks * size, pack_ref, copies)
    out_ref[...] = total.astype(jnp.bfloat16)


def rows_of(ref, low, size):
    starts = range(low, ref.shape[0], DILATION)
    return jnp.concatenate([ref[start : start + size] for start in starts])


def own_kernel(places, piece_rows, *refs):
    gain_ref, pack_ref = refs[3:5]
    pieces = refs[6 : 6 + len(places)]
    out_ref, res_ref, point_ref, act_ref, sems = refs[6 + len(places) :]
    ranks, groups = lax.axis_size("dp"), lax.axis_size("groups")
    me, group = lax.axis_index("dp"), lax.axis_index("groups")
    copies = []
    for index, (step, turn) in enumerate(places):
        place = lax.rem(me + step, ranks) * (piece_rows * groups)
        if step:
            place = place + lax.rem(group + turn, groups) * piece_rows
        source = pieces[index]
        if not step:
            columns = point_ref.shape[1]
            left = pl.multiple_of(lax.axis_index("strand") * columns, 128)
            source = source.at[:, pl.ds(left, columns)]
        target = pl.ds(pl.multiple_of(place, 16), source.shape[0])
        copies.append(pltpu.make_async_copy(source, point_ref.at[target], sems.at[index]))
        copies[-1].start()
    row_count = out_ref.shape[0]
    second = lax.axis_index("strand")
    taps = base_taps(refs[:3], 0, row_count)
    hot = one_hot(taps, second)
    here = slice(DILATION, DILATION + row_count)
    both = (hot[here] + one_hot(taps[:, here], 1 - second)).astype(jnp.bfloat16)
    plain = pack_ref[plain_rows(act_ref.shape[1], gain_ref.shape[0], pack_ref.shape[1])]
    res_ref[...] = jnp.dot(both, plain, preferred_element_type=jnp.float32)
    activate(hot.astype(jnp.bfloat16), gain_ref, pack_ref, act_ref)
    out_ref[...] = convolve(act_ref, DILATION, row_count, pack_ref)
    for copy in copies:
        copy.wait()


def middle_kernel(chunks, count, own_ref, gain_ref, *refs):
    out_ref = refs[-1]
    gain = gain_ref[...].reshape(1, -1)
    first, total_size = chunks[0][0], sum(size for _, size in chunks)
    for index, (low, size) in enumerate(chunks):
        parts = refs[index * count : (index + 1) * count]
        for block in range(own_ref.shape[0] // DILATION):
            for row in range(0, size, ROW_STEP):
                start = block * DILATION + low + row
                total = own_ref[start : start + ROW_STEP]
                start = block * size + row
                for ref in parts:
                    total = total + ref[start : start + ROW_STEP].astype(jnp.float32)
                mean = jnp.mean(total * total, axis=-1, keepdims=True)
                value = gelu(total * lax.rsqrt(mean + EPS) * gain)
                start = block * total_size + low - first + row
                out_ref[start : start + ROW_STEP] = value.astype(jnp.bfloat16)


def final_kernel(low, size, out_index, mine_ref, other_ref, res_ref, point_ref, *refs):
    out_ref, tick_ref = refs[out_index - 4 :]
    tick_ref[...] = jnp.zeros_like(tick_ref)
    total = mine_ref[...].astype(jnp.float32) + other_ref[...].astype(jnp.float32)
    branch = jnp.dot(
        total.astype(jnp.bfloat16), point_ref[...], preferred_element_type=jnp.float32
    )
    value = (0.5 * (branch + rows_of(res_ref, low, size))).astype(jnp.bfloat16)
    out_ref[...] = value.reshape(out_ref.shape)


def in_hbm(x):
    return pltpu.with_memory_space_constraint(x, pltpu.HBM)


def cost(kind):
    return pl.CostEstimate(
        flops=int(1e9 * WEIGHTS[kind]), bytes_accessed=2**20, transcendentals=0
    )


def per_device(tokens, stem_table, conv_weight, gain_in, gain_mid, point_weight):
    row_count = tokens.shape[1]
    width = stem_table.shape[2]
    depth, inner = conv_weight.shape[1:]
    count, groups = lax.axis_size("dp"), lax.axis_size("groups")
    half = width // 2
    vmem = pl.BlockSpec(memory_space=pltpu.VMEM)
    anywhere = pl.BlockSpec(memory_space=pl.ANY)
    bf16, f32 = jnp.bfloat16, jnp.float32
    params = pltpu.CompilerParams(vmem_limit_bytes=24 * MIB)

    others = [lax.ppermute(tokens, "dp", ring_pairs("dp", -step)) for step in range(1, count)]
    piece_rows = point_weight.shape[0] // groups
    piece, here = pl.pallas_call(
        slice_kernel,
        out_shape=[
            jax.ShapeDtypeStruct((piece_rows, half), bf16),
            jax.ShapeDtypeStruct(tokens.shape, tokens.dtype),
        ],
        in_specs=[anywhere] * 2,
        out_specs=[vmem] * 2,
        scratch_shapes=[pltpu.SemaphoreType.DMA((2,))],
        compiler_params=params,
        cost_estimate=cost("early"),
        name="point_slice",
    )(in_hbm(point_weight), in_hbm(tokens))
    joined = pl.pallas_call(
        join_kernel,
        out_shape=jax.ShapeDtypeStruct((1, count * row_count), tokens.dtype),
        in_specs=[vmem] * count,
        out_specs=vmem,
        compiler_params=params,
        cost_estimate=cost("early"),
        name="join",
    )(here, *others)
    even = lax.ppermute(joined, "seq", pair_pairs("seq", 0))
    odd = lax.ppermute(joined, "seq", pair_pairs("seq", 1))
    pack_rows = 3 * depth + (width // inner + 1) * TABLE
    pack = pl.pallas_call(
        load_kernel,
        out_shape=jax.ShapeDtypeStruct((pack_rows, inner), bf16),
        in_specs=[anywhere] * 2,
        out_specs=vmem,
        scratch_shapes=[
            pltpu.VMEM(stem_table.shape, bf16),
            pltpu.VMEM((TABLE, width), bf16),
            pltpu.SemaphoreType.DMA,
            pltpu.SemaphoreType.DMA((len(weight_parts(conv_weight, EARLY_TAPS)),)),
        ],
        compiler_params=params,
        cost_estimate=cost("load"),
        name="load",
    )(in_hbm(stem_table), in_hbm(conv_weight))
    crossed = [lax.ppermute(piece, "dp", ring_pairs("dp", -step)) for step in range(1, count)]

    received = [[] for _ in CHUNKS]
    for step in range(1, count):
        for index, (low, size) in enumerate(CHUNKS):
            rows = row_count // DILATION * size
            loading, passing = step == 1 and index == 0, index == 1
            operands = [even, joined, odd, gain_in, pack]
            shapes = [jax.ShapeDtypeStruct((rows, inner), bf16)]
            scratch = [pltpu.VMEM((rows + 2 * size, depth), bf16)]
            aliases = {}
            if loading:
                operands.append(in_hbm(conv_weight))
                shapes.append(jax.ShapeDtypeStruct(pack.shape, bf16))
                late = len(weight_parts(conv_weight, LATE_TAPS))
                scratch.append(pltpu.SemaphoreType.DMA((late,)))
                aliases = {4: 1}
            if passing:
                operands.append(crossed[step - 1])
                shapes.append(jax.ShapeDtypeStruct(crossed[step - 1].shape, bf16))
                aliases = {5: 1}
            if index:
                operands.append(part)
            part, *passed = pl.pallas_call(
                functools.partial(
                    chunk_kernel, step, low, size, row_count, len(operands), loading
                ),
                out_shape=shapes,
                in_specs=[vmem] * 5 + [anywhere] * (len(operands) - 5),
                out_specs=[vmem, vmem if loading else anywhere][: len(shapes)],
                scratch_shapes=scratch,
                input_output_aliases=aliases,
                compiler_params=params,
                cost_estimate=cost(f"sent{index}"),
                name="conv_sent",
            )(*operands)
            if loading:
                pack = passed.pop()
            if passed:
                crossed[step - 1] = passed[0]
            received[index].append(lax.ppermute(part, "dp", ring_pairs("dp", step)))

    places, pieces = [(0, 0)], [in_hbm(point_weight)]
    for step in range(1, count):
        for turn in range(groups):
            piece = crossed[step - 1]
            if turn:
                piece = lax.ppermute(piece, "groups", ring_pairs("groups", -turn))
            places.append((step, turn))
            pieces.append(piece)

    own, res, point = pl.pallas_call(
        functools.partial(own_kernel, places, piece_rows),
        out_shape=[
            jax.ShapeDtypeStruct((row_count, inner), f32),
            jax.ShapeDtypeStruct((row_count, half), f32),
            jax.ShapeDtypeStruct((inner, half), bf16),
        ],
        in_specs=[vmem] * 5 + [anywhere] * (1 + len(pieces)),
        out_specs=[vmem] * 3,
        scratch_shapes=[
            pltpu.VMEM((row_count + 2 * DILATION, depth), bf16),
            pltpu.SemaphoreType.DMA((len(pieces),)),
        ],
        compiler_params=params,
        cost_estimate=cost("own"),
        name="conv_own",
    )(even, joined, odd, gain_in, pack, part, *pieces)

    out, ticks = None, []
    blocks = row_count // DILATION
    for index, tail in enumerate(TAILS):
        chunks = [CHUNKS[chunk] for chunk in tail]
        low, size = chunks[0][0], sum(size for _, size in chunks)
        parts = [part for chunk in tail for part in received[chunk]]
        after = [] if index < 2 else [ticks[index - 2]]
        middle = pl.pallas_call(
            functools.partial(middle_kernel, chunks, count - 1),
            out_shape=jax.ShapeDtypeStruct((blocks * size, inner), bf16),
            in_specs=[vmem] * (2 + len(parts)) + [anywhere] * len(after),
            out_specs=vmem,
            compiler_params=params,
            cost_estimate=cost(f"middle{index}"),
            name="middle",
        )(own, gain_mid, *parts, *after)
        other = lax.ppermute(middle, "strand", ring_pairs("strand", 1))
        operands = [middle, other, res, point] + ([] if out is None else [out])
        out, tick = pl.pallas_call(
            functools.partial(final_kernel, low, size, len(operands)),
            grid=(1,),
            out_shape=[
                jax.ShapeDtypeStruct((blocks, DILATION, half), bf16),
                jax.ShapeDtypeStruct((8, 128), f32),
            ],
            in_specs=[vmem] * 4 + [anywhere] * (len(operands) - 4),
            out_specs=[
                pl.BlockSpec((blocks, size, half), lambda i, at=low // size: (0, at, 0)),
                vmem,
            ],
            input_output_aliases={} if out is None else {4: 0},
            compiler_params=params,
            cost_estimate=cost(f"final{index}"),
            name="final",
        )(*operands)
        ticks.append(tick)
    return out.reshape(1, row_count, half)


def solution(mesh):
    return jax.shard_map(
        per_device,
        mesh=mesh,
        in_specs=(P(("groups", "dp"), "seq"), P(), P(None, "dp", None), P(), P(), P("dp", None)),
        out_specs=P(("groups", "dp"), "seq", "strand"),
        check_vma=False,
    )
```

```python
import functools

import jax
import jax.numpy as jnp
from jax import lax
from jax.experimental import pallas as pl
from jax.experimental.pallas import tpu as pltpu
from jax.sharding import PartitionSpec as P

DILATION = 256
EPS = 1e-06
ROW_STEP = 32
CHUNKS = ((0, 96), (96, 96), (192, 64))
TAILS = ((0,), (1,), (2,))
EARLY_TAPS, LATE_TAPS = (0, 1, 2), ()
KINDS = 4
TABLE = 16 * KINDS
WEIGHTS = {
    "early": 0.1,
    "load": 0.1,
    "sent0": 15.0,
    "sent1": 0.5,
    "sent2": 5.0,
    "own": 15.0,
    "middle0": 0.05,
    "middle1": 5.0,
    "middle2": 5.0,
    "final0": 0.05,
    "final1": 0.5,
    "final2": 15.0,
}
MIB = 2**20


def pair_pairs(axis, first):
    count = lax.axis_size(axis)
    pairs = [(i, i + 1) for i in range(first, count - 1, 2)]
    return pairs + [(target, source) for source, target in pairs]


def ring_pairs(axis, distance):
    count = lax.axis_size(axis)
    return [(i, (i + distance) % count) for i in range(count)]


def base_taps(sides, step, row_count):
    blocks, here = lax.axis_size("seq"), lax.axis_index("seq")
    low = step * row_count
    even, middle, odd = [ref[:, low : low + row_count] for ref in sides]
    second = lax.rem(here, 2) == 1
    below, above = jnp.where(second, even, odd), jnp.where(second, odd, even)
    bases = jnp.concatenate([below, middle, above], axis=1)
    width, span = 3 * row_count, row_count + 2 * DILATION
    spread = jnp.broadcast_to(bases, (16, width))
    start = width - (row_count - DILATION + 8)
    taps = pltpu.roll(spread, start, 1, stride=1, stride_axis=0)[:, :span]
    place = lax.broadcasted_iota(jnp.int32, (16, span), 1) + (here * row_count - DILATION)
    source = place + 8 - lax.broadcasted_iota(jnp.int32, (16, span), 0)
    length = blocks * row_count
    inside = (place >= 0) & (place < length) & (source >= 0) & (source < length)
    return jnp.where(inside, taps, -1).astype(jnp.float32).astype(jnp.bfloat16)


def one_hot(taps, second):
    row = lax.broadcasted_iota(jnp.int32, (TABLE, 16), 0) // KINDS
    column = lax.broadcasted_iota(jnp.int32, (TABLE, 16), 1)
    chosen = (column == 15 - row + second * (2 * row - 14)).astype(jnp.float32)
    values = jnp.dot(chosen.astype(jnp.bfloat16), taps, preferred_element_type=jnp.float32)
    base = lax.broadcasted_iota(jnp.int32, values.shape, 0) % KINDS
    base = base + second * (KINDS - 1 - 2 * base)
    return (values == base.astype(jnp.float32)).astype(jnp.float32).T


def gelu(x):
    inner = x * (0.7978845608028654 + 0.035677408136300125 * (x * x))
    half = 0.5 * x
    return half + half * jnp.tanh(inner)


def activate(hot, gain_ref, pack_ref, act_ref):
    depth, width = act_ref.shape[1], gain_ref.shape[0]
    turn = lax.rem(width - lax.axis_index("dp") * depth, width)
    gain = jnp.broadcast_to(gain_ref[...].reshape(1, width), (8, width))
    gain = pltpu.roll(gain, turn, 1)[:1, :depth]
    tables = [pack_ref[rows] for rows in table_rows(depth, width, pack_ref.shape[1])]
    for start in range(0, hot.shape[0], ROW_STEP):
        rows = hot[start : start + ROW_STEP]
        parts = [jnp.dot(rows, table, preferred_element_type=jnp.float32) for table in tables]
        square = sum(part * part for part in parts)
        mean = jnp.sum(square, axis=-1, keepdims=True) * (1.0 / width)
        scaled = parts[0][:, :depth] * lax.rsqrt(mean + EPS) * gain
        act_ref[start : start + ROW_STEP] = gelu(scaled).astype(jnp.bfloat16)


def convolve(act_ref, size, rows, pack_ref, copies=()):
    second = lax.axis_index("strand")
    depth = act_ref.shape[1]
    total = None
    for tap in EARLY_TAPS + LATE_TAPS:
        if tap in LATE_TAPS:
            for copy in copies:
                copy.wait()
        start = pl.multiple_of((tap + second * (2 - 2 * tap)) * size, 16)
        block = act_ref[pl.ds(start, rows), :]
        weight = pack_ref[tap * depth : (tap + 1) * depth]
        part = jnp.dot(block, weight, preferred_element_type=jnp.float32)
        total = part if total is None else total + part
    return total


def table_rows(depth, width, columns):
    first = 3 * depth
    count = width // columns
    return [slice(first + i * TABLE, first + (i + 1) * TABLE) for i in range(count)]


def plain_rows(depth, width, columns):
    first = 3 * depth + width // columns * TABLE
    return slice(first, first + TABLE)


def slice_kernel(point_any, tok_any, piece_ref, tok_ref, sems):
    rows, columns = piece_ref.shape
    low = pl.multiple_of(lax.axis_index("groups") * rows, 16)
    left = pl.multiple_of(lax.axis_index("strand") * columns, 128)
    part = point_any.at[pl.ds(low, rows), pl.ds(left, columns)]
    copies = [
        pltpu.make_async_copy(part, piece_ref, sems.at[0]),
        pltpu.make_async_copy(tok_any, tok_ref, sems.at[1]),
    ]
    for copy in copies:
        copy.start()
    for copy in copies:
        copy.wait()


def join_kernel(*refs):
    refs[-1][...] = jnp.concatenate([ref[...] for ref in refs[:-1]], axis=1)


def load_kernel(stem_any, w_any, pack_ref, stem_ref, flat_ref, sem, sems):
    depth, columns = w_any.shape[1:]
    copies = [pltpu.make_async_copy(stem_any, stem_ref, sem)]
    copies += weight_copies(w_any, pack_ref, EARLY_TAPS, sems)
    for copy in copies:
        copy.start()
    copies[0].wait()
    taps, kinds, width = stem_ref.shape
    slabs = [stem_ref[tap].astype(jnp.float32) for tap in range(taps)]
    slabs += [jnp.zeros((kinds, width), jnp.float32)] * (16 - taps)
    flat = jnp.concatenate(slabs)
    flat_ref[...] = flat.astype(jnp.bfloat16)
    me = lax.axis_index("dp")
    if depth == columns:
        parts = [lax.rem(me + index, width // columns) for index in range(width // columns)]
        starts = [pl.multiple_of(part * columns, 128) for part in parts]
        turned = [flat_ref[:, pl.ds(start, columns)] for start in starts]
    else:
        whole = pltpu.roll(flat, lax.rem(width - me * depth, width), 1).astype(jnp.bfloat16)
        turned = jnp.split(whole, width // columns, axis=1)
    for rows, part in zip(table_rows(depth, width, columns), turned):
        pack_ref[rows] = part
    column = pl.multiple_of(lax.axis_index("strand") * columns, 128)
    pack_ref[plain_rows(depth, width, columns)] = flat_ref[:, pl.ds(column, columns)]
    for copy in copies[1:]:
        copy.wait()


def weight_parts(weight, taps):
    rows = weight.shape[1] // 2
    return [(tap, low, rows) for tap in taps for low in (0, rows)]


def weight_copies(w_any, pack_ref, taps, sems):
    depth = w_any.shape[1]
    return [
        pltpu.make_async_copy(
            w_any.at[tap, pl.ds(low, rows)],
            pack_ref.at[pl.ds(tap * depth + low, rows)],
            sems.at[index],
        )
        for index, (tap, low, rows) in enumerate(weight_parts(w_any, taps))
    ]


def chunk_kernel(step, low, size, row_count, out_index, loading, *refs):
    gain_ref, pack_ref = refs[3:5]
    out_ref, act_ref = refs[out_index], refs[out_index + 2 if loading else -1]
    copies = []
    if loading:
        pack_ref = refs[out_index + 1]
        copies = weight_copies(refs[5], pack_ref, LATE_TAPS, refs[-1])
    for copy in copies:
        copy.start()
    taps = base_taps(refs[:3], step, row_count)
    hot = one_hot(taps, lax.axis_index("strand"))
    blocks = row_count // DILATION
    pieces = [hot[b * DILATION + low :][:size] for b in range(blocks + 2)]
    activate(jnp.concatenate(pieces).astype(jnp.bfloat16), gain_ref, pack_ref, act_ref)
    total = convolve(act_ref, size, blocks * size, pack_ref, copies)
    out_ref[...] = total.astype(jnp.bfloat16)


def rows_of(ref, low, size):
    starts = range(low, ref.shape[0], DILATION)
    return jnp.concatenate([ref[start : start + size] for start in starts])


def own_kernel(places, piece_rows, *refs):
    gain_ref, pack_ref = refs[3:5]
    pieces = refs[6 : 6 + len(places)]
    out_ref, res_ref, point_ref, act_ref, sems = refs[6 + len(places) :]
    ranks, groups = lax.axis_size("dp"), lax.axis_size("groups")
    me, group = lax.axis_index("dp"), lax.axis_index("groups")
    copies = []
    for index, (step, turn) in enumerate(places):
        place = lax.rem(me + step, ranks) * (piece_rows * groups)
        if step:
            place = place + lax.rem(group + turn, groups) * piece_rows
        source = pieces[index]
        if not step:
            columns = point_ref.shape[1]
            left = pl.multiple_of(lax.axis_index("strand") * columns, 128)
            source = source.at[:, pl.ds(left, columns)]
        target = pl.ds(pl.multiple_of(place, 16), source.shape[0])
        copies.append(pltpu.make_async_copy(source, point_ref.at[target], sems.at[index]))
        copies[-1].start()
    row_count = out_ref.shape[0]
    second = lax.axis_index("strand")
    taps = base_taps(refs[:3], 0, row_count)
    hot = one_hot(taps, second)
    here = slice(DILATION, DILATION + row_count)
    both = (hot[here] + one_hot(taps[:, here], 1 - second)).astype(jnp.bfloat16)
    plain = pack_ref[plain_rows(act_ref.shape[1], gain_ref.shape[0], pack_ref.shape[1])]
    res_ref[...] = jnp.dot(both, plain, preferred_element_type=jnp.float32)
    activate(hot.astype(jnp.bfloat16), gain_ref, pack_ref, act_ref)
    out_ref[...] = convolve(act_ref, DILATION, row_count, pack_ref)
    for copy in copies:
        copy.wait()


def middle_kernel(chunks, count, own_ref, gain_ref, *refs):
    out_ref = refs[-1]
    gain = gain_ref[...].reshape(1, -1)
    first, total_size = chunks[0][0], sum(size for _, size in chunks)
    for index, (low, size) in enumerate(chunks):
        parts = refs[index * count : (index + 1) * count]
        for block in range(own_ref.shape[0] // DILATION):
            for row in range(0, size, ROW_STEP):
                start = block * DILATION + low + row
                total = own_ref[start : start + ROW_STEP]
                start = block * size + row
                for ref in parts:
                    total = total + ref[start : start + ROW_STEP].astype(jnp.float32)
                mean = jnp.mean(total * total, axis=-1, keepdims=True)
                value = gelu(total * lax.rsqrt(mean + EPS) * gain)
                start = block * total_size + low - first + row
                out_ref[start : start + ROW_STEP] = value.astype(jnp.bfloat16)


def final_kernel(low, size, out_index, mine_ref, other_ref, res_ref, point_ref, *refs):
    out_ref, tick_ref = refs[out_index - 4 :]
    tick_ref[...] = jnp.zeros_like(tick_ref)
    total = mine_ref[...].astype(jnp.float32) + other_ref[...].astype(jnp.float32)
    branch = jnp.dot(
        total.astype(jnp.bfloat16), point_ref[...], preferred_element_type=jnp.float32
    )
    value = (0.5 * (branch + rows_of(res_ref, low, size))).astype(jnp.bfloat16)
    out_ref[...] = value.reshape(out_ref.shape)


def in_hbm(x):
    return pltpu.with_memory_space_constraint(x, pltpu.HBM)


def cost(kind):
    return pl.CostEstimate(
        flops=int(1e9 * WEIGHTS[kind]), bytes_accessed=2**20, transcendentals=0
    )


def per_device(tokens, stem_table, conv_weight, gain_in, gain_mid, point_weight):
    row_count = tokens.shape[1]
    width = stem_table.shape[2]
    depth, inner = conv_weight.shape[1:]
    count, groups = lax.axis_size("dp"), lax.axis_size("groups")
    half = width // 2
    vmem = pl.BlockSpec(memory_space=pltpu.VMEM)
    anywhere = pl.BlockSpec(memory_space=pl.ANY)
    bf16, f32 = jnp.bfloat16, jnp.float32
    params = pltpu.CompilerParams(vmem_limit_bytes=24 * MIB)

    others = [lax.ppermute(tokens, "dp", ring_pairs("dp", -step)) for step in range(1, count)]
    piece_rows = point_weight.shape[0] // groups
    piece, here = pl.pallas_call(
        slice_kernel,
        out_shape=[
            jax.ShapeDtypeStruct((piece_rows, half), bf16),
            jax.ShapeDtypeStruct(tokens.shape, tokens.dtype),
        ],
        in_specs=[anywhere] * 2,
        out_specs=[vmem] * 2,
        scratch_shapes=[pltpu.SemaphoreType.DMA((2,))],
        compiler_params=params,
        cost_estimate=cost("early"),
        name="point_slice",
    )(in_hbm(point_weight), in_hbm(tokens))
    joined = pl.pallas_call(
        join_kernel,
        out_shape=jax.ShapeDtypeStruct((1, count * row_count), tokens.dtype),
        in_specs=[vmem] * count,
        out_specs=vmem,
        compiler_params=params,
        cost_estimate=cost("early"),
        name="join",
    )(here, *others)
    even = lax.ppermute(joined, "seq", pair_pairs("seq", 0))
    odd = lax.ppermute(joined, "seq", pair_pairs("seq", 1))
    pack_rows = 3 * depth + (width // inner + 1) * TABLE
    pack = pl.pallas_call(
        load_kernel,
        out_shape=jax.ShapeDtypeStruct((pack_rows, inner), bf16),
        in_specs=[anywhere] * 2,
        out_specs=vmem,
        scratch_shapes=[
            pltpu.VMEM(stem_table.shape, bf16),
            pltpu.VMEM((TABLE, width), bf16),
            pltpu.SemaphoreType.DMA,
            pltpu.SemaphoreType.DMA((len(weight_parts(conv_weight, EARLY_TAPS)),)),
        ],
        compiler_params=params,
        cost_estimate=cost("load"),
        name="load",
    )(in_hbm(stem_table), in_hbm(conv_weight))
    crossed = [lax.ppermute(piece, "dp", ring_pairs("dp", -step)) for step in range(1, count)]

    received = [[] for _ in CHUNKS]
    for step in range(1, count):
        for index, (low, size) in enumerate(CHUNKS):
            rows = row_count // DILATION * size
            loading = bool(LATE_TAPS) and step == 1 and index == 0
            passing = index == 1
            operands = [even, joined, odd, gain_in, pack]
            shapes = [jax.ShapeDtypeStruct((rows, inner), bf16)]
            scratch = [pltpu.VMEM((rows + 2 * size, depth), bf16)]
            aliases = {}
            if loading:
                operands.append(in_hbm(conv_weight))
                shapes.append(jax.ShapeDtypeStruct(pack.shape, bf16))
                late = len(weight_parts(conv_weight, LATE_TAPS))
                scratch.append(pltpu.SemaphoreType.DMA((late,)))
                aliases = {4: 1}
            if passing:
                operands.append(crossed[step - 1])
                shapes.append(jax.ShapeDtypeStruct(crossed[step - 1].shape, bf16))
                aliases = {5: 1}
            if index:
                operands.append(part)
            part, *passed = pl.pallas_call(
                functools.partial(
                    chunk_kernel, step, low, size, row_count, len(operands), loading
                ),
                out_shape=shapes,
                in_specs=[vmem] * 5 + [anywhere] * (len(operands) - 5),
                out_specs=[vmem, vmem if loading else anywhere][: len(shapes)],
                scratch_shapes=scratch,
                input_output_aliases=aliases,
                compiler_params=params,
                cost_estimate=cost(f"sent{index}"),
                name="conv_sent",
            )(*operands)
            if loading:
                pack = passed.pop()
            if passed:
                crossed[step - 1] = passed[0]
            received[index].append(lax.ppermute(part, "dp", ring_pairs("dp", step)))

    places, pieces = [(0, 0)], [in_hbm(point_weight)]
    for step in range(1, count):
        for turn in range(groups):
            piece = crossed[step - 1]
            if turn:
                piece = lax.ppermute(piece, "groups", ring_pairs("groups", -turn))
            places.append((step, turn))
            pieces.append(piece)

    own, res, point = pl.pallas_call(
        functools.partial(own_kernel, places, piece_rows),
        out_shape=[
            jax.ShapeDtypeStruct((row_count, inner), f32),
            jax.ShapeDtypeStruct((row_count, half), f32),
            jax.ShapeDtypeStruct((inner, half), bf16),
        ],
        in_specs=[vmem] * 5 + [anywhere] * (1 + len(pieces)),
        out_specs=[vmem] * 3,
        scratch_shapes=[
            pltpu.VMEM((row_count + 2 * DILATION, depth), bf16),
            pltpu.SemaphoreType.DMA((len(pieces),)),
        ],
        compiler_params=params,
        cost_estimate=cost("own"),
        name="conv_own",
    )(even, joined, odd, gain_in, pack, part, *pieces)

    out, ticks = None, []
    blocks = row_count // DILATION
    for index, tail in enumerate(TAILS):
        chunks = [CHUNKS[chunk] for chunk in tail]
        low, size = chunks[0][0], sum(size for _, size in chunks)
        parts = [part for chunk in tail for part in received[chunk]]
        after = [] if index < 2 else [ticks[index - 2]]
        middle = pl.pallas_call(
            functools.partial(middle_kernel, chunks, count - 1),
            out_shape=jax.ShapeDtypeStruct((blocks * size, inner), bf16),
            in_specs=[vmem] * (2 + len(parts)) + [anywhere] * len(after),
            out_specs=vmem,
            compiler_params=params,
            cost_estimate=cost(f"middle{index}"),
            name="middle",
        )(own, gain_mid, *parts, *after)
        other = lax.ppermute(middle, "strand", ring_pairs("strand", 1))
        operands = [middle, other, res, point] + ([] if out is None else [out])
        out, tick = pl.pallas_call(
            functools.partial(final_kernel, low, size, len(operands)),
            grid=(1,),
            out_shape=[
                jax.ShapeDtypeStruct((blocks, DILATION, half), bf16),
                jax.ShapeDtypeStruct((8, 128), f32),
            ],
            in_specs=[vmem] * 4 + [anywhere] * (len(operands) - 4),
            out_specs=[
                pl.BlockSpec((blocks, size, half), lambda i, at=low // size: (0, at, 0)),
                vmem,
            ],
            input_output_aliases={} if out is None else {4: 0},
            compiler_params=params,
            cost_estimate=cost(f"final{index}"),
            name="final",
        )(*operands)
        ticks.append(tick)
    return out.reshape(1, row_count, half)


def solution(mesh):
    return jax.shard_map(
        per_device,
        mesh=mesh,
        in_specs=(P(("groups", "dp"), "seq"), P(), P(None, "dp", None), P(), P(), P("dp", None)),
        out_specs=P(("groups", "dp"), "seq", "strand"),
        check_vma=False,
    )
```
